32 devices in a mesh: wide: 8 (over z, x), narrow: 4 (over y, core).
Axes of the slice: x: 2, y: 2, z: 4, core: 2. Of those that a mesh axis runs over, the one named last changes fastest.
Arguments:
- charges: bfloat16 [16, 32, 256, 256], P('narrow', 'wide'), may hold values from -6 to 6
- positions: float32 [16, 32, 2, 256], P('narrow', 'wide'), may hold values from -1 to 2
- noise: float32 [16, 32, 256], P('narrow', 'wide'), may hold values from 0.1 to 1
- leaf_basis: bfloat16 [16, 32, 64, 256], P('narrow', 'wide'), may hold values from -0.375 to 0.375
- transfer: bfloat16 [4, 8, 21, 64, 64], P('narrow', 'wide'), may hold values from -0.75 to 0.75
- near_list: int32 [16, 32, 10], P('narrow', 'wide'), may hold values from -1 to 24, as said below
Outputs:
- potential: bfloat16 [16, 32, 256, 256], P('narrow', 'wide')
The draws below stay inside these ranges and needn't reach their ends.
Inputs may be any that keep to these rules, and one draw needn't show every extreme that they name: `near_list`: A code names the offset (dy, dx) as (dy + 2) * 5 + dx + 2. Each leaf's list holds the nine codes with max(|dy|, |dx|) <= 1 and at most one code with max(|dy|, |dx|) = 2, each code once, in any order, with -1 in a slot left empty; some leaf holds ten codes.
All inputs are finite; a program needn't handle non-finite values.
Results may differ from the reference program's by a relative error of at most 0.006.
Values may be sent and summed in bfloat16 or wider, within the bound.
No kernel may reach another device: no remote copies, remote signals or barrier semaphores. Data moves between devices by JAX's collectives and lax.ppermute only.
A program may use at most 128 MiB of HBM per device.

```python
import math
import jax
import jax.numpy as jnp
import numpy as np
from jax import lax

LEAF = 256
CHEB = 8
RANK = 64
RHS = 256
LEVELS = 2
NEAR = 10
SIDE = 4
NODES = 21
GY = 16
GX = 32
BLOCK_Y = 4
BLOCK_X = 8
N_WIDE = 8
N_NARROW = 4


def draw_near_list(key, part):
    key_cycle, key_present, key_force, key_order = jax.random.split(key, 4)
    core_codes = jnp.asarray(np.array([(offset_y + 2) * 5 + offset_x + 2 for offset_y in (-1, 0, 1) for offset_x in (-1, 0, 1)], dtype=np.int32))
    cycle_codes = jnp.asarray(np.array([(offset_y + 2) * 5 + offset_x + 2 for offset_y in range(-2, 3) for offset_x in range(-2, 3) if max(abs(offset_y), abs(offset_x)) == 2], dtype=np.int32))
    leaves = GY * GX
    picked = jax.random.randint(key_cycle, (leaves,), 0, 16)
    present = jax.random.randint(key_present, (leaves,), 0, 2)
    forced = jax.random.randint(key_force, (), 0, leaves)
    present = jnp.maximum(present, (jnp.arange(leaves) == forced).astype(jnp.int32))
    extra = jnp.where(present == 1, cycle_codes[picked], -1)
    listing = jnp.concatenate([jnp.broadcast_to(core_codes, (leaves, 9)), extra[:, None]], axis=1)
    scores = jax.random.randint(key_order, (leaves, NEAR), 0, 1 << 20) * 16 + jnp.arange(NEAR)
    ordering = jnp.argsort(scores, axis=1)
    return jnp.take_along_axis(listing, ordering, axis=1).reshape(GY, GX, NEAR).astype(jnp.int32)


def shard_levels(key, shape, cuts, least, high):
    loudness, own = 1.0, jax.random.fold_in(key, 6)
    for axis_at, blocks in cuts:
        draws = jnp.exp(jax.random.uniform(jax.random.fold_in(own, axis_at), (blocks,), jnp.float32, least / len(cuts), high / len(cuts)))
        loudness = loudness * jnp.repeat(draws, shape[axis_at] // blocks).reshape([-1 if axis == axis_at else 1 for axis in range(len(shape))])
    return loudness


def bell_draw(key, shape, scale, bound, pieces=(), held_as=jnp.bfloat16):
    values = jax.random.normal(key, shape, jnp.float32) * scale
    if len(pieces) > 0:
        values = shard_levels(key, shape, pieces, -0.22, 0.18) * values
    return jnp.clip(values, min=-bound, max=bound).astype(held_as)


def setup_inputs(seed: int = 0) -> dict:
    keys = jax.random.split(jax.random.key(seed), 7)
    charges = bell_draw(keys[0], (GY, GX, LEAF, RHS), 1.0, 6.0, ((0, 4), (1, 8)))
    positions = jnp.clip(-1.0 + 3.0 * jax.random.uniform(keys[1], (GY, GX, 2, LEAF), jnp.float32) ** shard_levels(keys[1], (GY, GX, 2, LEAF), ((0, 4), (1, 8)), -0.2, 0.2), -1.0, 2.0)
    noise = jnp.clip(jnp.exp(math.log(1.0) - 2.3025851 * jax.random.uniform(keys[2], (GY, GX, LEAF), jnp.float32) ** shard_levels(keys[2], (GY, GX, LEAF), ((0, 4), (1, 8)), -0.2, 0.2)), 0.1, 1.0)
    leaf_basis = bell_draw(keys[3], (GY, GX, RANK, LEAF), LEAF ** -0.5, 0.375, ((0, 4), (1, 8)))
    transfer = bell_draw(keys[4], (BLOCK_Y, BLOCK_X, NODES, RANK, RANK), RANK ** -0.5, 0.75, ((0, 4), (1, 8)))
    near_list = draw_near_list(jax.random.fold_in(keys[6], 71), 0)
    return {"charges": charges, "positions": positions, "noise": noise, "leaf_basis": leaf_basis, "transfer": transfer, "near_list": near_list}


short_len = 0.125
long_weight = 0.03125
wave_number = 20.0 * math.pi

def kernel(squared):
    envelope = jnp.exp(squared * (-0.5 / (3.0 * SIDE * 3.0 * SIDE)))
    return jnp.exp(squared * (-0.5 / (short_len * short_len))) + long_weight * envelope * jnp.cos(wave_number * jnp.sqrt(squared))

def coupling(box_width, shift_y, shift_x):
    angles = (2.0 * jnp.arange(CHEB, dtype=jnp.float32) + 1.0) * (math.pi / (2.0 * CHEB))
    points = 0.5 * box_width * (1.0 + jnp.cos(angles))
    node_x = jnp.tile(points, CHEB)
    node_y = jnp.repeat(points, CHEB)
    offset_x = jnp.asarray(shift_x, jnp.float32)[..., None, None] * box_width
    offset_y = jnp.asarray(shift_y, jnp.float32)[..., None, None] * box_width
    gap_x = node_x[:, None] - node_x[None, :] - offset_x
    gap_y = node_y[:, None] - node_y[None, :] - offset_y
    return kernel(gap_x * gap_x + gap_y * gap_y)

def offset_tables(outer_y, outer_x):
    pair_range = np.arange(2)
    corner_grid = np.meshgrid(pair_range, pair_range, pair_range, pair_range, indexing='ij')
    shift_y = 2 * outer_y + corner_grid[0] - corner_grid[2]
    shift_x = 2 * outer_x + corner_grid[1] - corner_grid[3]
    reach_max = np.maximum(np.abs(shift_y), np.abs(shift_x))
    cycle_mask = (reach_max >= 2).astype(np.float32)
    code_table = np.where(reach_max <= 2, (shift_y + 2) * 5 + shift_x + 2, -2).astype(np.int32)
    return (shift_y, shift_x, cycle_mask, code_table)

def level_offset(height):
    return sum(((SIDE >> lower_level) ** 2 for lower_level in range(height)))

def rounded_copy(values):
    return lax.optimization_barrier(values.astype(jnp.bfloat16)).astype(jnp.float32)

def level_matrices(transfer, height):
    extent = SIDE >> height
    start = level_offset(height)
    packed = transfer[:, :, start:start + extent * extent]
    packed = packed.reshape(N_NARROW, N_WIDE, extent, extent, RANK, RANK).transpose(0, 2, 1, 3, 4, 5)
    return packed.reshape(N_NARROW * extent, N_WIDE * extent, RANK, RANK)

def level_far(coeffs, height, near_list):
    rows_all = coeffs.shape[0]
    cols_all = coeffs.shape[1]
    half_rows = rows_all // 2
    half_cols = cols_all // 2
    sample_count = coeffs.shape[-1]
    padded = jnp.pad(coeffs, ((2, 2), (2, 2), (0, 0), (0, 0)))
    blocks = padded.reshape(half_rows + 2, 2, half_cols + 2, 2, RANK, sample_count)
    box_width = float(2 ** height)
    if height == 0:
        list_blocks = near_list.reshape(half_rows, 2, half_cols, 2, NEAR).transpose(0, 2, 1, 3, 4)

    def parent_row(row_index):
        window = lax.dynamic_slice_in_dim(blocks, row_index, 3, 0)
        accumulated = jnp.zeros((2, half_cols, 2, RANK, sample_count), jnp.float32)
        for outer_y in (-1, 0, 1):
            for outer_x in (-1, 0, 1):
                source = window[1 + outer_y, :, 1 + outer_x:1 + outer_x + half_cols].astype(jnp.float32)
                shift_y, shift_x, cycle_mask, code_table = offset_tables(outer_y, outer_x)
                couple = coupling(box_width, shift_y, shift_x)
                if height > 0:
                    couple = rounded_copy(couple * jnp.asarray(cycle_mask)[..., None, None])
                    accumulated = accumulated + jnp.einsum('abcdkm,axbmr->cxdkr', couple, source)
                else:
                    couple = rounded_copy(couple)
                    products = jnp.einsum('abcdkm,axbmr->xabcdkr', couple, source)
                    row_lists = lax.dynamic_index_in_dim(list_blocks, row_index, 0, keepdims=False)
                    listed = jnp.any(row_lists[:, None, None, :, :, :] == jnp.asarray(code_table)[None, :, :, :, :, None], axis=-1)
                    far_mask = 1.0 - listed.astype(jnp.float32)
                    masked_sum = lax.optimization_barrier(jnp.sum(products * far_mask[..., None, None], axis=(1, 2)))
                    accumulated = accumulated + masked_sum.transpose(1, 0, 2, 3, 4)
        return accumulated
    rows_out = lax.map(parent_row, jnp.arange(half_rows, dtype=jnp.int32))
    return rows_out.reshape(rows_all, cols_all, RANK, sample_count)

def reference(charges, positions, noise, leaf_basis, transfer, near_list):
    sample_count = charges.shape[-1]
    row_ids = jnp.arange(GY, dtype=jnp.int32)

    def leaf_lift(row_index):
        lifted_row = jnp.einsum('xkp,xpr->xkr', leaf_basis[row_index].astype(jnp.float32), charges[row_index].astype(jnp.float32))
        return lifted_row.astype(jnp.bfloat16)
    coeffs = [lax.map(leaf_lift, row_ids)]
    for height in range(LEVELS + 1):
        matrices = level_matrices(transfer, height).astype(jnp.float32)
        lifted = jnp.einsum('yxkm,yxmr->yxkr', matrices, coeffs[-1].astype(jnp.float32))
        lifted = lifted.reshape(lifted.shape[0] // 2, 2, lifted.shape[1] // 2, 2, RANK, sample_count).sum(axis=(1, 3))
        coeffs.append(lifted.astype(jnp.bfloat16))
    coupled = [level_far(coeffs[height], height, near_list) for height in range(LEVELS + 2)]
    field = coupled[LEVELS + 1].astype(jnp.bfloat16)
    for height in range(LEVELS, -1, -1):
        matrices = level_matrices(transfer, height).astype(jnp.float32)
        parent_rows = field.shape[0]
        parent_cols = field.shape[1]
        spread = jnp.broadcast_to(field[:, None, :, None], (parent_rows, 2, parent_cols, 2, RANK, sample_count))
        spread = spread.reshape(2 * parent_rows, 2 * parent_cols, RANK, sample_count)
        summed = coupled[height] + jnp.einsum('yxkm,yxkr->yxmr', matrices, spread.astype(jnp.float32))
        field = summed.astype(jnp.bfloat16)
    padded_charges = jnp.pad(charges, ((2, 2), (2, 2), (0, 0), (0, 0)))
    padded_points = jnp.pad(positions, ((2, 2), (2, 2), (0, 0), (0, 0)))
    column_ids = jnp.arange(GX, dtype=jnp.int32)

    def output_row(row_index):
        code_row = near_list[row_index]
        present = code_row >= 0
        shift_y = jnp.where(present, code_row // 5 - 2, 0)
        shift_x = jnp.where(present, code_row % 5 - 2, 0)
        row_target = row_index + 2 + shift_y
        col_target = column_ids[:, None] + 2 + shift_x
        target = positions[row_index]

        def one_slot(accumulated, slot):
            rows_here = row_target[:, slot]
            cols_here = col_target[:, slot]
            sources = padded_charges[rows_here, cols_here].astype(jnp.float32)
            source_points = padded_points[rows_here, cols_here]
            gap_x = target[:, 0, :, None] - source_points[:, 0, None, :] - shift_x[:, slot].astype(jnp.float32)[:, None, None]
            gap_y = target[:, 1, :, None] - source_points[:, 1, None, :] - shift_y[:, slot].astype(jnp.float32)[:, None, None]
            blocks = jnp.where(present[:, slot, None, None], kernel(gap_x * gap_x + gap_y * gap_y), 0.0)
            blocks = rounded_copy(blocks)
            return (accumulated + jnp.einsum('gij,gjr->gir', blocks, sources), None)
        near_field = lax.scan(one_slot, jnp.zeros((GX, LEAF, sample_count), jnp.float32), jnp.arange(NEAR, dtype=jnp.int32))[0]
        far_field = jnp.einsum('xkp,xkr->xpr', leaf_basis[row_index].astype(jnp.float32), field[row_index].astype(jnp.float32))
        combined = near_field + noise[row_index][..., None] * charges[row_index].astype(jnp.float32) + far_field
        return combined.astype(jnp.bfloat16)
    return lax.map(output_row, row_ids)
```

```python
import math

import jax
import jax.numpy as jnp
import ml_dtypes
import numpy as np
from jax import lax
from jax.experimental import pallas as pl
from jax.experimental.pallas import tpu as pltpu
from jax.sharding import PartitionSpec as P

LEAF = 256
CHEB = 8
RANK = 64
NEAR = 10
SIDE = 4
LEAVES = SIDE * SIDE
TOP = 20
WINDOW = 36
PACK = RANK + 16
SIDEWAYS = 8 * RANK + 4 * RANK + 48
CORNER = 4 * RANK + 4 * RANK + 48
BF = jnp.bfloat16
F32 = jnp.float32

short_len = 0.125
long_weight = 0.03125
reach = 3.0 * SIDE
waves = 10.0
LOG2E = math.log2(math.e)
long_rate = -0.5 / (reach * reach) * LOG2E / (waves * waves)
short_rate = -0.5 / (short_len * short_len) * LOG2E / (waves * waves)
rounder = 1.5 * 2.0**23


def sine_terms(count):
    w = np.cos(np.pi * (np.arange(2000) + 0.5) / 2000) * 0.25
    powers = np.stack([w ** (2 * i + 1) for i in range(count)], 1)
    return [float(c) for c in np.linalg.lstsq(powers, np.sin(2 * np.pi * w) * long_weight, rcond=None)[0]]


SINE = sine_terms(4)


def coupling(height, shift_y, shift_x):
    points = 0.5 * (1.0 + np.cos((2.0 * np.arange(CHEB) + 1.0) * (math.pi / (2.0 * CHEB))))
    node_x = np.tile(points, CHEB)
    node_y = np.repeat(points, CHEB)
    gap_x = (node_x[:, None] - node_x[None, :] - shift_x) * 2.0**height
    gap_y = (node_y[:, None] - node_y[None, :] - shift_y) * 2.0**height
    squared = gap_x * gap_x + gap_y * gap_y
    return np.exp(squared * (-0.5 / (short_len * short_len))) + long_weight * np.exp(
        squared * (-0.5 / (reach * reach))
    ) * np.cos(2.0 * math.pi * waves * np.sqrt(squared))


def window_coupling(height):
    table = np.zeros((2, 2, RANK, 6, 6, RANK))
    for py in range(2):
        for px in range(2):
            for wy in range(6):
                for wx in range(6):
                    shift_y, shift_x = wy - 2 - py, wx - 2 - px
                    if max(abs(shift_y), abs(shift_x)) >= 2:
                        table[py, px, :, wy, wx] = coupling(height, shift_y, shift_x)
    return table.reshape(4 * RANK, WINDOW * RANK).astype(ml_dtypes.bfloat16)


def code_coupling():
    return np.stack([coupling(0, code // 5 - 2, code % 5 - 2) for code in range(25)]).astype(ml_dtypes.bfloat16)


def halo_slot(row, col):
    if 0 <= row < 4 and 0 <= col < 4:
        return row * 4 + col
    if 0 <= row < 4:
        return 16 + row * 2 + col + 2 if col < 0 else 24 + row * 2 + col - 4
    base, r = (32, row + 2) if row < 0 else (48, row - 4)
    if 0 <= col < 4:
        return base + r * 4 + col
    return base + 8 + r * 2 + col + 2 if col < 0 else base + 12 + r * 2 + col - 4


SLOT_OF = np.array([halo_slot(r - 2, c - 2) for r in range(8) for c in range(8)], np.int32)


def near_table(own):
    width = 9 if own else 5
    table = np.zeros((LEAVES, width, 3), np.int32)
    table[:, :, 0] = -1
    for r in range(SIDE):
        for c in range(SIDE):
            at = 0
            for dy in (-1, 0, 1):
                for dx in (-1, 0, 1):
                    slot = halo_slot(r + dy, c + dx)
                    if (slot < LEAVES) == own:
                        table[r * SIDE + c, at] = (slot, dy, dx)
                        at += 1
    return table


def bits(count):
    return [1 << i for i in range(count.bit_length() - 1)]


def gather_steps(wide, narrow):
    return (
        [("wide", 1), ("narrow", 1)]
        + [("wide", b) for b in reversed(bits(wide)[1:])]
        + [("narrow", b) for b in reversed(bits(narrow)[1:])]
    )


def shift(value, axis, steps):
    count = lax.axis_size(axis)
    return lax.ppermute(value, axis, [(i, i + steps) for i in range(count) if 0 <= i + steps < count])


def dot(a, b):
    return jnp.dot(a, b, preferred_element_type=F32)


def dot_first(a, b):
    return lax.dot_general(a, b, (((0,), (0,)), ((), ())), preferred_element_type=F32)


def up_body(q_ref, basis_ref, tree_ref, pos_ref, east_ref, west_ref, north_ref, south_ref, coef_ref, give_ref):
    level0 = []
    for leaf in range(LEAVES):
        coef = dot(basis_ref[leaf], q_ref[leaf]).astype(BF)
        level0.append(coef)
        r, c = leaf // SIDE, leaf % SIDE
        coef_ref[leaf * RANK : (leaf + 1) * RANK] = coef
        ref, at = (west_ref, r * 2 + c) if c < 2 else (east_ref, r * 2 + c - 2)
        ref[at * RANK : (at + 1) * RANK] = coef
        ref, at = (north_ref, r * 4 + c) if r < 2 else (south_ref, r * 4 + c - 8)
        ref[at * RANK : (at + 1) * RANK] = coef
    level1 = []
    for r in range(2):
        for c in range(2):
            total = None
            for dr in range(2):
                for dc in range(2):
                    leaf = (2 * r + dr) * SIDE + 2 * c + dc
                    part = dot(tree_ref[leaf], level0[leaf])
                    total = part if total is None else total + part
            coef = total.astype(BF)
            at = r * 2 + c
            level1.append(coef)
            coef_ref[(LEAVES + at) * RANK : (LEAVES + at + 1) * RANK] = coef
            for ref in (east_ref, west_ref, north_ref, south_ref):
                ref[(8 + at) * RANK : (9 + at) * RANK] = coef
    total = None
    for at in range(4):
        part = dot(tree_ref[LEAVES + at], level1[at])
        total = part if total is None else total + part
    give_ref[0:RANK] = total.astype(BF)
    top = tree_ref[TOP]
    give_ref[RANK:PACK] = jnp.concatenate([top[16 * k : 16 * k + 16] for k in range(4)], axis=1)
    for ref, leaves in (
        (west_ref, [r * 4 + c for r in range(4) for c in (0, 1)]),
        (east_ref, [r * 4 + c for r in range(4) for c in (2, 3)]),
        (north_ref, range(8)),
        (south_ref, range(8, 16)),
    ):
        rest = jnp.concatenate([pos_ref[leaf] for leaf in leaves], axis=0)
        for part in range(3):
            held = rest.astype(BF)
            at = 12 * RANK + 16 * part
            ref[at : at + 16] = held
            rest = rest - held.astype(F32)


def go_up(q, basis, tree, points):
    vmem = pl.BlockSpec(memory_space=pltpu.VMEM)
    side = jax.ShapeDtypeStruct((SIDEWAYS, LEAF), BF)
    return pl.pallas_call(
        up_body,
        out_shape=(
            side,
            side,
            side,
            side,
            jax.ShapeDtypeStruct(((LEAVES + 4) * RANK, LEAF), BF),
            jax.ShapeDtypeStruct((PACK, LEAF), BF),
        ),
        in_specs=[vmem] * 4,
        out_specs=[vmem] * 6,
        compiler_params=pltpu.CompilerParams(vmem_limit_bytes=32 << 20),
        cost_estimate=pl.CostEstimate(flops=300_000_000, bytes_accessed=5_000_000, transcendentals=0),
        name="upward",
    )(q, basis, tree, points)


def far_body(
    list_ref,
    meta_ref,
    coef_ref,
    west_ref,
    east_ref,
    north_ref,
    south_ref,
    all_ref,
    c0_ref,
    c1_ref,
    c2_ref,
    c3_ref,
    code_ref,
    tree_ref,
    field_ref,
    pad0,
    pad1,
    win,
    parents,
    sum0,
):
    def put(pad, extent, row, col, ref, at, count):
        to = ((row + 2) * (extent + 4) + col + 2) * RANK
        pad[to : to + count * RANK] = ref[at * RANK : (at + count) * RANK]

    for r in range(4):
        put(pad0, 4, r, 0, coef_ref, r * 4, 4)
        put(pad0, 4, r, -2, west_ref, r * 2, 2)
        put(pad0, 4, r, 4, east_ref, r * 2, 2)
    for ref, row in ((north_ref, -2), (south_ref, 4)):
        for r in range(2):
            put(pad0, 4, row + r, 0, ref, r * 4, 4)
    for r in range(2):
        put(pad1, 2, r, 0, coef_ref, LEAVES + r * 2, 2)
        put(pad1, 2, r, -2, west_ref, 8 + r * 2, 2)
        put(pad1, 2, r, 2, east_ref, 8 + r * 2, 2)
    for ref, row in ((north_ref, -2), (south_ref, 2)):
        for r in range(2):
            put(pad1, 2, row + r, 0, ref, 8 + r * 2, 2)
    for ref, row0, row1 in ((north_ref, -2, -2), (south_ref, 4, 2)):
        for col0, col1, base in ((-2, -2, SIDEWAYS), (4, 2, SIDEWAYS + CORNER)):
            for r in range(2):
                to = ((row0 + r + 2) * 8 + col0 + 2) * RANK
                pad0[to : to + 2 * RANK] = ref[base + r * 2 * RANK : base + (r + 1) * 2 * RANK]
                to = ((row1 + r + 2) * 6 + col1 + 2) * RANK
                pad1[to : to + 2 * RANK] = ref[base + (4 + r * 2) * RANK : base + (6 + r * 2) * RANK]

    for a in range(2):
        for b in range(2):
            total = None
            for wy in range(6):
                at = ((2 * a + wy) * 8 + 2 * b) * RANK
                part = dot(c0_ref[:, wy * 6 * RANK : (wy + 1) * 6 * RANK], pad0[at : at + 6 * RANK])
                total = part if total is None else total + part
            for child in range(4):
                leaf = (2 * a + child // 2) * SIDE + 2 * b + child % 2
                sum0[leaf] = total[child * RANK : (child + 1) * RANK]

    def listed(leaf, carry):
        code = second_cycle(list_ref, leaf)

        @pl.when(code >= 0)
        def _():
            row = leaf // SIDE + code // 5
            col = leaf % SIDE + code % 5
            at = pl.multiple_of((row * 8 + col) * RANK, RANK)
            sum0[leaf] = sum0[leaf] - dot(code_ref[code], pad0[pl.ds(at, RANK)])

        return carry

    lax.fori_loop(0, LEAVES, listed, 0)
    sum1 = dot(c1_ref[...], pad1[...])

    def lift(group, carry):
        total = jnp.zeros((RANK, LEAF), F32)
        for child in range(4):
            at = pl.multiple_of((group * 4 + child) * PACK, 16)
            packed = all_ref[pl.ds(at + RANK, 16)]
            matrix = jnp.concatenate([packed[:, k * RANK : (k + 1) * RANK] for k in range(4)], axis=0)
            total = total + dot(matrix, all_ref[pl.ds(at, RANK)])
        parents[pl.ds(pl.multiple_of(group * RANK, RANK), RANK)] = total.astype(BF)
        return carry

    lax.fori_loop(0, parents.shape[0] // RANK, lift, 0)

    def fill(start, source, stride):
        def one(i, carry):
            slot = meta_ref[start + i]
            to = pl.ds(pl.multiple_of(i * RANK, RANK), RANK)

            @pl.when(slot >= 0)
            def _():
                win[to] = source[pl.ds(pl.multiple_of(slot * stride, 16), RANK)]

            @pl.when(slot < 0)
            def _():
                win[to] = jnp.zeros((RANK, LEAF), BF)

            return carry

        lax.fori_loop(0, WINDOW, one, 0)

    fill(WINDOW, parents, RANK)
    part = pl.ds(pl.multiple_of(meta_ref[2 * WINDOW + 1] * RANK, RANK), RANK)
    field3 = dot(c3_ref[part], win[...]).astype(BF)
    fill(0, all_ref, PACK)
    part = pl.ds(pl.multiple_of(meta_ref[2 * WINDOW] * RANK, RANK), RANK)
    field2 = (dot(c2_ref[part], win[...]) + dot_first(tree_ref[TOP], field3)).astype(BF)
    field1 = []
    for at in range(4):
        field1.append(
            (sum1[at * RANK : (at + 1) * RANK] + dot_first(tree_ref[LEAVES + at], field2)).astype(BF)
        )
    for leaf in range(LEAVES):
        above = field1[leaf // SIDE // 2 * 2 + leaf % SIDE // 2]
        field_ref[leaf] = (sum0[leaf] + dot_first(tree_ref[leaf], above)).astype(BF)


def second_cycle(list_ref, leaf):
    found = jnp.int32(-1)
    for j in range(NEAR):
        code = list_ref[leaf * NEAR + j]
        y, x = code // 5, code % 5
        outer = (code >= 0) & ((y == 0) | (y == 4) | (x == 0) | (x == 4))
        found = jnp.where(outer, code, found)
    return found


def far_field(near_list, meta, coefs, west, east, north, south, gathered, tree):
    vmem = pl.BlockSpec(memory_space=pltpu.VMEM)
    smem = pl.BlockSpec(memory_space=pltpu.SMEM)
    devices = gathered.shape[0] // PACK
    return pl.pallas_call(
        far_body,
        out_shape=jax.ShapeDtypeStruct((LEAVES, RANK, LEAF), BF),
        in_specs=[smem, smem] + [vmem] * 12,
        out_specs=vmem,
        scratch_shapes=[
            pltpu.VMEM((64 * RANK, LEAF), BF),
            pltpu.VMEM((WINDOW * RANK, LEAF), BF),
            pltpu.VMEM((WINDOW * RANK, LEAF), BF),
            pltpu.VMEM((devices // 4 * RANK, LEAF), BF),
            pltpu.VMEM((LEAVES, RANK, LEAF), F32),
        ],
        compiler_params=pltpu.CompilerParams(vmem_limit_bytes=40 << 20),
        cost_estimate=pl.CostEstimate(flops=2_500_000_000, bytes_accessed=12_000_000, transcendentals=0),
        name="far",
    )(
        near_list,
        meta,
        coefs,
        west,
        east,
        north,
        south,
        gathered,
        *[jnp.asarray(window_coupling(height)) for height in range(4)],
        jnp.asarray(code_coupling()),
        tree,
    )


def kernel_of(target_x, target_y, source_x, source_y):
    gap_x = target_x - source_x
    gap_y = target_y - source_y
    squared = jnp.maximum(gap_x * gap_x + gap_y * gap_y, 1e-12)
    length = squared * lax.rsqrt(squared)
    phase = length - ((length + rounder) - rounder)
    w = 0.25 - jnp.abs(phase)
    s = w * w
    wave = w * (SINE[0] + s * (SINE[1] + s * (SINE[2] + s * SINE[3])))
    return (jnp.exp2(squared * short_rate) + jnp.exp2(squared * long_rate) * wave).astype(BF)


def spread_columns(rows, columns):
    turned = rows.T
    for k in range(columns.shape[1] // 128):
        columns[:, 128 * k : 128 * (k + 1)] = jnp.broadcast_to(turned[:, k : k + 1], (LEAF, 128))


def block_into(to, columns, points, shift_y, shift_x):
    source_x = (points[0:1] + shift_x.astype(F32)) * waves
    source_y = (points[1:2] + shift_y.astype(F32)) * waves
    rows = 32
    for i in range(0, LEAF, rows):
        for j in (0, 128):
            to[i : i + rows, j : j + 128] = kernel_of(
                columns[i : i + rows, 0:128],
                columns[i : i + rows, 128:256],
                jnp.broadcast_to(source_x[:, j : j + 128], (rows, 128)),
                jnp.broadcast_to(source_y[:, j : j + 128], (rows, 128)),
            )


def near_own_body(list_ref, table_ref, slot_ref, q_ref, pos_ref, noise_ref, out_ref, columns, blocks):
    leaf = pl.program_id(0)
    rows = jnp.concatenate([pos_ref[leaf] * waves, noise_ref[leaf], jnp.zeros((5, LEAF), F32)], axis=0)
    spread_columns(rows, columns)
    width = table_ref.shape[0] // (3 * LEAVES)
    own = q_ref[leaf].astype(F32)
    for j in (0, 128):
        out_ref[0, :, j : j + 128] = columns[:, 256:384] * own[:, j : j + 128]

    def one(j, carry):
        at = (leaf * width + j) * 3
        slot = table_ref[at]

        @pl.when(slot >= 0)
        def _():
            block_into(blocks.at[j], columns, pos_ref[slot], table_ref[at + 1], table_ref[at + 2])

        @pl.when(slot < 0)
        def _():
            blocks[j] = jnp.zeros((LEAF, LEAF), BF)

        return carry

    lax.fori_loop(0, width, one, 0)
    total = out_ref[0]
    for j in range(width):
        slot = jnp.maximum(table_ref[(leaf * width + j) * 3], 0)
        total = total + dot(blocks[j], q_ref[slot])
    out_ref[0] = total
    code = second_cycle(list_ref, leaf)
    place = (leaf // SIDE + code // 5) * 8 + leaf % SIDE + code % 5
    slot = slot_ref[jnp.where(code >= 0, place, 0)]

    @pl.when((code >= 0) & (slot < LEAVES))
    def _():
        block_into(blocks.at[0], columns, pos_ref[slot], code // 5 - 2, code % 5 - 2)
        out_ref[0] += dot(blocks[0], q_ref[slot])


def near_own(near_list, q, points, noise):
    vmem = pl.BlockSpec(memory_space=pltpu.VMEM)
    smem = pl.BlockSpec(memory_space=pltpu.SMEM)
    return pl.pallas_call(
        near_own_body,
        grid=(LEAVES,),
        out_shape=jax.ShapeDtypeStruct((LEAVES, LEAF, LEAF), F32),
        in_specs=[smem, smem, smem, vmem, vmem, vmem],
        out_specs=pl.BlockSpec((1, LEAF, LEAF), lambda i: (i, 0, 0)),
        scratch_shapes=[pltpu.VMEM((LEAF, 384), F32), pltpu.VMEM((9, LEAF, LEAF), BF)],
        compiler_params=pltpu.CompilerParams(vmem_limit_bytes=32 << 20),
        cost_estimate=pl.CostEstimate(flops=20_000_000_000, bytes_accessed=7_000_000, transcendentals=20_000_000),
        name="near_own",
    )(near_list, jnp.asarray(near_table(True).reshape(-1)), jnp.asarray(SLOT_OF), q, points, noise)


def near_halo_body(
    list_ref,
    table_ref,
    slot_ref,
    west_ref,
    east_ref,
    north_ref,
    north_corner_ref,
    south_ref,
    south_corner_ref,
    own_pos_ref,
    pos_ref,
    sum_ref,
    basis_ref,
    field_ref,
    out_ref,
    columns,
    blocks,
    held,
    total_ref,
    sems,
):
    leaf = pl.program_id(0)
    copies = [
        pltpu.make_async_copy(ref, held.at[pl.ds(8 * k, 8)], sems.at[k])
        for k, ref in enumerate(
            (west_ref, east_ref, north_ref, north_corner_ref, south_ref, south_corner_ref)
        )
    ]

    @pl.when(leaf == 0)
    def _():
        for copy in copies:
            copy.start()

    rows = jnp.concatenate([own_pos_ref[leaf] * waves, jnp.zeros((6, LEAF), F32)], axis=0)
    spread_columns(rows, columns)
    width = table_ref.shape[0] // (3 * LEAVES)

    def one(j, carry):
        at = (leaf * width + j) * 3
        slot = table_ref[at]

        @pl.when(slot >= 0)
        def _():
            block_into(blocks.at[j], columns, pos_ref[slot - LEAVES], table_ref[at + 1], table_ref[at + 2])

        return carry

    lax.fori_loop(0, width, one, 0)

    @pl.when(leaf == 0)
    def _():
        for copy in copies:
            copy.wait()


    def add(j, total):
        slot = table_ref[(leaf * width + j) * 3]
        return total + dot(blocks[j], held[slot - LEAVES])

    row, col = leaf // SIDE, leaf % SIDE
    edge_y = (row == 0) | (row == SIDE - 1)
    edge_x = (col == 0) | (col == SIDE - 1)
    corner = edge_y & edge_x
    total_ref[...] = sum_ref[0] + dot_first(basis_ref[leaf], field_ref[leaf])

    @pl.when(edge_y | edge_x)
    def _():
        total = total_ref[...]
        for j in range(3):
            total = add(j, total)
        total_ref[...] = total

    @pl.when(corner)
    def _():
        total = total_ref[...]
        for j in range(3, 5):
            total = add(j, total)
        total_ref[...] = total

    code = second_cycle(list_ref, leaf)
    place = (leaf // SIDE + code // 5) * 8 + leaf % SIDE + code % 5
    slot = slot_ref[jnp.where(code >= 0, place, 0)]

    @pl.when((code >= 0) & (slot >= LEAVES))
    def _():
        block_into(blocks.at[0], columns, pos_ref[slot - LEAVES], code // 5 - 2, code % 5 - 2)
        total_ref[...] += dot(blocks[0], held[slot - LEAVES])

    out_ref[0] = total_ref[...].astype(BF)


def near_halo(near_list, halos, own_points, halo_points, near_sum, basis, field):
    vmem = pl.BlockSpec(memory_space=pltpu.VMEM)
    smem = pl.BlockSpec(memory_space=pltpu.SMEM)
    block = pl.BlockSpec((1, LEAF, LEAF), lambda i: (i, 0, 0))
    return pl.pallas_call(
        near_halo_body,
        grid=(LEAVES,),
        out_shape=jax.ShapeDtypeStruct((LEAVES, LEAF, LEAF), BF),
        in_specs=[smem, smem, smem] + [pl.BlockSpec(memory_space=pl.ANY)] * 6 + [vmem, vmem, block, vmem, vmem],
        out_specs=block,
        scratch_shapes=[
            pltpu.VMEM((LEAF, 256), F32),
            pltpu.VMEM((5, LEAF, LEAF), BF),
            pltpu.VMEM((48, LEAF, LEAF), BF),
            pltpu.VMEM((LEAF, LEAF), F32),
            pltpu.SemaphoreType.DMA((6,)),
        ],
        compiler_params=pltpu.CompilerParams(vmem_limit_bytes=32 << 20),
        cost_estimate=pl.CostEstimate(flops=8_000_000_000, bytes_accessed=14_000_000, transcendentals=8_000_000),
        name="near_halo",
    )(
        near_list,
        jnp.asarray(near_table(False).reshape(-1)),
        jnp.asarray(SLOT_OF),
        *halos,
        own_points,
        halo_points,
        near_sum,
        basis,
        field,
    )


def points_of(message, leaves_at):
    parts = message[leaves_at : leaves_at + 48].astype(F32)
    whole = (parts[0:16] + parts[16:32]) + parts[32:48]
    return whole.reshape(8, 2, LEAF)


def window_slots(wide, narrow, steps):
    row, col = lax.axis_index("narrow"), lax.axis_index("wide")
    wy, wx = np.arange(WINDOW) // 6, np.arange(WINDOW) % 6

    def slots(target_y, target_x, scale):
        y = target_y // 2 * 2 - 2 + wy
        x = target_x // 2 * 2 - 2 + wx
        inside = (y >= 0) & (y < narrow // scale) & (x >= 0) & (x < wide // scale)
        apart = {"narrow": (y * scale) ^ row, "wide": (x * scale) ^ col}
        slot = 0
        for at, (axis, bit) in enumerate(steps):
            slot = slot + (apart[axis] // bit & 1) * (1 << at)
        return jnp.where(inside, slot if scale == 1 else slot // 4, -1)

    parity2 = row % 2 * 2 + col % 2
    parity3 = row // 2 % 2 * 2 + col // 2 % 2
    return jnp.concatenate(
        [slots(row, col, 1), slots(row // 2, col // 2, 2), jnp.stack([parity2, parity3])]
    ).astype(jnp.int32)


def per_device(wide, narrow, charges, positions, noise, leaf_basis, transfer, near_list):
    q = charges.reshape(LEAVES, LEAF, LEAF)
    points = positions.reshape(LEAVES, 2, LEAF)
    basis = leaf_basis.reshape(LEAVES, RANK, LEAF)
    tree = transfer[0, 0]
    listing = near_list.reshape(-1)
    steps = gather_steps(wide, narrow)
    meta = window_slots(wide, narrow, steps)

    east, west, north, south, coefs, give = go_up(q, basis, tree, points)
    from_west = shift(east, "wide", 1)
    from_east = shift(west, "wide", -1)
    gathered = give
    for axis, bit in steps:
        other = lax.ppermute(gathered, axis, [(i, i ^ bit) for i in range(lax.axis_size(axis))])
        gathered = jnp.concatenate([gathered, other], axis=0)

    def corner(message, lower):
        at = 4 * RANK if lower else 0
        return [message[at : at + 4 * RANK], message[8 * RANK :]]

    north = jnp.concatenate([north] + corner(from_west, False) + corner(from_east, False), axis=0)
    south = jnp.concatenate([south] + corner(from_west, True) + corner(from_east, True), axis=0)
    from_south = shift(north, "narrow", -1)
    from_north = shift(south, "narrow", 1)

    q_west = shift(charges[:, 2:4], "wide", 1)
    q_east = shift(charges[:, 0:2], "wide", -1)
    q_north = shift(charges[2:4], "narrow", 1)
    q_south = shift(charges[0:2], "narrow", -1)
    q_north_corner = shift(jnp.stack([q_west[2:4], q_east[2:4]]), "narrow", 1)
    q_south_corner = shift(jnp.stack([q_west[0:2], q_east[0:2]]), "narrow", -1)
    halos = [
        value.reshape(8, LEAF, LEAF)
        for value in (q_west, q_east, q_north, q_north_corner, q_south, q_south_corner)
    ]

    def corner_points(message, lower):
        first = points_of(message, SIDEWAYS + 8 * RANK)
        second = points_of(message, SIDEWAYS + CORNER + 8 * RANK)
        at = 4 if lower else 0
        return [first[at : at + 4], second[at : at + 4]]

    halo_points = jnp.concatenate(
        [points_of(from_west, 12 * RANK), points_of(from_east, 12 * RANK), points_of(from_north, 12 * RANK)]
        + corner_points(from_north, True)
        + [points_of(from_south, 12 * RANK)]
        + corner_points(from_south, False),
        axis=0,
    )

    near_sum = near_own(listing, q, points, noise.reshape(LEAVES, 1, LEAF))
    field = far_field(listing, meta, coefs, from_west, from_east, from_north, from_south, gathered, tree)
    out = near_halo(listing, halos, points, halo_points, near_sum, basis, field)
    return out.reshape(SIDE, SIDE, LEAF, LEAF)


def solution(mesh):
    wide, narrow = mesh.shape["wide"], mesh.shape["narrow"]
    in_specs = (
        P("narrow", "wide", None, None),
        P("narrow", "wide", None, None),
        P("narrow", "wide", None),
        P("narrow", "wide", None, None),
        P("narrow", "wide", None, None, None),
        P("narrow", "wide", None),
    )
    out_specs = P("narrow", "wide", None, None)

    def step(*arrays):
        return per_device(wide, narrow, *arrays)

    return jax.shard_map(step, mesh=mesh, in_specs=in_specs, out_specs=out_specs, check_vma=False)
```

```python
import math

import jax
import jax.numpy as jnp
import ml_dtypes
import numpy as np
from jax import lax
from jax.experimental import pallas as pl
from jax.experimental.pallas import tpu as pltpu
from jax.sharding import PartitionSpec as P

LEAF = 256
CHEB = 8
RANK = 64
NEAR = 10
SIDE = 4
LEAVES = SIDE * SIDE
TOP = 20
WINDOW = 36
PACK = RANK + 16
SIDEWAYS = 8 * RANK + 4 * RANK + 48
CORNER = 4 * RANK + 4 * RANK + 48
COPIES = 42
BF = jnp.bfloat16
F32 = jnp.float32

short_len = 0.125
long_weight = 0.03125
reach = 3.0 * SIDE
waves = 10.0
LOG2E = math.log2(math.e)
long_rate = -0.5 / (reach * reach) * LOG2E / (waves * waves)
short_rate = -0.5 / (short_len * short_len) * LOG2E / (waves * waves)
rounder = 1.5 * 2.0**23


def sine_terms(count):
    w = np.cos(np.pi * (np.arange(2000) + 0.5) / 2000) * 0.25
    powers = np.stack([w ** (2 * i + 1) for i in range(count)], 1)
    return [float(c) for c in np.linalg.lstsq(powers, np.sin(2 * np.pi * w) * long_weight, rcond=None)[0]]


SINE = sine_terms(4)


def coupling(height, shift_y, shift_x):
    points = 0.5 * (1.0 + np.cos((2.0 * np.arange(CHEB) + 1.0) * (math.pi / (2.0 * CHEB))))
    node_x = np.tile(points, CHEB)
    node_y = np.repeat(points, CHEB)
    gap_x = (node_x[:, None] - node_x[None, :] - shift_x) * 2.0**height
    gap_y = (node_y[:, None] - node_y[None, :] - shift_y) * 2.0**height
    squared = gap_x * gap_x + gap_y * gap_y
    return np.exp(squared * (-0.5 / (short_len * short_len))) + long_weight * np.exp(
        squared * (-0.5 / (reach * reach))
    ) * np.cos(2.0 * math.pi * waves * np.sqrt(squared))


def window_coupling(height):
    table = np.zeros((2, 2, RANK, 6, 6, RANK))
    for py in range(2):
        for px in range(2):
            for wy in range(6):
                for wx in range(6):
                    shift_y, shift_x = wy - 2 - py, wx - 2 - px
                    if max(abs(shift_y), abs(shift_x)) >= 2:
                        table[py, px, :, wy, wx] = coupling(height, shift_y, shift_x)
    return table.reshape(4 * RANK, WINDOW * RANK).astype(ml_dtypes.bfloat16)


def code_coupling():
    return np.stack([coupling(0, code // 5 - 2, code % 5 - 2) for code in range(25)]).astype(ml_dtypes.bfloat16)


def halo_slot(row, col):
    if 0 <= row < 4 and 0 <= col < 4:
        return row * 4 + col
    if 0 <= row < 4:
        return 16 + row * 2 + col + 2 if col < 0 else 24 + row * 2 + col - 4
    base, r = (32, row + 2) if row < 0 else (48, row - 4)
    if 0 <= col < 4:
        return base + r * 4 + col
    return base + 8 + r * 2 + col + 2 if col < 0 else base + 12 + r * 2 + col - 4


SLOT_OF = np.array([halo_slot(r - 2, c - 2) for r in range(8) for c in range(8)], np.int32)


def near_table(own):
    width = 9 if own else 5
    table = np.zeros((LEAVES, width, 3), np.int32)
    table[:, :, 0] = -1
    for r in range(SIDE):
        for c in range(SIDE):
            at = 0
            for dy in (-1, 0, 1):
                for dx in (-1, 0, 1):
                    slot = halo_slot(r + dy, c + dx)
                    if (slot < LEAVES) == own:
                        table[r * SIDE + c, at] = (slot, dy, dx)
                        at += 1
    return table


def bits(count):
    return [1 << i for i in range(count.bit_length() - 1)]


def gather_steps(wide, narrow):
    return (
        [("wide", 1), ("narrow", 1)]
        + [("wide", b) for b in reversed(bits(wide)[1:])]
        + [("narrow", b) for b in reversed(bits(narrow)[1:])]
    )


def shift(value, axis, steps):
    count = lax.axis_size(axis)
    return lax.ppermute(value, axis, [(i, i + steps) for i in range(count) if 0 <= i + steps < count])


def dot(a, b):
    return jnp.dot(a, b, preferred_element_type=F32)


def dot_first(a, b):
    return lax.dot_general(a, b, (((0,), (0,)), ((), ())), preferred_element_type=F32)


def up_body(
    q_any, basis_any, tree_any, pos_ref, east_ref, west_ref, north_ref, south_ref, coef_ref, give_ref, q_ref, basis_ref, tree_ref, sems
):
    loads = []
    for k in range(4):
        part = pl.ds(4 * k, 4)
        loads.append(pltpu.make_async_copy(basis_any.at[part], basis_ref.at[part], sems.at[2 * k]))
        loads.append(pltpu.make_async_copy(q_any.at[part], q_ref.at[part], sems.at[2 * k + 1]))
    loads.append(pltpu.make_async_copy(tree_any, tree_ref, sems.at[8]))
    for load in loads:
        load.start()
    level0 = []
    for leaf in range(LEAVES):
        if leaf % 4 == 0:
            loads[leaf // 2].wait()
            loads[leaf // 2 + 1].wait()
        coef = dot(basis_ref[leaf], q_ref[leaf]).astype(BF)
        level0.append(coef)
        r, c = leaf // SIDE, leaf % SIDE
        coef_ref[leaf * RANK : (leaf + 1) * RANK] = coef
        ref, at = (west_ref, r * 2 + c) if c < 2 else (east_ref, r * 2 + c - 2)
        ref[at * RANK : (at + 1) * RANK] = coef
        ref, at = (north_ref, r * 4 + c) if r < 2 else (south_ref, r * 4 + c - 8)
        ref[at * RANK : (at + 1) * RANK] = coef
    loads[8].wait()
    level1 = []
    for r in range(2):
        for c in range(2):
            total = None
            for dr in range(2):
                for dc in range(2):
                    leaf = (2 * r + dr) * SIDE + 2 * c + dc
                    part = dot(tree_ref[leaf], level0[leaf])
                    total = part if total is None else total + part
            coef = total.astype(BF)
            at = r * 2 + c
            level1.append(coef)
            coef_ref[(LEAVES + at) * RANK : (LEAVES + at + 1) * RANK] = coef
            for ref in (east_ref, west_ref, north_ref, south_ref):
                ref[(8 + at) * RANK : (9 + at) * RANK] = coef
    total = None
    for at in range(4):
        part = dot(tree_ref[LEAVES + at], level1[at])
        total = part if total is None else total + part
    give_ref[0:RANK] = total.astype(BF)
    top = tree_ref[TOP]
    give_ref[RANK:PACK] = jnp.concatenate([top[16 * k : 16 * k + 16] for k in range(4)], axis=1)
    for ref, leaves in (
        (west_ref, [r * 4 + c for r in range(4) for c in (0, 1)]),
        (east_ref, [r * 4 + c for r in range(4) for c in (2, 3)]),
        (north_ref, range(8)),
        (south_ref, range(8, 16)),
    ):
        rest = jnp.concatenate([pos_ref[leaf] for leaf in leaves], axis=0)
        for part in range(3):
            held = rest.astype(BF)
            at = 12 * RANK + 16 * part
            ref[at : at + 16] = held
            rest = rest - held.astype(F32)


def go_up(q, basis, tree, points):
    vmem = pl.BlockSpec(memory_space=pltpu.VMEM)
    side = jax.ShapeDtypeStruct((SIDEWAYS, LEAF), BF)
    return pl.pallas_call(
        up_body,
        out_shape=(
            side,
            side,
            side,
            side,
            jax.ShapeDtypeStruct(((LEAVES + 4) * RANK, LEAF), BF),
            jax.ShapeDtypeStruct((PACK, LEAF), BF),
        ),
        in_specs=[pl.BlockSpec(memory_space=pl.ANY)] * 3 + [vmem],
        out_specs=[vmem] * 6,
        scratch_shapes=[
            pltpu.VMEM((LEAVES, LEAF, LEAF), BF),
            pltpu.VMEM((LEAVES, RANK, LEAF), BF),
            pltpu.VMEM((TOP + 1, RANK, RANK), BF),
            pltpu.SemaphoreType.DMA((9,)),
        ],
        compiler_params=pltpu.CompilerParams(vmem_limit_bytes=32 << 20),
        cost_estimate=pl.CostEstimate(flops=300_000_000, bytes_accessed=5_000_000, transcendentals=0),
        name="upward",
    )(q, basis, tree, points)


def far_body(
    list_ref,
    meta_ref,
    coef_any,
    west_any,
    east_any,
    north_any,
    south_any,
    all_any,
    c0_any,
    c1_any,
    c2_any,
    c3_any,
    code_any,
    tree_any,
    field_ref,
    pad0,
    pad1,
    win,
    parents,
    sum0,
    all_ref,
    c0_ref,
    c1_ref,
    c2_ref,
    c3_ref,
    code_ref,
    tree_ref,
    sems,
):
    loads = []

    def load(source, at, to, row, count):
        rows = pl.ds(at * RANK if at < 100 else at, count * RANK)
        copy = pltpu.make_async_copy(source.at[rows], to.at[pl.ds(row, count * RANK)], sems.at[len(loads)])
        copy.start()
        loads.append(copy)

    def put(pad, extent, row, col, ref, at, count):
        load(ref, at, pad, ((row + 2) * (extent + 4) + col + 2) * RANK, count)

    whole = []
    for k, (source, to) in enumerate(((c0_any, c0_ref), (c1_any, c1_ref), (code_any, code_ref), (tree_any, tree_ref), (all_any, all_ref), (c3_any, c3_ref), (c2_any, c2_ref))):
        whole.append(pltpu.make_async_copy(source, to, sems.at[COPIES + k]))
    whole[0].start()
    for r in range(4):
        put(pad0, 4, r, 0, coef_any, r * 4, 4)
        put(pad0, 4, r, -2, west_any, r * 2, 2)
        put(pad0, 4, r, 4, east_any, r * 2, 2)
    for ref, row in ((north_any, -2), (south_any, 4)):
        for r in range(2):
            put(pad0, 4, row + r, 0, ref, r * 4, 4)
            for col, base in ((-2, SIDEWAYS), (4, SIDEWAYS + CORNER)):
                load(ref, base + r * 2 * RANK, pad0, ((row + r + 2) * 8 + col + 2) * RANK, 2)
    split = len(loads)
    for copy in whole[1:]:
        copy.start()
    for r in range(2):
        put(pad1, 2, r, 0, coef_any, LEAVES + r * 2, 2)
        put(pad1, 2, r, -2, west_any, 8 + r * 2, 2)
        put(pad1, 2, r, 2, east_any, 8 + r * 2, 2)
    for ref, row in ((north_any, -2), (south_any, 2)):
        for r in range(2):
            put(pad1, 2, row + r, 0, ref, 8 + r * 2, 2)
            for col, base in ((-2, SIDEWAYS), (2, SIDEWAYS + CORNER)):
                load(ref, base + (4 + r * 2) * RANK, pad1, ((row + r + 2) * 6 + col + 2) * RANK, 2)
    whole[0].wait()
    for copy in loads[:split]:
        copy.wait()

    for a in range(2):
        for b in range(2):
            total = None
            for wy in range(6):
                at = ((2 * a + wy) * 8 + 2 * b) * RANK
                part = dot(c0_ref[:, wy * 6 * RANK : (wy + 1) * 6 * RANK], pad0[at : at + 6 * RANK])
                total = part if total is None else total + part
            for child in range(4):
                leaf = (2 * a + child // 2) * SIDE + 2 * b + child % 2
                sum0[leaf] = total[child * RANK : (child + 1) * RANK]

    for copy in loads[split:] + whole[1:]:
        copy.wait()

    def listed(leaf, carry):
        code = second_cycle(list_ref, leaf)

        @pl.when(code >= 0)
        def _():
            row = leaf // SIDE + code // 5
            col = leaf % SIDE + code % 5
            at = pl.multiple_of((row * 8 + col) * RANK, RANK)
            sum0[leaf] = sum0[leaf] - dot(code_ref[code], pad0[pl.ds(at, RANK)])

        return carry

    lax.fori_loop(0, LEAVES, listed, 0)
    sum1 = dot(c1_ref[...], pad1[...])

    def lift(group, carry):
        total = jnp.zeros((RANK, LEAF), F32)
        for child in range(4):
            at = pl.multiple_of((group * 4 + child) * PACK, 16)
            packed = all_ref[pl.ds(at + RANK, 16)]
            matrix = jnp.concatenate([packed[:, k * RANK : (k + 1) * RANK] for k in range(4)], axis=0)
            total = total + dot(matrix, all_ref[pl.ds(at, RANK)])
        parents[pl.ds(pl.multiple_of(group * RANK, RANK), RANK)] = total.astype(BF)
        return carry

    lax.fori_loop(0, parents.shape[0] // RANK, lift, 0)

    def fill(start, source, stride):
        def one(i, carry):
            slot = meta_ref[start + i]
            to = pl.ds(pl.multiple_of(i * RANK, RANK), RANK)

            @pl.when(slot >= 0)
            def _():
                win[to] = source[pl.ds(pl.multiple_of(slot * stride, 16), RANK)]

            @pl.when(slot < 0)
            def _():
                win[to] = jnp.zeros((RANK, LEAF), BF)

            return carry

        lax.fori_loop(0, WINDOW, one, 0)

    fill(WINDOW, parents, RANK)
    part = pl.ds(pl.multiple_of(meta_ref[2 * WINDOW + 1] * RANK, RANK), RANK)
    field3 = dot(c3_ref[part], win[...]).astype(BF)
    fill(0, all_ref, PACK)
    part = pl.ds(pl.multiple_of(meta_ref[2 * WINDOW] * RANK, RANK), RANK)
    field2 = (dot(c2_ref[part], win[...]) + dot_first(tree_ref[TOP], field3)).astype(BF)
    field1 = []
    for at in range(4):
        field1.append(
            (sum1[at * RANK : (at + 1) * RANK] + dot_first(tree_ref[LEAVES + at], field2)).astype(BF)
        )
    for leaf in range(LEAVES):
        above = field1[leaf // SIDE // 2 * 2 + leaf % SIDE // 2]
        field_ref[leaf] = (sum0[leaf] + dot_first(tree_ref[leaf], above)).astype(BF)


def second_cycle(list_ref, leaf):
    found = jnp.int32(-1)
    for j in range(NEAR):
        code = list_ref[leaf * NEAR + j]
        y, x = code // 5, code % 5
        outer = (code >= 0) & ((y == 0) | (y == 4) | (x == 0) | (x == 4))
        found = jnp.where(outer, code, found)
    return found


def far_field(near_list, meta, coefs, west, east, north, south, gathered, tree):
    vmem = pl.BlockSpec(memory_space=pltpu.VMEM)
    smem = pl.BlockSpec(memory_space=pltpu.SMEM)
    devices = gathered.shape[0] // PACK
    return pl.pallas_call(
        far_body,
        out_shape=jax.ShapeDtypeStruct((LEAVES, RANK, LEAF), BF),
        in_specs=[smem, smem] + [pl.BlockSpec(memory_space=pl.ANY)] * 12,
        out_specs=vmem,
        scratch_shapes=[
            pltpu.VMEM((64 * RANK, LEAF), BF),
            pltpu.VMEM((WINDOW * RANK, LEAF), BF),
            pltpu.VMEM((WINDOW * RANK, LEAF), BF),
            pltpu.VMEM((devices // 4 * RANK, LEAF), BF),
            pltpu.VMEM((LEAVES, RANK, LEAF), F32),
            pltpu.VMEM(gathered.shape, BF),
        ]
        + [pltpu.VMEM((4 * RANK, WINDOW * RANK), BF)] * 4
        + [
            pltpu.VMEM((25, RANK, RANK), BF),
            pltpu.VMEM((TOP + 1, RANK, RANK), BF),
            pltpu.SemaphoreType.DMA((COPIES + 7,)),
        ],
        compiler_params=pltpu.CompilerParams(vmem_limit_bytes=40 << 20),
        cost_estimate=pl.CostEstimate(flops=2_500_000_000, bytes_accessed=12_000_000, transcendentals=0),
        name="far",
    )(
        near_list,
        meta,
        coefs,
        west,
        east,
        north,
        south,
        gathered,
        *[jnp.asarray(window_coupling(height)) for height in range(4)],
        jnp.asarray(code_coupling()),
        tree,
    )


def kernel_of(target_x, target_y, source_x, source_y):
    gap_x = target_x - source_x
    gap_y = target_y - source_y
    squared = jnp.maximum(gap_x * gap_x + gap_y * gap_y, 1e-12)
    length = squared * lax.rsqrt(squared)
    phase = length - ((length + rounder) - rounder)
    w = 0.25 - jnp.abs(phase)
    s = w * w
    wave = w * (SINE[0] + s * (SINE[1] + s * (SINE[2] + s * SINE[3])))
    return (jnp.exp2(squared * short_rate) + jnp.exp2(squared * long_rate) * wave).astype(BF)


def spread_columns(rows, columns):
    turned = rows.T
    for k in range(columns.shape[1] // 128):
        columns[:, 128 * k : 128 * (k + 1)] = jnp.broadcast_to(turned[:, k : k + 1], (LEAF, 128))


def block_into(to, columns, points, shift_y, shift_x):
    source_x = (points[0:1] + shift_x.astype(F32)) * waves
    source_y = (points[1:2] + shift_y.astype(F32)) * waves
    rows = 32
    for i in range(0, LEAF, rows):
        for j in (0, 128):
            to[i : i + rows, j : j + 128] = kernel_of(
                columns[i : i + rows, 0:128],
                columns[i : i + rows, 128:256],
                jnp.broadcast_to(source_x[:, j : j + 128], (rows, 128)),
                jnp.broadcast_to(source_y[:, j : j + 128], (rows, 128)),
            )


def near_own_body(first, table_ref, q_ref, pos_ref, noise_ref, *refs):
    out_ref, columns, blocks = refs[-3:]
    leaf = pl.program_id(0) + first
    rows = jnp.concatenate([pos_ref[leaf] * waves, noise_ref[leaf], jnp.zeros((5, LEAF), F32)], axis=0)
    spread_columns(rows, columns)
    width = table_ref.shape[0] // (3 * LEAVES)
    wide = 6 if first in (0, LEAVES - SIDE) else width

    def one(j, carry):
        at = (leaf * width + j) * 3
        slot = table_ref[at]

        @pl.when(slot >= 0)
        def _():
            block_into(blocks.at[j], columns, pos_ref[slot], table_ref[at + 1], table_ref[at + 2])

        @pl.when(slot < 0)
        def _():
            blocks[j] = jnp.zeros((LEAF, LEAF), BF)

        return carry

    lax.fori_loop(0, wide, one, 0)
    total = None
    for j in range(wide):
        slot = jnp.maximum(table_ref[(leaf * width + j) * 3], 0)
        part = dot(blocks[j], q_ref[slot])
        total = part if total is None else total + part
    own = q_ref[leaf].astype(F32)
    noise = jnp.concatenate([columns[:, 256:384]] * 2, axis=1)
    out_ref[0] = total + noise * own


def near_own(row, q, points, noise, before, held):
    vmem = pl.BlockSpec(memory_space=pltpu.VMEM)
    smem = pl.BlockSpec(memory_space=pltpu.SMEM)
    kept = [before] + ([] if held is None else [held])

    def body(*refs):
        near_own_body(SIDE * row, *refs)

    return pl.pallas_call(
        body,
        grid=(SIDE,),
        out_shape=jax.ShapeDtypeStruct((LEAVES, LEAF, LEAF), F32),
        in_specs=[smem, vmem, vmem, vmem] + [pl.BlockSpec(memory_space=pl.ANY)] * len(kept),
        out_specs=pl.BlockSpec((1, LEAF, LEAF), lambda i: (i + SIDE * row, 0, 0)),
        scratch_shapes=[pltpu.VMEM((LEAF, 384), F32), pltpu.VMEM((9, LEAF, LEAF), BF)],
        input_output_aliases={} if held is None else {5: 0},
        compiler_params=pltpu.CompilerParams(vmem_limit_bytes=32 << 20),
        cost_estimate=pl.CostEstimate(flops=6_000_000_000, bytes_accessed=4_000_000, transcendentals=5_000_000),
        name="near_own",
    )(jnp.asarray(near_table(True).reshape(-1)), q, points, noise, *kept)


def edge_items():
    table = near_table(False)
    items = [[leaf, *table[leaf, j]] for leaf in range(LEAVES) for j in range(5) if table[leaf, j, 0] >= 0]
    plain = [item for item in items if not is_corner(item[1])]
    return plain + [item for item in items if is_corner(item[1])]


def is_corner(slot):
    return (slot >= 32) & (slot // 8 % 2 == 1)


ITEMS = edge_items()
PLAIN = sum(not is_corner(item[1]) for item in ITEMS)
EDGES = len(ITEMS)


def extra_of(list_ref, slot_ref, leaf):
    code = second_cycle(list_ref, leaf)
    place = (leaf // SIDE + code // 5) * 8 + leaf % SIDE + code % 5
    slot = slot_ref[jnp.where(code >= 0, place, 0)]
    return code, slot


def edge_body(list_ref, table_ref, slot_ref, own_pos_ref, pos_ref, out_ref, columns):
    item = pl.program_id(0)

    def turn(leaf):
        spread_columns(jnp.concatenate([own_pos_ref[leaf] * waves, jnp.zeros((6, LEAF), F32)], axis=0), columns)

    @pl.when(item < EDGES)
    def _():
        at = item * 4
        leaf = table_ref[at]

        @pl.when((item == 0) | (table_ref[jnp.maximum(at - 4, 0)] != leaf))
        def _():
            turn(leaf)

        block_into(out_ref.at[0], columns, pos_ref[table_ref[at + 1] - LEAVES], table_ref[at + 2], table_ref[at + 3])

    @pl.when(item >= EDGES)
    def _():
        leaf = item - EDGES
        code, slot = extra_of(list_ref, slot_ref, leaf)

        @pl.when(code >= 0)
        def _():
            turn(leaf)

        @pl.when((code >= 0) & (slot >= LEAVES))
        def _():
            block_into(out_ref.at[0], columns, pos_ref[jnp.maximum(slot - LEAVES, 0)], code // 5 - 2, code % 5 - 2)

        @pl.when((code >= 0) & (slot < LEAVES))
        def _():
            block_into(out_ref.at[0], columns, own_pos_ref[jnp.minimum(slot, LEAVES - 1)], code // 5 - 2, code % 5 - 2)


def edge_blocks(near_list, own_points, halo_points, before):
    vmem = pl.BlockSpec(memory_space=pltpu.VMEM)
    smem = pl.BlockSpec(memory_space=pltpu.SMEM)

    def body(list_ref, table_ref, slot_ref, own_pos_ref, pos_ref, before_ref, out_ref, columns):
        edge_body(list_ref, table_ref, slot_ref, own_pos_ref, pos_ref, out_ref, columns)

    return pl.pallas_call(
        body,
        grid=(EDGES + LEAVES,),
        out_shape=jax.ShapeDtypeStruct((EDGES + LEAVES, LEAF, LEAF), BF),
        in_specs=[smem, smem, smem, vmem, vmem, pl.BlockSpec(memory_space=pl.ANY)],
        out_specs=pl.BlockSpec((1, LEAF, LEAF), lambda i: (i, 0, 0)),
        scratch_shapes=[pltpu.VMEM((LEAF, 256), F32)],
        compiler_params=pltpu.CompilerParams(vmem_limit_bytes=32 << 20),
        cost_estimate=pl.CostEstimate(flops=12_000_000_000, bytes_accessed=8_000_000, transcendentals=12_000_000),
        name="edge_blocks",
    )(near_list, jnp.asarray(np.array(ITEMS, np.int32).reshape(-1)), jnp.asarray(SLOT_OF), own_points, halo_points, before)


def side_body(
    list_ref, slot_ref, q_any, west_any, east_any, north_any, south_any, block_any, sum_any, basis_ref, field_ref,
    out_ref, total_ref, held, blocks, sems,
):
    copies = []
    pieces = ((q_any, 0, 16), (west_any, 16, 8), (east_any, 24, 8), (north_any, 32, 8), (south_any, 48, 8))
    for source, at, count in pieces:
        copies.append(pltpu.make_async_copy(source, held.at[pl.ds(at, count)], sems.at[len(copies)]))
    copies.append(pltpu.make_async_copy(block_any, blocks, sems.at[5]))
    copies.append(pltpu.make_async_copy(sum_any, total_ref, sems.at[6]))
    for copy in copies:
        copy.start()
    for copy in copies:
        copy.wait()
    of_leaf = {}
    for at in range(PLAIN):
        of_leaf.setdefault(ITEMS[at][0], []).append((at, ITEMS[at][1]))
    for leaf in range(LEAVES):
        total = dot_first(basis_ref[leaf], field_ref[leaf])
        for at, slot in of_leaf.get(leaf, []):
            total = total + dot(blocks[at], held[slot])
        total_ref[leaf] += total

    def extra(leaf, carry):
        code, slot = extra_of(list_ref, slot_ref, leaf)

        @pl.when((code >= 0) & jnp.logical_not(is_corner(slot)))
        def _():
            total_ref[leaf] += dot(blocks[EDGES + leaf], held[slot])

        return carry

    lax.fori_loop(0, LEAVES, extra, 0)
    back = pltpu.make_async_copy(total_ref, out_ref, sems.at[7])
    back.start()
    back.wait()


def add_sides(near_list, q, halos, blocks, near_sum, basis, field, before):
    vmem = pl.BlockSpec(memory_space=pltpu.VMEM)
    smem = pl.BlockSpec(memory_space=pltpu.SMEM)
    anywhere = pl.BlockSpec(memory_space=pl.ANY)

    def body(list_ref, slot_ref, before_ref, *refs):
        side_body(list_ref, slot_ref, *refs)

    return pl.pallas_call(
        body,
        out_shape=jax.ShapeDtypeStruct((LEAVES, LEAF, LEAF), F32),
        in_specs=[smem, smem, anywhere] + [anywhere] * 7 + [vmem, vmem],
        out_specs=anywhere,
        scratch_shapes=[
            pltpu.VMEM((LEAVES, LEAF, LEAF), F32),
            pltpu.VMEM((64, LEAF, LEAF), BF),
            pltpu.VMEM((EDGES + LEAVES, LEAF, LEAF), BF),
            pltpu.SemaphoreType.DMA((8,)),
        ],
        compiler_params=pltpu.CompilerParams(vmem_limit_bytes=48 << 20),
        cost_estimate=pl.CostEstimate(flops=4_000_000_000, bytes_accessed=24_000_000, transcendentals=0),
        name="add_sides",
    )(near_list, jnp.asarray(SLOT_OF), before, q, *halos, blocks, near_sum, basis, field)


def corner_body(list_ref, slot_ref, north_ref, south_ref, block_ref, extra_ref, sum_ref, out_ref, total):
    leaf = pl.program_id(0)
    total[...] = sum_ref[0]
    for at in range(PLAIN, EDGES):

        @pl.when(leaf == ITEMS[at][0])
        def _(at=at):
            slot = ITEMS[at][1]
            ref, start = (north_ref, 40) if slot < 48 else (south_ref, 56)
            total[...] += dot(block_ref[at - PLAIN], ref[slot - start])

    code, slot = extra_of(list_ref, slot_ref, leaf)

    @pl.when((code >= 0) & is_corner(slot))
    def _():
        source = jnp.where(slot < 48, north_ref[slot % 8], south_ref[slot % 8])
        total[...] += dot(extra_ref[0], source)

    out_ref[0] = total[...].astype(BF)


def add_corners(near_list, north, south, blocks, total):
    vmem = pl.BlockSpec(memory_space=pltpu.VMEM)
    smem = pl.BlockSpec(memory_space=pltpu.SMEM)
    block = pl.BlockSpec((1, LEAF, LEAF), lambda i: (i, 0, 0))
    corners = EDGES - PLAIN
    return pl.pallas_call(
        corner_body,
        grid=(LEAVES,),
        out_shape=jax.ShapeDtypeStruct((LEAVES, LEAF, LEAF), BF),
        in_specs=[
            smem,
            smem,
            vmem,
            vmem,
            pl.BlockSpec((corners, LEAF, LEAF), lambda i: (PLAIN // corners, 0, 0)),
            pl.BlockSpec((1, LEAF, LEAF), lambda i: (EDGES + i, 0, 0)),
            block,
        ],
        out_specs=block,
        scratch_shapes=[pltpu.VMEM((LEAF, LEAF), F32)],
        compiler_params=pltpu.CompilerParams(vmem_limit_bytes=32 << 20),
        cost_estimate=pl.CostEstimate(flops=500_000_000, bytes_accessed=10_000_000, transcendentals=0),
        name="add_corners",
    )(near_list, jnp.asarray(SLOT_OF), north, south, blocks, blocks, total)


def points_of(message, leaves_at):
    parts = message[leaves_at : leaves_at + 48].astype(F32)
    whole = (parts[0:16] + parts[16:32]) + parts[32:48]
    return whole.reshape(8, 2, LEAF)


def window_slots(wide, narrow, steps):
    row, col = lax.axis_index("narrow"), lax.axis_index("wide")
    wy, wx = np.arange(WINDOW) // 6, np.arange(WINDOW) % 6

    def slots(target_y, target_x, scale):
        y = target_y // 2 * 2 - 2 + wy
        x = target_x // 2 * 2 - 2 + wx
        inside = (y >= 0) & (y < narrow // scale) & (x >= 0) & (x < wide // scale)
        apart = {"narrow": (y * scale) ^ row, "wide": (x * scale) ^ col}
        slot = 0
        for at, (axis, bit) in enumerate(steps):
            slot = slot + (apart[axis] // bit & 1) * (1 << at)
        return jnp.where(inside, slot if scale == 1 else slot // 4, -1)

    parity2 = row % 2 * 2 + col % 2
    parity3 = row // 2 % 2 * 2 + col // 2 % 2
    return jnp.concatenate(
        [slots(row, col, 1), slots(row // 2, col // 2, 2), jnp.stack([parity2, parity3])]
    ).astype(jnp.int32)


def per_device(wide, narrow, charges, positions, noise, leaf_basis, transfer, near_list):
    q = charges.reshape(LEAVES, LEAF, LEAF)
    points = positions.reshape(LEAVES, 2, LEAF)
    basis = leaf_basis.reshape(LEAVES, RANK, LEAF)
    tree = transfer[0, 0]
    listing = near_list.reshape(-1)
    steps = gather_steps(wide, narrow)
    meta = window_slots(wide, narrow, steps)

    east, west, north, south, coefs, give = go_up(q, basis, tree, points)
    from_west = shift(east, "wide", 1)
    from_east = shift(west, "wide", -1)
    q_west = shift(charges[:, 2:4], "wide", 1)
    q_east = shift(charges[:, 0:2], "wide", -1)
    q_north = shift(charges[2:4], "narrow", 1)
    q_south = shift(charges[0:2], "narrow", -1)

    noise_rows = noise.reshape(LEAVES, 1, LEAF)
    near_sum = None
    gathered, before = give, give
    for at, (axis, bit) in enumerate(steps):
        other = lax.ppermute(gathered, axis, [(i, i ^ bit) for i in range(lax.axis_size(axis))])
        if at < SIDE:
            near_sum = near_own(at, q, points, noise_rows, before, near_sum)
            other, near_sum = lax.optimization_barrier((other, near_sum))
        if at == 1:
            from_west, from_east, near_sum = lax.optimization_barrier((from_west, from_east, near_sum))
        if at == 2:
            north, south, from_south, from_north = narrow_messages(north, south, from_west, from_east)
        before = other
        gathered = jnp.concatenate([gathered, other], axis=0)

    def corner_points(message, lower):
        first = points_of(message, SIDEWAYS + 8 * RANK)
        second = points_of(message, SIDEWAYS + CORNER + 8 * RANK)
        at = 4 if lower else 0
        return [first[at : at + 4], second[at : at + 4]]

    halo_points = jnp.concatenate(
        [points_of(from_west, 12 * RANK), points_of(from_east, 12 * RANK), points_of(from_north, 12 * RANK)]
        + corner_points(from_north, True)
        + [points_of(from_south, 12 * RANK)]
        + corner_points(from_south, False),
        axis=0,
    )
    blocks = edge_blocks(listing, points, halo_points, near_sum)
    gathered, blocks = lax.optimization_barrier((gathered, blocks))
    field = far_field(listing, meta, coefs, from_west, from_east, from_north, from_south, gathered, tree)
    q_west, q_east, field = lax.optimization_barrier((q_west, q_east, field))
    q_north_corner = shift(jnp.stack([q_west[2:4], q_east[2:4]]), "narrow", 1)
    q_south_corner = shift(jnp.stack([q_west[0:2], q_east[0:2]]), "narrow", -1)
    halos = [value.reshape(8, LEAF, LEAF) for value in (q_west, q_east, q_north, q_south)]
    total = add_sides(listing, q, halos, blocks, near_sum, basis, field, q_west)
    q_north_corner, q_south_corner, total = lax.optimization_barrier((q_north_corner, q_south_corner, total))
    out = add_corners(
        listing, q_north_corner.reshape(8, LEAF, LEAF), q_south_corner.reshape(8, LEAF, LEAF), blocks, total
    )
    return out.reshape(SIDE, SIDE, LEAF, LEAF)


def narrow_messages(north, south, from_west, from_east):
    def corner(message, lower):
        at = 4 * RANK if lower else 0
        return [message[at : at + 4 * RANK], message[8 * RANK :]]

    north = jnp.concatenate([north] + corner(from_west, False) + corner(from_east, False), axis=0)
    south = jnp.concatenate([south] + corner(from_west, True) + corner(from_east, True), axis=0)
    return north, south, shift(north, "narrow", -1), shift(south, "narrow", 1)


def solution(mesh):
    wide, narrow = mesh.shape["wide"], mesh.shape["narrow"]
    in_specs = (
        P("narrow", "wide", None, None),
        P("narrow", "wide", None, None),
        P("narrow", "wide", None),
        P("narrow", "wide", None, None),
        P("narrow", "wide", None, None, None),
        P("narrow", "wide", None),
    )
    out_specs = P("narrow", "wide", None, None)

    def step(*arrays):
        return per_device(wide, narrow, *arrays)

    return jax.shard_map(step, mesh=mesh, in_specs=in_specs, out_specs=out_specs, check_vma=False)
```

```python
import math

import jax
import jax.numpy as jnp
import ml_dtypes
import numpy as np
from jax import lax
from jax.experimental import pallas as pl
from jax.experimental.pallas import tpu as pltpu
from jax.sharding import PartitionSpec as P

LEAF = 256
CHEB = 8
RANK = 64
NEAR = 10
SIDE = 4
LEAVES = SIDE * SIDE
TOP = 20
WINDOW = 36
PACK = RANK + 16
SIDEWAYS = 8 * RANK + 4 * RANK + 48
CORNER = 4 * RANK + 4 * RANK + 48
COPIES = 42
BF = jnp.bfloat16
F32 = jnp.float32

short_len = 0.125
long_weight = 0.03125
reach = 3.0 * SIDE
waves = 10.0
LOG2E = math.log2(math.e)
long_rate = -0.5 / (reach * reach) * LOG2E / (waves * waves)
short_rate = -0.5 / (short_len * short_len) * LOG2E / (waves * waves)
rounder = 1.5 * 2.0**23


def sine_terms(count):
    w = np.cos(np.pi * (np.arange(2000) + 0.5) / 2000) * 0.25
    powers = np.stack([w ** (2 * i + 1) for i in range(count)], 1)
    return [float(c) for c in np.linalg.lstsq(powers, np.sin(2 * np.pi * w) * long_weight, rcond=None)[0]]


SINE = sine_terms(4)


def coupling(height, shift_y, shift_x):
    points = 0.5 * (1.0 + np.cos((2.0 * np.arange(CHEB) + 1.0) * (math.pi / (2.0 * CHEB))))
    node_x = np.tile(points, CHEB)
    node_y = np.repeat(points, CHEB)
    gap_x = (node_x[:, None] - node_x[None, :] - shift_x) * 2.0**height
    gap_y = (node_y[:, None] - node_y[None, :] - shift_y) * 2.0**height
    squared = gap_x * gap_x + gap_y * gap_y
    return np.exp(squared * (-0.5 / (short_len * short_len))) + long_weight * np.exp(
        squared * (-0.5 / (reach * reach))
    ) * np.cos(2.0 * math.pi * waves * np.sqrt(squared))


def window_coupling(height):
    table = np.zeros((2, 2, RANK, 6, 6, RANK))
    for py in range(2):
        for px in range(2):
            for wy in range(6):
                for wx in range(6):
                    shift_y, shift_x = wy - 2 - py, wx - 2 - px
                    if max(abs(shift_y), abs(shift_x)) >= 2:
                        table[py, px, :, wy, wx] = coupling(height, shift_y, shift_x)
    return table.reshape(4 * RANK, WINDOW * RANK).astype(ml_dtypes.bfloat16)


def code_coupling():
    return np.stack([coupling(0, code // 5 - 2, code % 5 - 2) for code in range(25)]).astype(ml_dtypes.bfloat16)


def halo_slot(row, col):
    if 0 <= row < 4 and 0 <= col < 4:
        return row * 4 + col
    if 0 <= row < 4:
        return 16 + row * 2 + col + 2 if col < 0 else 24 + row * 2 + col - 4
    base, r = (32, row + 2) if row < 0 else (48, row - 4)
    if 0 <= col < 4:
        return base + r * 4 + col
    return base + 8 + r * 2 + col + 2 if col < 0 else base + 12 + r * 2 + col - 4


SLOT_OF = np.array([halo_slot(r - 2, c - 2) for r in range(8) for c in range(8)], np.int32)


def near_table(own):
    width = 9 if own else 5
    table = np.zeros((LEAVES, width, 3), np.int32)
    table[:, :, 0] = -1
    for r in range(SIDE):
        for c in range(SIDE):
            at = 0
            for dy in (-1, 0, 1):
                for dx in (-1, 0, 1):
                    slot = halo_slot(r + dy, c + dx)
                    if (slot < LEAVES) == own:
                        table[r * SIDE + c, at] = (slot, dy, dx)
                        at += 1
    return table


def bits(count):
    return [1 << i for i in range(count.bit_length() - 1)]


def gather_steps(wide, narrow):
    return (
        [("wide", 1), ("narrow", 1)]
        + [("wide", b) for b in reversed(bits(wide)[1:])]
        + [("narrow", b) for b in reversed(bits(narrow)[1:])]
    )


def shift(value, axis, steps):
    count = lax.axis_size(axis)
    return lax.ppermute(value, axis, [(i, i + steps) for i in range(count) if 0 <= i + steps < count])


def dot(a, b):
    return jnp.dot(a, b, preferred_element_type=F32)


def dot_first(a, b):
    return lax.dot_general(a, b, (((0,), (0,)), ((), ())), preferred_element_type=F32)


def up_body(q_ref, basis_ref, tree_ref, pos_ref, east_ref, west_ref, north_ref, south_ref, coef_ref, give_ref):
    level0 = []
    for leaf in range(LEAVES):
        coef = dot(basis_ref[leaf], q_ref[leaf]).astype(BF)
        level0.append(coef)
        r, c = leaf // SIDE, leaf % SIDE
        coef_ref[leaf * RANK : (leaf + 1) * RANK] = coef
        ref, at = (west_ref, r * 2 + c) if c < 2 else (east_ref, r * 2 + c - 2)
        ref[at * RANK : (at + 1) * RANK] = coef
        ref, at = (north_ref, r * 4 + c) if r < 2 else (south_ref, r * 4 + c - 8)
        ref[at * RANK : (at + 1) * RANK] = coef
    level1 = []
    for r in range(2):
        for c in range(2):
            total = None
            for dr in range(2):
                for dc in range(2):
                    leaf = (2 * r + dr) * SIDE + 2 * c + dc
                    part = dot(tree_ref[leaf], level0[leaf])
                    total = part if total is None else total + part
            coef = total.astype(BF)
            at = r * 2 + c
            level1.append(coef)
            coef_ref[(LEAVES + at) * RANK : (LEAVES + at + 1) * RANK] = coef
            for ref in (east_ref, west_ref, north_ref, south_ref):
                ref[(8 + at) * RANK : (9 + at) * RANK] = coef
    total = None
    for at in range(4):
        part = dot(tree_ref[LEAVES + at], level1[at])
        total = part if total is None else total + part
    give_ref[0:RANK] = total.astype(BF)
    top = tree_ref[TOP]
    give_ref[RANK:PACK] = jnp.concatenate([top[16 * k : 16 * k + 16] for k in range(4)], axis=1)
    for ref, leaves in (
        (west_ref, [r * 4 + c for r in range(4) for c in (0, 1)]),
        (east_ref, [r * 4 + c for r in range(4) for c in (2, 3)]),
        (north_ref, range(8)),
        (south_ref, range(8, 16)),
    ):
        rest = jnp.concatenate([pos_ref[leaf] for leaf in leaves], axis=0)
        for part in range(3):
            held = rest.astype(BF)
            at = 12 * RANK + 16 * part
            ref[at : at + 16] = held
            rest = rest - held.astype(F32)


def go_up(q, basis, tree, points):
    vmem = pl.BlockSpec(memory_space=pltpu.VMEM)
    side = jax.ShapeDtypeStruct((SIDEWAYS, LEAF), BF)
    return pl.pallas_call(
        up_body,
        out_shape=(
            side,
            side,
            side,
            side,
            jax.ShapeDtypeStruct(((LEAVES + 4) * RANK, LEAF), BF),
            jax.ShapeDtypeStruct((PACK, LEAF), BF),
        ),
        in_specs=[vmem] * 4,
        out_specs=[vmem] * 6,
        compiler_params=pltpu.CompilerParams(vmem_limit_bytes=32 << 20),
        cost_estimate=pl.CostEstimate(flops=300_000_000, bytes_accessed=5_000_000, transcendentals=0),
        name="upward",
    )(q, basis, tree, points)


def local_body(
    list_ref, coef_any, west_any, east_any, north_any, south_any, c0_any, c1_any, code_any, sum0, sum1, pad0, pad1, c0_ref, c1_ref, code_ref, sems
):
    loads = []

    def load(source, at, to, row, count):
        rows = pl.ds(at * RANK if at < 100 else at, count * RANK)
        copy = pltpu.make_async_copy(source.at[rows], to.at[pl.ds(row, count * RANK)], sems.at[len(loads)])
        copy.start()
        loads.append(copy)

    def put(pad, extent, row, col, ref, at, count):
        load(ref, at, pad, ((row + 2) * (extent + 4) + col + 2) * RANK, count)

    whole = []
    for k, (source, to) in enumerate(((c0_any, c0_ref), (c1_any, c1_ref), (code_any, code_ref))):
        whole.append(pltpu.make_async_copy(source, to, sems.at[COPIES + k]))
    whole[0].start()
    for r in range(4):
        put(pad0, 4, r, 0, coef_any, r * 4, 4)
        put(pad0, 4, r, -2, west_any, r * 2, 2)
        put(pad0, 4, r, 4, east_any, r * 2, 2)
    for ref, row in ((north_any, -2), (south_any, 4)):
        for r in range(2):
            put(pad0, 4, row + r, 0, ref, r * 4, 4)
            for col, base in ((-2, SIDEWAYS), (4, SIDEWAYS + CORNER)):
                load(ref, base + r * 2 * RANK, pad0, ((row + r + 2) * 8 + col + 2) * RANK, 2)
    split = len(loads)
    for copy in whole[1:]:
        copy.start()
    for r in range(2):
        put(pad1, 2, r, 0, coef_any, LEAVES + r * 2, 2)
        put(pad1, 2, r, -2, west_any, 8 + r * 2, 2)
        put(pad1, 2, r, 2, east_any, 8 + r * 2, 2)
    for ref, row in ((north_any, -2), (south_any, 2)):
        for r in range(2):
            put(pad1, 2, row + r, 0, ref, 8 + r * 2, 2)
            for col, base in ((-2, SIDEWAYS), (2, SIDEWAYS + CORNER)):
                load(ref, base + (4 + r * 2) * RANK, pad1, ((row + r + 2) * 6 + col + 2) * RANK, 2)
    whole[0].wait()
    for copy in loads[:split]:
        copy.wait()
    for a in range(2):
        for b in range(2):
            total = None
            for wy in range(6):
                at = ((2 * a + wy) * 8 + 2 * b) * RANK
                part = dot(c0_ref[:, wy * 6 * RANK : (wy + 1) * 6 * RANK], pad0[at : at + 6 * RANK])
                total = part if total is None else total + part
            for child in range(4):
                leaf = (2 * a + child // 2) * SIDE + 2 * b + child % 2
                sum0[leaf] = total[child * RANK : (child + 1) * RANK]
    for copy in loads[split:] + whole[1:]:
        copy.wait()

    def listed(leaf, carry):
        code = second_cycle(list_ref, leaf)

        @pl.when(code >= 0)
        def _():
            row = leaf // SIDE + code // 5
            col = leaf % SIDE + code % 5
            at = pl.multiple_of((row * 8 + col) * RANK, RANK)
            sum0[leaf] = sum0[leaf] - dot(code_ref[code], pad0[pl.ds(at, RANK)])

        return carry

    lax.fori_loop(0, LEAVES, listed, 0)
    sum1[...] = dot(c1_ref[...], pad1[...])


def local_far(near_list, coefs, west, east, north, south):
    vmem = pl.BlockSpec(memory_space=pltpu.VMEM)
    smem = pl.BlockSpec(memory_space=pltpu.SMEM)
    return pl.pallas_call(
        local_body,
        out_shape=(
            jax.ShapeDtypeStruct((LEAVES, RANK, LEAF), F32),
            jax.ShapeDtypeStruct((4 * RANK, LEAF), F32),
        ),
        in_specs=[smem] + [pl.BlockSpec(memory_space=pl.ANY)] * 8,
        out_specs=[vmem] * 2,
        scratch_shapes=[
            pltpu.VMEM((64 * RANK, LEAF), BF),
            pltpu.VMEM((WINDOW * RANK, LEAF), BF),
            pltpu.VMEM((4 * RANK, WINDOW * RANK), BF),
            pltpu.VMEM((4 * RANK, WINDOW * RANK), BF),
            pltpu.VMEM((25, RANK, RANK), BF),
            pltpu.SemaphoreType.DMA((COPIES + 3,)),
        ],
        compiler_params=pltpu.CompilerParams(vmem_limit_bytes=32 << 20),
        cost_estimate=pl.CostEstimate(flops=5_000_000_000, bytes_accessed=8_000_000, transcendentals=0),
        name="local_far",
    )(
        near_list,
        coefs,
        west,
        east,
        north,
        south,
        jnp.asarray(window_coupling(0)),
        jnp.asarray(window_coupling(1)),
        jnp.asarray(code_coupling()),
    )


def top_body(meta_ref, all_ref, c2_any, c3_any, tree_ref, sum0, sum1, field_ref, win, parents, c2_ref, c3_ref, sems):
    def slab(source, to, at):
        part = pl.ds(pl.multiple_of(meta_ref[2 * WINDOW + at] * RANK, RANK), RANK)
        copy = pltpu.make_async_copy(source.at[part], to, sems.at[at])
        copy.start()
        return copy

    slabs = [slab(c2_any, c2_ref, 0), slab(c3_any, c3_ref, 1)]

    def lift(group, carry):
        total = jnp.zeros((RANK, LEAF), F32)
        for child in range(4):
            at = pl.multiple_of((group * 4 + child) * PACK, 16)
            packed = all_ref[pl.ds(at + RANK, 16)]
            matrix = jnp.concatenate([packed[:, k * RANK : (k + 1) * RANK] for k in range(4)], axis=0)
            total = total + dot(matrix, all_ref[pl.ds(at, RANK)])
        parents[pl.ds(pl.multiple_of(group * RANK, RANK), RANK)] = total.astype(BF)
        return carry

    lax.fori_loop(0, parents.shape[0] // RANK, lift, 0)

    def fill(start, source, stride):
        def one(i, carry):
            slot = meta_ref[start + i]
            to = pl.ds(pl.multiple_of(i * RANK, RANK), RANK)

            @pl.when(slot >= 0)
            def _():
                win[to] = source[pl.ds(pl.multiple_of(slot * stride, 16), RANK)]

            @pl.when(slot < 0)
            def _():
                win[to] = jnp.zeros((RANK, LEAF), BF)

            return carry

        lax.fori_loop(0, WINDOW, one, 0)

    fill(WINDOW, parents, RANK)
    slabs[1].wait()
    field3 = dot(c3_ref[...], win[...]).astype(BF)
    fill(0, all_ref, PACK)
    slabs[0].wait()
    field2 = (dot(c2_ref[...], win[...]) + dot_first(tree_ref[TOP], field3)).astype(BF)
    field1 = []
    for at in range(4):
        field1.append(
            (sum1[at * RANK : (at + 1) * RANK] + dot_first(tree_ref[LEAVES + at], field2)).astype(BF)
        )
    for leaf in range(LEAVES):
        above = field1[leaf // SIDE // 2 * 2 + leaf % SIDE // 2]
        field_ref[leaf] = (sum0[leaf] + dot_first(tree_ref[leaf], above)).astype(BF)


def second_cycle(list_ref, leaf):
    found = jnp.int32(-1)
    for j in range(NEAR):
        code = list_ref[leaf * NEAR + j]
        y, x = code // 5, code % 5
        outer = (code >= 0) & ((y == 0) | (y == 4) | (x == 0) | (x == 4))
        found = jnp.where(outer, code, found)
    return found


def top_far(meta, gathered, tree, sum0, sum1):
    vmem = pl.BlockSpec(memory_space=pltpu.VMEM)
    smem = pl.BlockSpec(memory_space=pltpu.SMEM)
    anywhere = pl.BlockSpec(memory_space=pl.ANY)
    devices = gathered.shape[0] // PACK
    return pl.pallas_call(
        top_body,
        out_shape=jax.ShapeDtypeStruct((LEAVES, RANK, LEAF), BF),
        in_specs=[smem, vmem, anywhere, anywhere, vmem, vmem, vmem],
        out_specs=vmem,
        scratch_shapes=[
            pltpu.VMEM((WINDOW * RANK, LEAF), BF),
            pltpu.VMEM((devices // 4 * RANK, LEAF), BF),
            pltpu.VMEM((RANK, WINDOW * RANK), BF),
            pltpu.VMEM((RANK, WINDOW * RANK), BF),
            pltpu.SemaphoreType.DMA((2,)),
        ],
        compiler_params=pltpu.CompilerParams(vmem_limit_bytes=32 << 20),
        cost_estimate=pl.CostEstimate(flops=3_000_000_000, bytes_accessed=5_000_000, transcendentals=0),
        name="top_far",
    )(meta, gathered, jnp.asarray(window_coupling(2)), jnp.asarray(window_coupling(3)), tree, sum0, sum1)


def join_body(north_ref, south_ref, west_ref, east_ref, to_north, to_south, sems):
    copies = []

    def move(source, at, to, row, count):
        copy = pltpu.make_async_copy(source.at[pl.ds(at, count)], to.at[pl.ds(row, count)], sems.at[len(copies)])
        copy.start()
        copies.append(copy)

    for own, to, lower in ((north_ref, to_north, 0), (south_ref, to_south, 1)):
        move(own, 0, to, 0, SIDEWAYS)
        for side, base in ((west_ref, SIDEWAYS), (east_ref, SIDEWAYS + CORNER)):
            move(side, 4 * RANK * lower, to, base, 4 * RANK)
            move(side, 8 * RANK, to, base + 4 * RANK, CORNER - 4 * RANK)
    for copy in copies:
        copy.wait()


def join(north, south, west, east):
    anywhere = pl.BlockSpec(memory_space=pl.ANY)
    message = jax.ShapeDtypeStruct((SIDEWAYS + 2 * CORNER, LEAF), BF)
    return pl.pallas_call(
        join_body,
        out_shape=(message, message),
        in_specs=[anywhere] * 4,
        out_specs=[anywhere] * 2,
        scratch_shapes=[pltpu.SemaphoreType.DMA((10,))],
        cost_estimate=pl.CostEstimate(flops=0, bytes_accessed=4_000_000, transcendentals=0),
        name="join",
    )(north, south, west, east)


def kernel_of(target_x, target_y, source_x, source_y):
    gap_x = target_x - source_x
    gap_y = target_y - source_y
    squared = jnp.maximum(gap_x * gap_x + gap_y * gap_y, 1e-12)
    length = squared * lax.rsqrt(squared)
    phase = length - ((length + rounder) - rounder)
    w = 0.25 - jnp.abs(phase)
    s = w * w
    wave = w * (SINE[0] + s * (SINE[1] + s * (SINE[2] + s * SINE[3])))
    return (jnp.exp2(squared * short_rate) + jnp.exp2(squared * long_rate) * wave).astype(BF)


def spread_columns(rows, columns):
    turned = rows.T
    for k in range(columns.shape[1] // 128):
        columns[:, 128 * k : 128 * (k + 1)] = jnp.broadcast_to(turned[:, k : k + 1], (LEAF, 128))


def block_into(to, columns, points, shift_y, shift_x):
    source_x = (points[0:1] + shift_x.astype(F32)) * waves
    source_y = (points[1:2] + shift_y.astype(F32)) * waves
    rows = 32
    for i in range(0, LEAF, rows):
        for j in (0, 128):
            to[i : i + rows, j : j + 128] = kernel_of(
                columns[i : i + rows, 0:128],
                columns[i : i + rows, 128:256],
                jnp.broadcast_to(source_x[:, j : j + 128], (rows, 128)),
                jnp.broadcast_to(source_y[:, j : j + 128], (rows, 128)),
            )


def turn_points(columns, leaf, position, noise):
    rows = jnp.concatenate([position * waves, noise, jnp.zeros((5, LEAF), F32)], axis=0)
    spread_columns(rows, columns.at[leaf])


def own_pairs(first):
    pairs = []
    for r in (first, first + 1):
        for c in range(SIDE):
            for dy, dx in ((0, 1), (1, -1), (1, 0), (1, 1)):
                if r + dy < SIDE and 0 <= c + dx < SIDE:
                    pairs.append((r * SIDE + c, (r + dy) * SIDE + c + dx, dy, dx))
    return pairs


def near_own_body(first, table_ref, q_ref, pos_ref, noise_ref, *refs):
    before_ref, out_ref, columns, blocks = (None,) * (4 - len(refs)) + refs
    pairs = own_pairs(first)
    start = first * SIDE

    def turn(leaf, carry):
        turn_points(columns, leaf, pos_ref[leaf], noise_ref[leaf])
        return carry

    lax.fori_loop(start, start + 8, turn, 0)
    zero = jnp.int32(0)

    def selves(i, carry):
        for half in range(2):
            leaf = start + 2 * i + half
            block_into(blocks.at[2 * i + half], columns.at[leaf], pos_ref[leaf], zero, zero)
        return carry

    lax.fori_loop(0, 4, selves, 0)

    def both(i, carry):
        for half in range(2):
            at = 8 * i + 4 * half
            place = 8 + 4 * i + 2 * half
            target, source = table_ref[at], table_ref[at + 1]
            block_into(
                blocks.at[place], columns.at[target], pos_ref[source], table_ref[at + 2], table_ref[at + 3]
            )
            blocks[place + 1] = blocks[place].T
        return carry

    lax.fori_loop(0, len(pairs) // 2, both, 0)
    parts = {leaf: [(leaf - start, leaf)] for leaf in range(start, start + 8)}
    for i, (target, source, _, _) in enumerate(pairs):
        parts[target].append((8 + 2 * i, source))
        parts.setdefault(source, []).append((9 + 2 * i, target))
    for leaf, terms in sorted(parts.items()):
        total = None
        for place, source in terms:
            part = dot(blocks[place], q_ref[source])
            total = part if total is None else total + part
        if leaf < start + 8:
            noise = jnp.concatenate([columns[leaf, :, 256:384]] * 2, axis=1)
            total = total + noise * q_ref[leaf].astype(F32)
        if before_ref is not None and leaf < start + SIDE:
            total = total + before_ref[leaf]
        out_ref[leaf - start] = total


def near_own(first, q, points, noise, after, before):
    vmem = pl.BlockSpec(memory_space=pltpu.VMEM)
    smem = pl.BlockSpec(memory_space=pltpu.SMEM)
    anywhere = pl.BlockSpec(memory_space=pl.ANY)
    pairs = own_pairs(first)

    def body(after_ref, *refs):
        near_own_body(first, *refs)

    return pl.pallas_call(
        body,
        out_shape=jax.ShapeDtypeStruct((12 if first == 0 else 8, LEAF, LEAF), F32),
        in_specs=[anywhere, smem, vmem, vmem, vmem] + [vmem] * len(before),
        out_specs=vmem,
        scratch_shapes=[
            pltpu.VMEM((LEAVES, LEAF, 384), F32),
            pltpu.VMEM((8 + 2 * len(pairs), LEAF, LEAF), BF),
        ],
        compiler_params=pltpu.CompilerParams(vmem_limit_bytes=40 << 20),
        cost_estimate=pl.CostEstimate(flops=10_000_000_000, bytes_accessed=4_000_000, transcendentals=8_000_000),
        name="near_own",
    )(after, jnp.asarray(np.array(pairs, np.int32).reshape(-1)), q, points, noise, *before)


def edge_items():
    table = near_table(False)
    return [[leaf, *table[leaf, j]] for leaf in range(LEAVES) for j in range(5) if table[leaf, j, 0] >= 0]


ITEMS = edge_items()
EDGES = len(ITEMS)


def extra_of(list_ref, slot_ref, leaf):
    code = second_cycle(list_ref, leaf)
    place = (leaf // SIDE + code // 5) * 8 + leaf % SIDE + code % 5
    slot = slot_ref[jnp.where(code >= 0, place, 0)]
    return code, slot


def edge_body(
    list_ref, table_ref, slot_ref, after_ref, own_pos_ref, west_any, east_any, north_any, south_any, out_ref,
    columns, parts, points, sems,
):
    copies = []
    sources = (
        (west_any, 12 * RANK),
        (east_any, 12 * RANK),
        (north_any, 12 * RANK),
        (north_any, SIDEWAYS + 8 * RANK),
        (north_any, SIDEWAYS + CORNER + 8 * RANK),
        (south_any, 12 * RANK),
        (south_any, SIDEWAYS + 8 * RANK),
        (south_any, SIDEWAYS + CORNER + 8 * RANK),
    )
    for k, (source, at) in enumerate(sources):
        copies.append(pltpu.make_async_copy(source.at[pl.ds(at, 48)], parts.at[k], sems.at[k]))
    for copy in copies:
        copy.start()

    def turn(leaf, carry):
        turn_points(columns, leaf, own_pos_ref[leaf], jnp.zeros((1, LEAF), F32))
        points[leaf] = own_pos_ref[leaf]
        return carry

    lax.fori_loop(0, LEAVES, turn, 0)
    for copy in copies:
        copy.wait()
    slots = (16, 24, 32, 40, 44, 48, 56, 60)
    for k in range(8):
        whole = parts[k].astype(F32)
        whole = (whole[0:16] + whole[16:32]) + whole[32:48]
        first, count = {3: (4, 4), 4: (4, 4), 6: (0, 4), 7: (0, 4)}.get(k, (0, 8))
        for i in range(count):
            points[slots[k] + i] = whole[2 * (first + i) : 2 * (first + i) + 2]

    def fixed(i, carry):
        for half in range(2):
            at = 8 * i + 4 * half
            block_into(
                out_ref.at[2 * i + half],
                columns.at[table_ref[at]],
                points[table_ref[at + 1]],
                table_ref[at + 2],
                table_ref[at + 3],
            )
        return carry

    lax.fori_loop(0, EDGES // 2, fixed, 0)

    def extra(i, carry):
        for half in range(2):
            leaf = 2 * i + half
            code, slot = extra_of(list_ref, slot_ref, leaf)
            code = jnp.maximum(code, 0)
            block_into(out_ref.at[EDGES + leaf], columns.at[leaf], points[slot], code // 5 - 2, code % 5 - 2)
        return carry

    lax.fori_loop(0, LEAVES // 2, extra, 0)


def edge_blocks(near_list, after, own_points, west, east, north, south):
    vmem = pl.BlockSpec(memory_space=pltpu.VMEM)
    smem = pl.BlockSpec(memory_space=pltpu.SMEM)
    anywhere = pl.BlockSpec(memory_space=pl.ANY)
    return pl.pallas_call(
        edge_body,
        out_shape=jax.ShapeDtypeStruct((EDGES + LEAVES, LEAF, LEAF), BF),
        in_specs=[smem, smem, smem, anywhere, vmem] + [anywhere] * 4,
        out_specs=vmem,
        scratch_shapes=[
            pltpu.VMEM((LEAVES, LEAF, 384), F32),
            pltpu.VMEM((8, 48, LEAF), BF),
            pltpu.VMEM((64, 2, LEAF), F32),
            pltpu.SemaphoreType.DMA((8,)),
        ],
        compiler_params=pltpu.CompilerParams(vmem_limit_bytes=40 << 20),
        cost_estimate=pl.CostEstimate(flops=12_000_000_000, bytes_accessed=8_000_000, transcendentals=12_000_000),
        name="edge_blocks",
    )(
        near_list, jnp.asarray(np.array(ITEMS, np.int32).reshape(-1)), jnp.asarray(SLOT_OF), after, own_points,
        west, east, north, south,
    )


def final_body(
    list_ref, slot_ref, q_any, west_any, east_any, north_any, north_corner_any, south_any, south_corner_any,
    block_any, upper_any, lower_any, basis_ref, field_ref, out_any, held, blocks, sums, extra_sum, outs, sems,
):
    firsts = [min(at for at in range(EDGES) if ITEMS[at][0] // SIDE == r) for r in range(SIDE)] + [EDGES]
    stages = [[], [], [], []]
    count = 0

    def copy(stage, source, to):
        nonlocal count
        made = pltpu.make_async_copy(source, to, sems.at[count])
        count += 1
        stages[stage].append(made)
        made.start()

    for r in range(SIDE):
        if r == 0:
            for source, at in ((north_any, 32), (north_corner_any, 40), (west_any, 16), (east_any, 24)):
                copy(r, source, held.at[pl.ds(at, 8)])
        if r == SIDE - 1:
            for source, at in ((south_any, 48), (south_corner_any, 56)):
                copy(r, source, held.at[pl.ds(at, 8)])
        part = pl.ds(firsts[r], firsts[r + 1] - firsts[r])
        copy(r, block_any.at[part], blocks.at[part])
        source = upper_any.at[pl.ds(SIDE * r, SIDE)] if r < 2 else lower_any.at[pl.ds(SIDE * (r - 2), SIDE)]
        copy(r, source, sums.at[pl.ds(SIDE * r, SIDE)])
    copy(SIDE - 1, q_any, held.at[pl.ds(0, 16)])
    part = pl.ds(EDGES, LEAVES)
    copy(SIDE - 1, block_any.at[part], blocks.at[part])
    for leaf in range(LEAVES):
        if leaf % SIDE == 0:
            for made in stages[leaf // SIDE]:
                made.wait()
        total = dot_first(basis_ref[leaf], field_ref[leaf])
        for at in range(EDGES):
            if ITEMS[at][0] == leaf:
                total = total + dot(blocks[at], held[ITEMS[at][1]])
        sums[leaf] += total

    backs = []
    for r in range(SIDE):
        part = pl.ds(SIDE * r, SIDE)
        backs.append(pltpu.make_async_copy(outs.at[part], out_any.at[part], sems.at[count + r]))

    for r in range(SIDE):

        def finish(leaf, carry):
            code, slot = extra_of(list_ref, slot_ref, leaf)

            @pl.when(code >= 0)
            def _():
                outs[leaf] = (sums[leaf] + dot(blocks[EDGES + leaf], held[slot])).astype(BF)

            @pl.when(code < 0)
            def _():
                outs[leaf] = sums[leaf].astype(BF)

            return carry

        lax.fori_loop(SIDE * r, SIDE * (r + 1), finish, 0)
        backs[r].start()
    for back in backs:
        back.wait()


def finish(near_list, q, halos, blocks, upper, lower, basis, field):
    vmem = pl.BlockSpec(memory_space=pltpu.VMEM)
    smem = pl.BlockSpec(memory_space=pltpu.SMEM)
    anywhere = pl.BlockSpec(memory_space=pl.ANY)

    return pl.pallas_call(
        final_body,
        out_shape=jax.ShapeDtypeStruct((LEAVES, LEAF, LEAF), BF),
        in_specs=[smem, smem] + [anywhere] * 10 + [vmem, vmem],
        out_specs=anywhere,
        scratch_shapes=[
            pltpu.VMEM((64, LEAF, LEAF), BF),
            pltpu.VMEM((EDGES + LEAVES, LEAF, LEAF), BF),
            pltpu.VMEM((LEAVES, LEAF, LEAF), F32),
            pltpu.VMEM((LEAF, LEAF), F32),
            pltpu.VMEM((LEAVES, LEAF, LEAF), BF),
            pltpu.SemaphoreType.DMA((20,)),
        ],
        compiler_params=pltpu.CompilerParams(vmem_limit_bytes=48 << 20),
        cost_estimate=pl.CostEstimate(flops=4_000_000_000, bytes_accessed=24_000_000, transcendentals=0),
        name="finish",
    )(near_list, jnp.asarray(SLOT_OF), q, *halos, blocks, upper, lower, basis, field)


def window_slots(wide, narrow, steps):
    row, col = lax.axis_index("narrow"), lax.axis_index("wide")
    wy, wx = np.arange(WINDOW) // 6, np.arange(WINDOW) % 6

    def slots(target_y, target_x, scale):
        y = target_y // 2 * 2 - 2 + wy
        x = target_x // 2 * 2 - 2 + wx
        inside = (y >= 0) & (y < narrow // scale) & (x >= 0) & (x < wide // scale)
        apart = {"narrow": (y * scale) ^ row, "wide": (x * scale) ^ col}
        slot = 0
        for at, (axis, bit) in enumerate(steps):
            slot = slot + (apart[axis] // bit & 1) * (1 << at)
        return jnp.where(inside, slot if scale == 1 else slot // 4, -1)

    parity2 = row % 2 * 2 + col % 2
    parity3 = row // 2 % 2 * 2 + col // 2 % 2
    return jnp.concatenate(
        [slots(row, col, 1), slots(row // 2, col // 2, 2), jnp.stack([parity2, parity3])]
    ).astype(jnp.int32)


def per_device(wide, narrow, charges, positions, noise, leaf_basis, transfer, near_list):
    q = charges.reshape(LEAVES, LEAF, LEAF)
    points = positions.reshape(LEAVES, 2, LEAF)
    basis = leaf_basis.reshape(LEAVES, RANK, LEAF)
    tree = transfer[0, 0]
    listing = near_list.reshape(-1)
    steps = gather_steps(wide, narrow)
    meta = window_slots(wide, narrow, steps)

    east, west, north, south, coefs, give = go_up(q, basis, tree, points)
    from_west = shift(east, "wide", 1)
    from_east = shift(west, "wide", -1)
    q_west = shift(charges[:, 2:4], "wide", 1)
    q_east = shift(charges[:, 0:2], "wide", -1)
    q_north = shift(charges[2:4], "narrow", 1)
    q_south = shift(charges[0:2], "narrow", -1)

    noise_rows = noise.reshape(LEAVES, 1, LEAF)

    def step(value, at):
        axis, bit = steps[at]
        return lax.ppermute(value, axis, [(i, i ^ bit) for i in range(lax.axis_size(axis))])

    def tie(*values):
        return lax.optimization_barrier(values)

    gathered = give
    other = step(gathered, 0)
    upper = near_own(0, q, points, noise_rows, give, [])
    other, from_west, from_east, upper = tie(other, from_west, from_east, upper)
    gathered = jnp.concatenate([gathered, other], axis=0)
    other = step(gathered, 1)
    to_north, to_south = join(north, south, from_west, from_east)
    from_south = shift(to_north, "narrow", -1)
    from_north = shift(to_south, "narrow", 1)
    lower = near_own(2, q, points, noise_rows, from_west, [upper])
    other, from_south, from_north, lower = tie(other, from_south, from_north, lower)
    for at in range(2, len(steps)):
        gathered = jnp.concatenate([gathered, other], axis=0)
        other = step(gathered, at)
        if at == 2:
            sums = local_far(listing, coefs, from_west, from_east, from_north, from_south)
            other, *sums = tie(other, *sums)
        if at == 3:
            blocks = edge_blocks(listing, sums[1], points, from_west, from_east, from_north, from_south)
            other, blocks = tie(other, blocks)
    gathered = jnp.concatenate([gathered, other], axis=0)
    q_west, q_east, blocks = tie(q_west, q_east, blocks)
    q_north_corner = shift(jnp.stack([q_west[2:4], q_east[2:4]]), "narrow", 1)
    q_south_corner = shift(jnp.stack([q_west[0:2], q_east[0:2]]), "narrow", -1)
    field = top_far(meta, gathered, tree, *sums)
    q_north_corner, q_south_corner, field = tie(q_north_corner, q_south_corner, field)
    halos = [
        value.reshape(8, LEAF, LEAF)
        for value in (q_west, q_east, q_north, q_north_corner, q_south, q_south_corner)
    ]
    out = finish(listing, q, halos, blocks, upper, lower, basis, field)
    return out.reshape(SIDE, SIDE, LEAF, LEAF)


def solution(mesh):
    wide, narrow = mesh.shape["wide"], mesh.shape["narrow"]
    in_specs = (
        P("narrow", "wide", None, None),
        P("narrow", "wide", None, None),
        P("narrow", "wide", None),
        P("narrow", "wide", None, None),
        P("narrow", "wide", None, None, None),
        P("narrow", "wide", None),
    )
    out_specs = P("narrow", "wide", None, None)

    def step(*arrays):
        return per_device(wide, narrow, *arrays)

    return jax.shard_map(step, mesh=mesh, in_specs=in_specs, out_specs=out_specs, check_vma=False)
```

```python
import math

import jax
import jax.numpy as jnp
import ml_dtypes
import numpy as np
from jax import lax
from jax.experimental import pallas as pl
from jax.experimental.pallas import tpu as pltpu
from jax.sharding import PartitionSpec as P

LEAF = 256
CHEB = 8
RANK = 64
NEAR = 10
SIDE = 4
LEAVES = SIDE * SIDE
TOP = 20
WINDOW = 36
PACK = RANK + 16
SIDEWAYS = 8 * RANK + 4 * RANK + 48
CORNER = 4 * RANK + 4 * RANK + 48
BIG = 58 << 20
COPIES = 42
BF = jnp.bfloat16
F32 = jnp.float32

short_len = 0.125
long_weight = 0.03125
reach = 3.0 * SIDE
waves = 10.0
LOG2E = math.log2(math.e)
long_rate = -0.5 / (reach * reach) * LOG2E / (waves * waves)
short_rate = -0.5 / (short_len * short_len) * LOG2E / (waves * waves)
rounder = 1.5 * 2.0**23


def sine_terms(count):
    w = np.cos(np.pi * (np.arange(2000) + 0.5) / 2000) * 0.25
    powers = np.stack([w ** (2 * i + 1) for i in range(count)], 1)
    return [float(c) for c in np.linalg.lstsq(powers, np.sin(2 * np.pi * w) * long_weight, rcond=None)[0]]


SINE = sine_terms(3)


def coupling(height, shift_y, shift_x):
    points = 0.5 * (1.0 + np.cos((2.0 * np.arange(CHEB) + 1.0) * (math.pi / (2.0 * CHEB))))
    node_x = np.tile(points, CHEB)
    node_y = np.repeat(points, CHEB)
    gap_x = (node_x[:, None] - node_x[None, :] - shift_x) * 2.0**height
    gap_y = (node_y[:, None] - node_y[None, :] - shift_y) * 2.0**height
    squared = gap_x * gap_x + gap_y * gap_y
    return np.exp(squared * (-0.5 / (short_len * short_len))) + long_weight * np.exp(
        squared * (-0.5 / (reach * reach))
    ) * np.cos(2.0 * math.pi * waves * np.sqrt(squared))


def window_coupling(height):
    table = np.zeros((2, 2, RANK, 6, 6, RANK))
    for py in range(2):
        for px in range(2):
            for wy in range(6):
                for wx in range(6):
                    shift_y, shift_x = wy - 2 - py, wx - 2 - px
                    if max(abs(shift_y), abs(shift_x)) >= 2:
                        table[py, px, :, wy, wx] = coupling(height, shift_y, shift_x)
    return table.reshape(4 * RANK, WINDOW * RANK).astype(ml_dtypes.bfloat16)


def code_coupling():
    return np.stack([coupling(0, code // 5 - 2, code % 5 - 2) for code in range(25)]).astype(ml_dtypes.bfloat16)


def halo_slot(row, col):
    if 0 <= row < 4 and 0 <= col < 4:
        return row * 4 + col
    if 0 <= row < 4:
        return 16 + row * 2 + col + 2 if col < 0 else 24 + row * 2 + col - 4
    base, r = (32, row + 2) if row < 0 else (48, row - 4)
    if 0 <= col < 4:
        return base + r * 4 + col
    return base + 8 + r * 2 + col + 2 if col < 0 else base + 12 + r * 2 + col - 4


SLOT_OF = np.array([halo_slot(r - 2, c - 2) for r in range(8) for c in range(8)], np.int32)


def near_table(own):
    width = 9 if own else 5
    table = np.zeros((LEAVES, width, 3), np.int32)
    table[:, :, 0] = -1
    for r in range(SIDE):
        for c in range(SIDE):
            at = 0
            for dy in (-1, 0, 1):
                for dx in (-1, 0, 1):
                    slot = halo_slot(r + dy, c + dx)
                    if (slot < LEAVES) == own:
                        table[r * SIDE + c, at] = (slot, dy, dx)
                        at += 1
    return table


def bits(count):
    return [1 << i for i in range(count.bit_length() - 1)]


def gather_steps(wide, narrow):
    return (
        [("wide", 1), ("narrow", 1)]
        + [("wide", b) for b in reversed(bits(wide)[1:])]
        + [("narrow", b) for b in reversed(bits(narrow)[1:])]
    )


def shift(value, axis, steps):
    count = lax.axis_size(axis)
    return lax.ppermute(value, axis, [(i, i + steps) for i in range(count) if 0 <= i + steps < count])


def dot(a, b):
    return jnp.dot(a, b, preferred_element_type=F32)


def dot_first(a, b):
    return lax.dot_general(a, b, (((0,), (0,)), ((), ())), preferred_element_type=F32)


def up_body(
    q_any, basis_any, tree_any, pos_ref, east_ref, west_ref, north_ref, south_ref, coef_ref, give_ref, q_ref, basis_ref, tree_ref, sems
):
    loads = []
    for k in range(4):
        part = pl.ds(4 * k, 4)
        loads.append(pltpu.make_async_copy(basis_any.at[part], basis_ref.at[part], sems.at[2 * k]))
        loads.append(pltpu.make_async_copy(q_any.at[part], q_ref.at[part], sems.at[2 * k + 1]))
    loads.append(pltpu.make_async_copy(tree_any, tree_ref, sems.at[8]))
    for load in loads:
        load.start()
    level0 = []
    for leaf in range(LEAVES):
        if leaf % 4 == 0:
            loads[leaf // 2].wait()
            loads[leaf // 2 + 1].wait()
        coef = dot(basis_ref[leaf], q_ref[leaf]).astype(BF)
        level0.append(coef)
        r, c = leaf // SIDE, leaf % SIDE
        coef_ref[leaf * RANK : (leaf + 1) * RANK] = coef
        ref, at = (west_ref, r * 2 + c) if c < 2 else (east_ref, r * 2 + c - 2)
        ref[at * RANK : (at + 1) * RANK] = coef
        ref, at = (north_ref, r * 4 + c) if r < 2 else (south_ref, r * 4 + c - 8)
        ref[at * RANK : (at + 1) * RANK] = coef
    loads[8].wait()
    level1 = []
    for r in range(2):
        for c in range(2):
            total = None
            for dr in range(2):
                for dc in range(2):
                    leaf = (2 * r + dr) * SIDE + 2 * c + dc
                    part = dot(tree_ref[leaf], level0[leaf])
                    total = part if total is None else total + part
            coef = total.astype(BF)
            at = r * 2 + c
            level1.append(coef)
            coef_ref[(LEAVES + at) * RANK : (LEAVES + at + 1) * RANK] = coef
            for ref in (east_ref, west_ref, north_ref, south_ref):
                ref[(8 + at) * RANK : (9 + at) * RANK] = coef
    total = None
    for at in range(4):
        part = dot(tree_ref[LEAVES + at], level1[at])
        total = part if total is None else total + part
    give_ref[0:RANK] = total.astype(BF)
    top = tree_ref[TOP]
    give_ref[RANK:PACK] = jnp.concatenate([top[16 * k : 16 * k + 16] for k in range(4)], axis=1)
    for ref, leaves in (
        (west_ref, [r * 4 + c for r in range(4) for c in (0, 1)]),
        (east_ref, [r * 4 + c for r in range(4) for c in (2, 3)]),
        (north_ref, range(8)),
        (south_ref, range(8, 16)),
    ):
        rest = jnp.concatenate([pos_ref[leaf] for leaf in leaves], axis=0)
        for part in range(3):
            held = rest.astype(BF)
            at = 12 * RANK + 16 * part
            ref[at : at + 16] = held
            rest = rest - held.astype(F32)


def go_up(q, basis, tree, points):
    vmem = pl.BlockSpec(memory_space=pltpu.VMEM)
    side = jax.ShapeDtypeStruct((SIDEWAYS, LEAF), BF)
    return pl.pallas_call(
        up_body,
        out_shape=(
            side,
            side,
            side,
            side,
            jax.ShapeDtypeStruct(((LEAVES + 4) * RANK, LEAF), BF),
            jax.ShapeDtypeStruct((PACK, LEAF), BF),
        ),
        in_specs=[pl.BlockSpec(memory_space=pl.ANY)] * 3 + [vmem],
        out_specs=[vmem] * 6,
        scratch_shapes=[
            pltpu.VMEM((LEAVES, LEAF, LEAF), BF),
            pltpu.VMEM((LEAVES, RANK, LEAF), BF),
            pltpu.VMEM((TOP + 1, RANK, RANK), BF),
            pltpu.SemaphoreType.DMA((9,)),
        ],
        compiler_params=pltpu.CompilerParams(vmem_limit_bytes=BIG),
        cost_estimate=pl.CostEstimate(flops=300_000_000, bytes_accessed=5_000_000, transcendentals=0),
        name="upward",
    )(q, basis, tree, points)


def local_body(
    list_ref, coef_any, west_any, east_any, north_any, south_any, c0_any, c1_any, code_any, sum0, sum1, pad0, pad1, c0_ref, c1_ref, code_ref, sems
):
    loads = []

    def load(source, at, to, row, count):
        rows = pl.ds(at * RANK if at < 100 else at, count * RANK)
        copy = pltpu.make_async_copy(source.at[rows], to.at[pl.ds(row, count * RANK)], sems.at[len(loads)])
        copy.start()
        loads.append(copy)

    def put(pad, extent, row, col, ref, at, count):
        load(ref, at, pad, ((row + 2) * (extent + 4) + col + 2) * RANK, count)

    whole = []
    for k, (source, to) in enumerate(((c0_any, c0_ref), (c1_any, c1_ref), (code_any, code_ref))):
        whole.append(pltpu.make_async_copy(source, to, sems.at[COPIES + k]))
    whole[0].start()
    for r in range(4):
        put(pad0, 4, r, 0, coef_any, r * 4, 4)
        put(pad0, 4, r, -2, west_any, r * 2, 2)
        put(pad0, 4, r, 4, east_any, r * 2, 2)
    for ref, row in ((north_any, -2), (south_any, 4)):
        for r in range(2):
            put(pad0, 4, row + r, 0, ref, r * 4, 4)
            for col, base in ((-2, SIDEWAYS), (4, SIDEWAYS + CORNER)):
                load(ref, base + r * 2 * RANK, pad0, ((row + r + 2) * 8 + col + 2) * RANK, 2)
    split = len(loads)
    for copy in whole[1:]:
        copy.start()
    for r in range(2):
        put(pad1, 2, r, 0, coef_any, LEAVES + r * 2, 2)
        put(pad1, 2, r, -2, west_any, 8 + r * 2, 2)
        put(pad1, 2, r, 2, east_any, 8 + r * 2, 2)
    for ref, row in ((north_any, -2), (south_any, 2)):
        for r in range(2):
            put(pad1, 2, row + r, 0, ref, 8 + r * 2, 2)
            for col, base in ((-2, SIDEWAYS), (2, SIDEWAYS + CORNER)):
                load(ref, base + (4 + r * 2) * RANK, pad1, ((row + r + 2) * 6 + col + 2) * RANK, 2)
    whole[0].wait()
    for copy in loads[:split]:
        copy.wait()
    for a in range(2):
        for b in range(2):
            total = None
            for wy in range(6):
                at = ((2 * a + wy) * 8 + 2 * b) * RANK
                part = dot(c0_ref[:, wy * 6 * RANK : (wy + 1) * 6 * RANK], pad0[at : at + 6 * RANK])
                total = part if total is None else total + part
            for child in range(4):
                leaf = (2 * a + child // 2) * SIDE + 2 * b + child % 2
                sum0[leaf] = total[child * RANK : (child + 1) * RANK]
    for copy in loads[split:] + whole[1:]:
        copy.wait()

    def listed(leaf, carry):
        code = second_cycle(list_ref, leaf)

        @pl.when(code >= 0)
        def _():
            row = leaf // SIDE + code // 5
            col = leaf % SIDE + code % 5
            at = pl.multiple_of((row * 8 + col) * RANK, RANK)
            sum0[leaf] = sum0[leaf] - dot(code_ref[code], pad0[pl.ds(at, RANK)])

        return carry

    lax.fori_loop(0, LEAVES, listed, 0)
    sum1[...] = dot(c1_ref[...], pad1[...])


def local_far(near_list, coefs, west, east, north, south):
    vmem = pl.BlockSpec(memory_space=pltpu.VMEM)
    smem = pl.BlockSpec(memory_space=pltpu.SMEM)
    return pl.pallas_call(
        local_body,
        out_shape=(
            jax.ShapeDtypeStruct((LEAVES, RANK, LEAF), F32),
            jax.ShapeDtypeStruct((4 * RANK, LEAF), F32),
        ),
        in_specs=[smem] + [pl.BlockSpec(memory_space=pl.ANY)] * 8,
        out_specs=[vmem] * 2,
        scratch_shapes=[
            pltpu.VMEM((64 * RANK, LEAF), BF),
            pltpu.VMEM((WINDOW * RANK, LEAF), BF),
            pltpu.VMEM((4 * RANK, WINDOW * RANK), BF),
            pltpu.VMEM((4 * RANK, WINDOW * RANK), BF),
            pltpu.VMEM((25, RANK, RANK), BF),
            pltpu.SemaphoreType.DMA((COPIES + 3,)),
        ],
        compiler_params=pltpu.CompilerParams(vmem_limit_bytes=BIG),
        cost_estimate=pl.CostEstimate(flops=5_000_000_000, bytes_accessed=8_000_000, transcendentals=0),
        name="local_far",
    )(
        near_list,
        coefs,
        west,
        east,
        north,
        south,
        jnp.asarray(window_coupling(0)),
        jnp.asarray(window_coupling(1)),
        jnp.asarray(code_coupling()),
    )


def top_body(
    meta_ref, all_any, c2_any, c3_any, tree_any, sum0_any, sum1_any, field_ref, win, parents, c2_ref, c3_ref, all_ref, tree_ref, sum0, sum1, sems
):
    loads = []
    for k, (source, to) in enumerate(((all_any, all_ref), (tree_any, tree_ref), (sum1_any, sum1), (sum0_any, sum0))):
        loads.append(pltpu.make_async_copy(source, to, sems.at[2 + k]))
        loads[-1].start()

    def slab(source, to, at):
        part = pl.ds(pl.multiple_of(meta_ref[2 * WINDOW + at] * RANK, RANK), RANK)
        copy = pltpu.make_async_copy(source.at[part], to, sems.at[at])
        copy.start()
        return copy

    slabs = [slab(c2_any, c2_ref, 0), slab(c3_any, c3_ref, 1)]

    loads[0].wait()

    def lift(group, carry):
        total = jnp.zeros((RANK, LEAF), F32)
        for child in range(4):
            at = pl.multiple_of((group * 4 + child) * PACK, 16)
            packed = all_ref[pl.ds(at + RANK, 16)]
            matrix = jnp.concatenate([packed[:, k * RANK : (k + 1) * RANK] for k in range(4)], axis=0)
            total = total + dot(matrix, all_ref[pl.ds(at, RANK)])
        parents[pl.ds(pl.multiple_of(group * RANK, RANK), RANK)] = total.astype(BF)
        return carry

    lax.fori_loop(0, parents.shape[0] // RANK, lift, 0)

    def fill(start, source, stride):
        def one(i, carry):
            slot = meta_ref[start + i]
            to = pl.ds(pl.multiple_of(i * RANK, RANK), RANK)

            @pl.when(slot >= 0)
            def _():
                win[to] = source[pl.ds(pl.multiple_of(slot * stride, 16), RANK)]

            @pl.when(slot < 0)
            def _():
                win[to] = jnp.zeros((RANK, LEAF), BF)

            return carry

        lax.fori_loop(0, WINDOW, one, 0)

    fill(WINDOW, parents, RANK)
    slabs[1].wait()
    field3 = dot(c3_ref[...], win[...]).astype(BF)
    fill(0, all_ref, PACK)
    slabs[0].wait()
    for load in loads[1:]:
        load.wait()
    field2 = (dot(c2_ref[...], win[...]) + dot_first(tree_ref[TOP], field3)).astype(BF)
    field1 = []
    for at in range(4):
        field1.append(
            (sum1[at * RANK : (at + 1) * RANK] + dot_first(tree_ref[LEAVES + at], field2)).astype(BF)
        )
    for leaf in range(LEAVES):
        above = field1[leaf // SIDE // 2 * 2 + leaf % SIDE // 2]
        field_ref[leaf] = (sum0[leaf] + dot_first(tree_ref[leaf], above)).astype(BF)


def second_cycle(list_ref, leaf):
    found = jnp.int32(-1)
    for j in range(NEAR):
        code = list_ref[leaf * NEAR + j]
        y, x = code // 5, code % 5
        outer = (code >= 0) & ((y == 0) | (y == 4) | (x == 0) | (x == 4))
        found = jnp.where(outer, code, found)
    return found


def top_far(meta, gathered, tree, sum0, sum1):
    vmem = pl.BlockSpec(memory_space=pltpu.VMEM)
    smem = pl.BlockSpec(memory_space=pltpu.SMEM)
    anywhere = pl.BlockSpec(memory_space=pl.ANY)
    devices = gathered.shape[0] // PACK
    return pl.pallas_call(
        top_body,
        out_shape=jax.ShapeDtypeStruct((LEAVES, RANK, LEAF), BF),
        in_specs=[smem] + [anywhere] * 6,
        out_specs=vmem,
        scratch_shapes=[
            pltpu.VMEM((WINDOW * RANK, LEAF), BF),
            pltpu.VMEM((devices // 4 * RANK, LEAF), BF),
            pltpu.VMEM((RANK, WINDOW * RANK), BF),
            pltpu.VMEM((RANK, WINDOW * RANK), BF),
            pltpu.VMEM(gathered.shape, BF),
            pltpu.VMEM((TOP + 1, RANK, RANK), BF),
            pltpu.VMEM((LEAVES, RANK, LEAF), F32),
            pltpu.VMEM((4 * RANK, LEAF), F32),
            pltpu.SemaphoreType.DMA((6,)),
        ],
        compiler_params=pltpu.CompilerParams(vmem_limit_bytes=BIG),
        cost_estimate=pl.CostEstimate(flops=3_000_000_000, bytes_accessed=5_000_000, transcendentals=0),
        name="top_far",
    )(meta, gathered, jnp.asarray(window_coupling(2)), jnp.asarray(window_coupling(3)), tree, sum0, sum1)


def join_body(north_ref, south_ref, west_ref, east_ref, to_north, to_south, sems):
    copies = []

    def move(source, at, to, row, count):
        copy = pltpu.make_async_copy(source.at[pl.ds(at, count)], to.at[pl.ds(row, count)], sems.at[len(copies)])
        copy.start()
        copies.append(copy)

    for own, to, lower in ((north_ref, to_north, 0), (south_ref, to_south, 1)):
        move(own, 0, to, 0, SIDEWAYS)
        for side, base in ((west_ref, SIDEWAYS), (east_ref, SIDEWAYS + CORNER)):
            move(side, 4 * RANK * lower, to, base, 4 * RANK)
            move(side, 8 * RANK, to, base + 4 * RANK, CORNER - 4 * RANK)
    for copy in copies:
        copy.wait()


def join(north, south, west, east):
    anywhere = pl.BlockSpec(memory_space=pl.ANY)
    message = jax.ShapeDtypeStruct((SIDEWAYS + 2 * CORNER, LEAF), BF)
    return pl.pallas_call(
        join_body,
        out_shape=(message, message),
        in_specs=[anywhere] * 4,
        out_specs=[pl.BlockSpec(memory_space=pltpu.VMEM)] * 2,
        scratch_shapes=[pltpu.SemaphoreType.DMA((10,))],
        cost_estimate=pl.CostEstimate(flops=0, bytes_accessed=4_000_000, transcendentals=0),
        name="join",
    )(north, south, west, east)


def kernel_of(target_x, target_y, source_x, source_y):
    gap_x = target_x - source_x
    gap_y = target_y - source_y
    squared = jnp.maximum(gap_x * gap_x + gap_y * gap_y, 1e-12)
    length = squared * lax.rsqrt(squared)
    phase = length - ((length + rounder) - rounder)
    w = 0.25 - jnp.abs(phase)
    s = w * w
    wave = w * (SINE[0] + s * (SINE[1] + s * SINE[2]))
    return (jnp.exp2(squared * short_rate) + jnp.exp2(squared * long_rate) * wave).astype(BF)


def spread_columns(rows, columns):
    turned = rows.T
    for k in range(columns.shape[1] // 128):
        columns[:, 128 * k : 128 * (k + 1)] = jnp.broadcast_to(turned[:, k : k + 1], (LEAF, 128))


def block_into(to, columns, points, shift_y, shift_x):
    source_x = (points[0:1] + shift_x.astype(F32)) * waves
    source_y = (points[1:2] + shift_y.astype(F32)) * waves
    rows = 32
    for i in range(0, LEAF, rows):
        for j in (0, 128):
            to[i : i + rows, j : j + 128] = kernel_of(
                columns[i : i + rows, 0:128],
                columns[i : i + rows, 128:256],
                jnp.broadcast_to(source_x[:, j : j + 128], (rows, 128)),
                jnp.broadcast_to(source_y[:, j : j + 128], (rows, 128)),
            )


def turn_points(columns, leaf, position, noise):
    rows = jnp.concatenate([position * waves, noise, jnp.zeros((5, LEAF), F32)], axis=0)
    spread_columns(rows, columns.at[leaf])


def own_pairs(first):
    pairs = []
    for r in (first, first + 1):
        for c in range(SIDE):
            for dy, dx in ((0, 1), (1, -1), (1, 0), (1, 1)):
                if r + dy < SIDE and 0 <= c + dx < SIDE:
                    pairs.append((r * SIDE + c, (r + dy) * SIDE + c + dx, dy, dx))
    return pairs


def near_own_body(first, table_ref, q_any, pos_ref, noise_ref, *refs):
    before_any, out_ref, columns, blocks, q_ref, before_ref, sems = (None,) * (7 - len(refs)) + refs
    loads = [pltpu.make_async_copy(q_any, q_ref, sems.at[0])]
    if first:
        loads.append(pltpu.make_async_copy(before_any.at[pl.ds(8, SIDE)], before_ref, sems.at[1]))
    for load in loads:
        load.start()
    pairs = own_pairs(first)
    start = first * SIDE

    def turn(leaf, carry):
        turn_points(columns, leaf, pos_ref[leaf], noise_ref[leaf])
        return carry

    lax.fori_loop(start, start + 8, turn, 0)
    zero = jnp.int32(0)

    def selves(i, carry):
        for half in range(2):
            leaf = start + 2 * i + half
            block_into(blocks.at[2 * i + half], columns.at[leaf], pos_ref[leaf], zero, zero)
        return carry

    lax.fori_loop(0, 4, selves, 0)

    def both(i, carry):
        for half in range(2):
            at = 8 * i + 4 * half
            place = 8 + 4 * i + 2 * half
            target, source = table_ref[at], table_ref[at + 1]
            block_into(
                blocks.at[place], columns.at[target], pos_ref[source], table_ref[at + 2], table_ref[at + 3]
            )
            blocks[place + 1] = blocks[place].T
        return carry

    lax.fori_loop(0, len(pairs) // 2, both, 0)
    for load in loads:
        load.wait()
    parts = {leaf: [(leaf - start, leaf)] for leaf in range(start, start + 8)}
    for i, (target, source, _, _) in enumerate(pairs):
        parts[target].append((8 + 2 * i, source))
        parts.setdefault(source, []).append((9 + 2 * i, target))
    for leaf, terms in sorted(parts.items()):
        total = None
        for place, source in terms:
            part = dot(blocks[place], q_ref[source])
            total = part if total is None else total + part
        if leaf < start + 8:
            noise = jnp.concatenate([columns[leaf, :, 256:384]] * 2, axis=1)
            total = total + noise * q_ref[leaf].astype(F32)
        if first and leaf < start + SIDE:
            total = total + before_ref[leaf - start]
        out_ref[leaf - start] = total


def near_own(first, q, points, noise, after, before):
    vmem = pl.BlockSpec(memory_space=pltpu.VMEM)
    smem = pl.BlockSpec(memory_space=pltpu.SMEM)
    anywhere = pl.BlockSpec(memory_space=pl.ANY)
    pairs = own_pairs(first)

    def body(after_ref, *refs):
        near_own_body(first, *refs)

    return pl.pallas_call(
        body,
        out_shape=jax.ShapeDtypeStruct((12 if first == 0 else 8, LEAF, LEAF), F32),
        in_specs=[anywhere, smem, anywhere, vmem, vmem] + [anywhere] * len(before),
        out_specs=vmem,
        scratch_shapes=[
            pltpu.VMEM((LEAVES, LEAF, 384), F32),
            pltpu.VMEM((8 + 2 * len(pairs), LEAF, LEAF), BF),
            pltpu.VMEM((LEAVES, LEAF, LEAF), BF),
            pltpu.VMEM((SIDE, LEAF, LEAF), F32),
            pltpu.SemaphoreType.DMA((2,)),
        ],
        compiler_params=pltpu.CompilerParams(vmem_limit_bytes=40 << 20),
        cost_estimate=pl.CostEstimate(flops=10_000_000_000, bytes_accessed=4_000_000, transcendentals=8_000_000),
        name="near_own",
    )(after, jnp.asarray(np.array(pairs, np.int32).reshape(-1)), q, points, noise, *before)


def edge_items():
    table = near_table(False)
    return [[leaf, *table[leaf, j]] for leaf in range(LEAVES) for j in range(5) if table[leaf, j, 0] >= 0]


ITEMS = edge_items()
EDGES = len(ITEMS)


def extra_of(list_ref, slot_ref, leaf):
    code = second_cycle(list_ref, leaf)
    place = (leaf // SIDE + code // 5) * 8 + leaf % SIDE + code % 5
    slot = slot_ref[jnp.where(code >= 0, place, 0)]
    return code, slot


def edge_body(
    half_at, list_ref, table_ref, slot_ref, after_ref, own_pos_ref, west_any, east_any, north_any, south_any, out_any,
    columns, parts, points, out_ref, sems,
):
    start = 8 * half_at
    copies = []
    sources = (
        (west_any, 12 * RANK),
        (east_any, 12 * RANK),
        (north_any, 12 * RANK),
        (north_any, SIDEWAYS + 8 * RANK),
        (north_any, SIDEWAYS + CORNER + 8 * RANK),
        (south_any, 12 * RANK),
        (south_any, SIDEWAYS + 8 * RANK),
        (south_any, SIDEWAYS + CORNER + 8 * RANK),
    )
    for k, (source, at) in enumerate(sources):
        copies.append(pltpu.make_async_copy(source.at[pl.ds(at, 48)], parts.at[k], sems.at[k]))
    for copy in copies:
        copy.start()

    def turn(leaf, carry):
        turn_points(columns, leaf, own_pos_ref[leaf], jnp.zeros((1, LEAF), F32))
        return carry

    lax.fori_loop(start, start + 8, turn, 0)
    points[0:LEAVES] = own_pos_ref[...]
    for copy in copies:
        copy.wait()
    slots = (16, 24, 32, 40, 44, 48, 56, 60)
    for k in range(8):
        whole = parts[k].astype(F32)
        whole = (whole[0:16] + whole[16:32]) + whole[32:48]
        first, count = {3: (4, 4), 4: (4, 4), 6: (0, 4), 7: (0, 4)}.get(k, (0, 8))
        for i in range(count):
            points[slots[k] + i] = whole[2 * (first + i) : 2 * (first + i) + 2]

    def fixed(i, carry):
        for half in range(2):
            at = 8 * i + 4 * half
            block_into(
                out_ref.at[2 * i + half],
                columns.at[table_ref[at]],
                points[table_ref[at + 1]],
                table_ref[at + 2],
                table_ref[at + 3],
            )
        return carry

    lax.fori_loop(0, EDGES // 4, fixed, 0)
    backs = []
    for k, part in enumerate((pl.ds(0, EDGES // 2), pl.ds(EDGES // 2, 8))):
        backs.append(pltpu.make_async_copy(out_ref.at[part], out_any.at[part], sems.at[8 + k]))
    backs[0].start()

    def extra(i, carry):
        for half in range(2):
            leaf = start + 2 * i + half
            code, slot = extra_of(list_ref, slot_ref, leaf)
            code = jnp.maximum(code, 0)
            block_into(out_ref.at[EDGES // 2 + 2 * i + half], columns.at[leaf], points[slot], code // 5 - 2, code % 5 - 2)
        return carry

    lax.fori_loop(0, 4, extra, 0)
    backs[1].start()
    for back in backs:
        back.wait()


def edge_blocks(half_at, near_list, after, own_points, west, east, north, south):
    vmem = pl.BlockSpec(memory_space=pltpu.VMEM)
    smem = pl.BlockSpec(memory_space=pltpu.SMEM)
    anywhere = pl.BlockSpec(memory_space=pl.ANY)
    items = [item for item in ITEMS if item[0] // 8 == half_at]
    assert len(items) * 2 == EDGES

    def body(*refs):
        edge_body(half_at, *refs)

    return pl.pallas_call(
        body,
        out_shape=jax.ShapeDtypeStruct((EDGES // 2 + 8, LEAF, LEAF), BF),
        in_specs=[smem, smem, smem, anywhere, vmem] + [anywhere] * 4,
        out_specs=anywhere,
        scratch_shapes=[
            pltpu.VMEM((LEAVES, LEAF, 384), F32),
            pltpu.VMEM((8, 48, LEAF), BF),
            pltpu.VMEM((64, 2, LEAF), F32),
            pltpu.VMEM((EDGES // 2 + 8, LEAF, LEAF), BF),
            pltpu.SemaphoreType.DMA((10,)),
        ],
        compiler_params=pltpu.CompilerParams(vmem_limit_bytes=BIG),
        cost_estimate=pl.CostEstimate(flops=6_000_000_000, bytes_accessed=8_000_000, transcendentals=12_000_000),
        name="edge_blocks",
    )(
        near_list, jnp.asarray(np.array(items, np.int32).reshape(-1)), jnp.asarray(SLOT_OF), after, own_points,
        west, east, north, south,
    )


def final_body(
    list_ref, slot_ref, q_any, west_any, east_any, north_any, north_corner_any, south_any, south_corner_any,
    upper_blocks_any, lower_blocks_any, upper_any, lower_any, basis_ref, field_ref, out_any, held, blocks, sums, outs, sems,
):
    firsts = [min(at for at in range(EDGES) if ITEMS[at][0] // SIDE == r) for r in range(SIDE)] + [EDGES]
    stages = [[], [], [], []]
    count = 0

    def copy(stage, source, to):
        nonlocal count
        made = pltpu.make_async_copy(source, to, sems.at[count])
        count += 1
        stages[stage].append(made)
        made.start()

    for r in range(SIDE):
        if r == 0:
            for source, at in ((north_any, 32), (north_corner_any, 40), (west_any, 16), (east_any, 24)):
                copy(r, source, held.at[pl.ds(at, 8)])
        if r == SIDE - 1:
            for source, at in ((south_any, 48), (south_corner_any, 56)):
                copy(r, source, held.at[pl.ds(at, 8)])
        part = pl.ds(firsts[r], firsts[r + 1] - firsts[r])
        source, back = (upper_blocks_any, 0) if r < 2 else (lower_blocks_any, EDGES // 2)
        copy(r, source.at[pl.ds(firsts[r] - back, firsts[r + 1] - firsts[r])], blocks.at[part])
        source = upper_any.at[pl.ds(SIDE * r, SIDE)] if r < 2 else lower_any.at[pl.ds(SIDE * (r - 2), SIDE)]
        copy(r, source, sums.at[pl.ds(SIDE * r, SIDE)])
    copy(SIDE - 1, q_any, held.at[pl.ds(0, 16)])
    for half_at, source in enumerate((upper_blocks_any, lower_blocks_any)):
        copy(SIDE - 1, source.at[pl.ds(EDGES // 2, 8)], blocks.at[pl.ds(EDGES + 8 * half_at, 8)])
    for leaf in range(LEAVES):
        if leaf % SIDE == 0:
            for made in stages[leaf // SIDE]:
                made.wait()
        total = dot_first(basis_ref[leaf], field_ref[leaf])
        for at in range(EDGES):
            if ITEMS[at][0] == leaf:
                total = total + dot(blocks[at], held[ITEMS[at][1]])
        sums[leaf] += total

    backs = []
    for r in range(SIDE):
        part = pl.ds(SIDE * r, SIDE)
        backs.append(pltpu.make_async_copy(outs.at[part], out_any.at[part], sems.at[count + r]))

    for r in range(SIDE):

        def finish(leaf, carry):
            code, slot = extra_of(list_ref, slot_ref, leaf)

            @pl.when(code >= 0)
            def _():
                outs[leaf] = (sums[leaf] + dot(blocks[EDGES + leaf], held[slot])).astype(BF)

            @pl.when(code < 0)
            def _():
                outs[leaf] = sums[leaf].astype(BF)

            return carry

        lax.fori_loop(SIDE * r, SIDE * (r + 1), finish, 0)
        backs[r].start()
    for back in backs:
        back.wait()


def finish(near_list, q, halos, upper_blocks, lower_blocks, upper, lower, basis, field):
    vmem = pl.BlockSpec(memory_space=pltpu.VMEM)
    smem = pl.BlockSpec(memory_space=pltpu.SMEM)
    anywhere = pl.BlockSpec(memory_space=pl.ANY)

    return pl.pallas_call(
        final_body,
        out_shape=jax.ShapeDtypeStruct((LEAVES, LEAF, LEAF), BF),
        in_specs=[smem, smem] + [anywhere] * 11 + [vmem, vmem],
        out_specs=anywhere,
        scratch_shapes=[
            pltpu.VMEM((64, LEAF, LEAF), BF),
            pltpu.VMEM((EDGES + LEAVES, LEAF, LEAF), BF),
            pltpu.VMEM((LEAVES, LEAF, LEAF), F32),
            pltpu.VMEM((LEAVES, LEAF, LEAF), BF),
            pltpu.SemaphoreType.DMA((21,)),
        ],
        compiler_params=pltpu.CompilerParams(vmem_limit_bytes=BIG),
        cost_estimate=pl.CostEstimate(flops=4_000_000_000, bytes_accessed=24_000_000, transcendentals=0),
        name="finish",
    )(near_list, jnp.asarray(SLOT_OF), q, *halos, upper_blocks, lower_blocks, upper, lower, basis, field)


def window_slots(wide, narrow, steps):
    row, col = lax.axis_index("narrow"), lax.axis_index("wide")
    wy, wx = np.arange(WINDOW) // 6, np.arange(WINDOW) % 6

    def slots(target_y, target_x, scale):
        y = target_y // 2 * 2 - 2 + wy
        x = target_x // 2 * 2 - 2 + wx
        inside = (y >= 0) & (y < narrow // scale) & (x >= 0) & (x < wide // scale)
        apart = {"narrow": (y * scale) ^ row, "wide": (x * scale) ^ col}
        slot = 0
        for at, (axis, bit) in enumerate(steps):
            slot = slot + (apart[axis] // bit & 1) * (1 << at)
        return jnp.where(inside, slot if scale == 1 else slot // 4, -1)

    parity2 = row % 2 * 2 + col % 2
    parity3 = row // 2 % 2 * 2 + col // 2 % 2
    return jnp.concatenate(
        [slots(row, col, 1), slots(row // 2, col // 2, 2), jnp.stack([parity2, parity3])]
    ).astype(jnp.int32)


def per_device(wide, narrow, charges, positions, noise, leaf_basis, transfer, near_list):
    q = charges.reshape(LEAVES, LEAF, LEAF)
    points = positions.reshape(LEAVES, 2, LEAF)
    basis = leaf_basis.reshape(LEAVES, RANK, LEAF)
    tree = transfer[0, 0]
    listing = near_list.reshape(-1)
    steps = gather_steps(wide, narrow)
    meta = window_slots(wide, narrow, steps)

    east, west, north, south, coefs, give = go_up(q, basis, tree, points)
    from_west = shift(east, "wide", 1)
    from_east = shift(west, "wide", -1)
    q_north = shift(charges[2:4], "narrow", 1)
    q_south = shift(charges[0:2], "narrow", -1)

    noise_rows = noise.reshape(LEAVES, 1, LEAF)

    def step(value, at):
        axis, bit = steps[at]
        return lax.ppermute(value, axis, [(i, i ^ bit) for i in range(lax.axis_size(axis))])

    def tie(*values):
        return lax.optimization_barrier(values)

    gathered = give
    other = step(gathered, 0)
    upper = near_own(0, q, points, noise_rows, give, [])
    to_east, to_west = charges[:, 2:4], charges[:, 0:2]
    other, from_west, from_east, upper, to_east, to_west = tie(other, from_west, from_east, upper, to_east, to_west)
    to_north, to_south = join(north, south, from_west, from_east)
    from_south = shift(to_north, "narrow", -1)
    from_north = shift(to_south, "narrow", 1)
    q_west = shift(to_east, "wide", 1)
    q_east = shift(to_west, "wide", -1)
    gathered = jnp.concatenate([gathered, other], axis=0)
    other = step(gathered, 1)
    lower = near_own(2, q, points, noise_rows, to_north, [upper])
    other, from_south, from_north, lower = tie(other, from_south, from_north, lower)
    for at in range(2, len(steps)):
        gathered = jnp.concatenate([gathered, other], axis=0)
        other = step(gathered, at)
        if at == 2:
            sums = local_far(listing, coefs, from_west, from_east, from_north, from_south)
            other, *sums = tie(other, *sums)
        if at == 3:
            upper_blocks = edge_blocks(0, listing, sums[1], points, from_west, from_east, from_north, from_south)
            other, upper_blocks, q_west, q_east = tie(other, upper_blocks, q_west, q_east)
            q_north_corner = shift(jnp.stack([q_west[2:4], q_east[2:4]]), "narrow", 1)
            q_south_corner = shift(jnp.stack([q_west[0:2], q_east[0:2]]), "narrow", -1)
        if at == 4:
            lower_blocks = edge_blocks(1, listing, upper_blocks, points, from_west, from_east, from_north, from_south)
            other, lower_blocks = tie(other, lower_blocks)
    gathered = jnp.concatenate([gathered, other], axis=0)
    field = top_far(meta, gathered, tree, *sums)
    q_north_corner, q_south_corner, field = tie(q_north_corner, q_south_corner, field)
    halos = [
        value.reshape(8, LEAF, LEAF)
        for value in (q_west, q_east, q_north, q_north_corner, q_south, q_south_corner)
    ]
    out = finish(listing, q, halos, upper_blocks, lower_blocks, upper, lower, basis, field)
    return out.reshape(SIDE, SIDE, LEAF, LEAF)


def solution(mesh):
    wide, narrow = mesh.shape["wide"], mesh.shape["narrow"]
    in_specs = (
        P("narrow", "wide", None, None),
        P("narrow", "wide", None, None),
        P("narrow", "wide", None),
        P("narrow", "wide", None, None),
        P("narrow", "wide", None, None, None),
        P("narrow", "wide", None),
    )
    out_specs = P("narrow", "wide", None, None)

    def step(*arrays):
        return per_device(wide, narrow, *arrays)

    return jax.shard_map(step, mesh=mesh, in_specs=in_specs, out_specs=out_specs, check_vma=False)
```

```python
import math

import jax
import jax.numpy as jnp
import ml_dtypes
import numpy as np
from jax import lax
from jax.experimental import pallas as pl
from jax.experimental.pallas import tpu as pltpu
from jax.sharding import PartitionSpec as P

LEAF = 256
CHEB = 8
RANK = 64
NEAR = 10
SIDE = 4
LEAVES = SIDE * SIDE
TOP = 20
WINDOW = 36
PACK = RANK + 16
SIDEWAYS = 8 * RANK + 4 * RANK + 48
CORNER = 4 * RANK + 4 * RANK + 48
BIG = 58 << 20
COPIES = 42
BF = jnp.bfloat16
F32 = jnp.float32

short_len = 0.125
long_weight = 0.03125
reach = 3.0 * SIDE
waves = 10.0
LOG2E = math.log2(math.e)
long_rate = -0.5 / (reach * reach) * LOG2E / (waves * waves)
short_rate = -0.5 / (short_len * short_len) * LOG2E / (waves * waves)
rounder = 1.5 * 2.0**23


def sine_terms(count):
    w = np.cos(np.pi * (np.arange(2000) + 0.5) / 2000) * 0.25
    powers = np.stack([w ** (2 * i + 1) for i in range(count)], 1)
    return [float(c) for c in np.linalg.lstsq(powers, np.sin(2 * np.pi * w) * long_weight, rcond=None)[0]]


SINE = sine_terms(3)


def coupling(height, shift_y, shift_x):
    points = 0.5 * (1.0 + np.cos((2.0 * np.arange(CHEB) + 1.0) * (math.pi / (2.0 * CHEB))))
    node_x = np.tile(points, CHEB)
    node_y = np.repeat(points, CHEB)
    gap_x = (node_x[:, None] - node_x[None, :] - shift_x) * 2.0**height
    gap_y = (node_y[:, None] - node_y[None, :] - shift_y) * 2.0**height
    squared = gap_x * gap_x + gap_y * gap_y
    return np.exp(squared * (-0.5 / (short_len * short_len))) + long_weight * np.exp(
        squared * (-0.5 / (reach * reach))
    ) * np.cos(2.0 * math.pi * waves * np.sqrt(squared))


def window_coupling(height):
    table = np.zeros((2, 2, RANK, 6, 6, RANK))
    for py in range(2):
        for px in range(2):
            for wy in range(6):
                for wx in range(6):
                    shift_y, shift_x = wy - 2 - py, wx - 2 - px
                    if max(abs(shift_y), abs(shift_x)) >= 2:
                        table[py, px, :, wy, wx] = coupling(height, shift_y, shift_x)
    return table.reshape(4 * RANK, WINDOW * RANK).astype(ml_dtypes.bfloat16)


def code_coupling():
    return np.stack([coupling(0, code // 5 - 2, code % 5 - 2) for code in range(25)]).astype(ml_dtypes.bfloat16)


def halo_slot(row, col):
    if 0 <= row < 4 and 0 <= col < 4:
        return row * 4 + col
    if 0 <= row < 4:
        return 16 + row * 2 + col + 2 if col < 0 else 24 + row * 2 + col - 4
    base, r = (32, row + 2) if row < 0 else (48, row - 4)
    if 0 <= col < 4:
        return base + r * 4 + col
    return base + 8 + r * 2 + col + 2 if col < 0 else base + 12 + r * 2 + col - 4


SLOT_OF = np.array([halo_slot(r - 2, c - 2) for r in range(8) for c in range(8)], np.int32)


def near_table(own):
    width = 9 if own else 5
    table = np.zeros((LEAVES, width, 3), np.int32)
    table[:, :, 0] = -1
    for r in range(SIDE):
        for c in range(SIDE):
            at = 0
            for dy in (-1, 0, 1):
                for dx in (-1, 0, 1):
                    slot = halo_slot(r + dy, c + dx)
                    if (slot < LEAVES) == own:
                        table[r * SIDE + c, at] = (slot, dy, dx)
                        at += 1
    return table


def bits(count):
    return [1 << i for i in range(count.bit_length() - 1)]


def gather_steps(wide, narrow):
    return (
        [("wide", 1), ("narrow", 1)]
        + [("wide", b) for b in reversed(bits(wide)[1:])]
        + [("narrow", b) for b in reversed(bits(narrow)[1:])]
    )


def shift(value, axis, steps):
    count = lax.axis_size(axis)
    return lax.ppermute(value, axis, [(i, i + steps) for i in range(count) if 0 <= i + steps < count])


def dot(a, b):
    return jnp.dot(a, b, preferred_element_type=F32)


def dot_first(a, b):
    return lax.dot_general(a, b, (((0,), (0,)), ((), ())), preferred_element_type=F32)


def up_body(
    q_any, basis_any, tree_any, pos_ref, east_ref, west_ref, north_ref, south_ref, coef_ref, give_ref, q_ref, basis_ref, tree_ref, sems
):
    loads = []
    for k in range(4):
        part = pl.ds(4 * k, 4)
        loads.append(pltpu.make_async_copy(basis_any.at[part], basis_ref.at[part], sems.at[2 * k]))
        loads.append(pltpu.make_async_copy(q_any.at[part], q_ref.at[part], sems.at[2 * k + 1]))
    loads.append(pltpu.make_async_copy(tree_any, tree_ref, sems.at[8]))
    for load in loads:
        load.start()
    level0 = []
    for leaf in range(LEAVES):
        if leaf % 4 == 0:
            loads[leaf // 2].wait()
            loads[leaf // 2 + 1].wait()
        coef = dot(basis_ref[leaf], q_ref[leaf]).astype(BF)
        level0.append(coef)
        r, c = leaf // SIDE, leaf % SIDE
        coef_ref[leaf * RANK : (leaf + 1) * RANK] = coef
        ref, at = (west_ref, r * 2 + c) if c < 2 else (east_ref, r * 2 + c - 2)
        ref[at * RANK : (at + 1) * RANK] = coef
        ref, at = (north_ref, r * 4 + c) if r < 2 else (south_ref, r * 4 + c - 8)
        ref[at * RANK : (at + 1) * RANK] = coef
    loads[8].wait()
    level1 = []
    for r in range(2):
        for c in range(2):
            total = None
            for dr in range(2):
                for dc in range(2):
                    leaf = (2 * r + dr) * SIDE + 2 * c + dc
                    part = dot(tree_ref[leaf], level0[leaf])
                    total = part if total is None else total + part
            coef = total.astype(BF)
            at = r * 2 + c
            level1.append(coef)
            coef_ref[(LEAVES + at) * RANK : (LEAVES + at + 1) * RANK] = coef
            for ref in (east_ref, west_ref, north_ref, south_ref):
                ref[(8 + at) * RANK : (9 + at) * RANK] = coef
    total = None
    for at in range(4):
        part = dot(tree_ref[LEAVES + at], level1[at])
        total = part if total is None else total + part
    give_ref[0:RANK] = total.astype(BF)
    top = tree_ref[TOP]
    give_ref[RANK:PACK] = jnp.concatenate([top[16 * k : 16 * k + 16] for k in range(4)], axis=1)
    for ref, leaves in (
        (west_ref, [r * 4 + c for r in range(4) for c in (0, 1)]),
        (east_ref, [r * 4 + c for r in range(4) for c in (2, 3)]),
        (north_ref, range(8)),
        (south_ref, range(8, 16)),
    ):
        rest = jnp.concatenate([pos_ref[leaf] for leaf in leaves], axis=0)
        for part in range(3):
            held = rest.astype(BF)
            at = 12 * RANK + 16 * part
            ref[at : at + 16] = held
            rest = rest - held.astype(F32)


def go_up(q, basis, tree, points):
    vmem = pl.BlockSpec(memory_space=pltpu.VMEM)
    side = jax.ShapeDtypeStruct((SIDEWAYS, LEAF), BF)
    return pl.pallas_call(
        up_body,
        out_shape=(
            side,
            side,
            side,
            side,
            jax.ShapeDtypeStruct(((LEAVES + 4) * RANK, LEAF), BF),
            jax.ShapeDtypeStruct((PACK, LEAF), BF),
        ),
        in_specs=[pl.BlockSpec(memory_space=pl.ANY)] * 3 + [vmem],
        out_specs=[vmem] * 6,
        scratch_shapes=[
            pltpu.VMEM((LEAVES, LEAF, LEAF), BF),
            pltpu.VMEM((LEAVES, RANK, LEAF), BF),
            pltpu.VMEM((TOP + 1, RANK, RANK), BF),
            pltpu.SemaphoreType.DMA((9,)),
        ],
        compiler_params=pltpu.CompilerParams(vmem_limit_bytes=BIG),
        cost_estimate=pl.CostEstimate(flops=300_000_000, bytes_accessed=5_000_000, transcendentals=0),
        name="upward",
    )(q, basis, tree, points)


def local_body(
    list_ref, coef_any, west_any, east_any, north_any, south_any, c0_any, c1_any, code_any, sum0, sum1, pad0, pad1, c0_ref, c1_ref, code_ref, sems
):
    loads = []

    def load(source, at, to, row, count):
        rows = pl.ds(at * RANK if at < 100 else at, count * RANK)
        copy = pltpu.make_async_copy(source.at[rows], to.at[pl.ds(row, count * RANK)], sems.at[len(loads)])
        copy.start()
        loads.append(copy)

    def put(pad, extent, row, col, ref, at, count):
        load(ref, at, pad, ((row + 2) * (extent + 4) + col + 2) * RANK, count)

    whole = []
    for k, (source, to) in enumerate(((c0_any, c0_ref), (c1_any, c1_ref), (code_any, code_ref))):
        whole.append(pltpu.make_async_copy(source, to, sems.at[COPIES + k]))
    whole[0].start()
    for r in range(4):
        put(pad0, 4, r, 0, coef_any, r * 4, 4)
        put(pad0, 4, r, -2, west_any, r * 2, 2)
        put(pad0, 4, r, 4, east_any, r * 2, 2)
    for ref, row in ((north_any, -2), (south_any, 4)):
        for r in range(2):
            put(pad0, 4, row + r, 0, ref, r * 4, 4)
            for col, base in ((-2, SIDEWAYS), (4, SIDEWAYS + CORNER)):
                load(ref, base + r * 2 * RANK, pad0, ((row + r + 2) * 8 + col + 2) * RANK, 2)
    split = len(loads)
    for copy in whole[1:]:
        copy.start()
    for r in range(2):
        put(pad1, 2, r, 0, coef_any, LEAVES + r * 2, 2)
        put(pad1, 2, r, -2, west_any, 8 + r * 2, 2)
        put(pad1, 2, r, 2, east_any, 8 + r * 2, 2)
    for ref, row in ((north_any, -2), (south_any, 2)):
        for r in range(2):
            put(pad1, 2, row + r, 0, ref, 8 + r * 2, 2)
            for col, base in ((-2, SIDEWAYS), (2, SIDEWAYS + CORNER)):
                load(ref, base + (4 + r * 2) * RANK, pad1, ((row + r + 2) * 6 + col + 2) * RANK, 2)
    whole[0].wait()
    for copy in loads[:split]:
        copy.wait()
    for a in range(2):
        for b in range(2):
            total = None
            for wy in range(6):
                at = ((2 * a + wy) * 8 + 2 * b) * RANK
                part = dot(c0_ref[:, wy * 6 * RANK : (wy + 1) * 6 * RANK], pad0[at : at + 6 * RANK])
                total = part if total is None else total + part
            for child in range(4):
                leaf = (2 * a + child // 2) * SIDE + 2 * b + child % 2
                sum0[leaf] = total[child * RANK : (child + 1) * RANK]
    for copy in loads[split:] + whole[1:]:
        copy.wait()

    def listed(leaf, carry):
        code = second_cycle(list_ref, leaf)

        @pl.when(code >= 0)
        def _():
            row = leaf // SIDE + code // 5
            col = leaf % SIDE + code % 5
            at = pl.multiple_of((row * 8 + col) * RANK, RANK)
            sum0[leaf] = sum0[leaf] - dot(code_ref[code], pad0[pl.ds(at, RANK)])

        return carry

    lax.fori_loop(0, LEAVES, listed, 0)
    sum1[...] = dot(c1_ref[...], pad1[...])


def local_far(near_list, coefs, west, east, north, south):
    vmem = pl.BlockSpec(memory_space=pltpu.VMEM)
    smem = pl.BlockSpec(memory_space=pltpu.SMEM)
    return pl.pallas_call(
        local_body,
        out_shape=(
            jax.ShapeDtypeStruct((LEAVES, RANK, LEAF), F32),
            jax.ShapeDtypeStruct((4 * RANK, LEAF), F32),
        ),
        in_specs=[smem] + [pl.BlockSpec(memory_space=pl.ANY)] * 8,
        out_specs=[vmem] * 2,
        scratch_shapes=[
            pltpu.VMEM((64 * RANK, LEAF), BF),
            pltpu.VMEM((WINDOW * RANK, LEAF), BF),
            pltpu.VMEM((4 * RANK, WINDOW * RANK), BF),
            pltpu.VMEM((4 * RANK, WINDOW * RANK), BF),
            pltpu.VMEM((25, RANK, RANK), BF),
            pltpu.SemaphoreType.DMA((COPIES + 3,)),
        ],
        compiler_params=pltpu.CompilerParams(vmem_limit_bytes=BIG),
        cost_estimate=pl.CostEstimate(flops=5_000_000_000, bytes_accessed=8_000_000, transcendentals=0),
        name="local_far",
    )(
        near_list,
        coefs,
        west,
        east,
        north,
        south,
        jnp.asarray(window_coupling(0)),
        jnp.asarray(window_coupling(1)),
        jnp.asarray(code_coupling()),
    )


def top_body(
    meta_ref, all_any, c2_any, c3_any, tree_any, sum0_any, sum1_any, field_ref, win, parents, c2_ref, c3_ref, all_ref, tree_ref, sum0, sum1, sems
):
    loads = []
    for k, (source, to) in enumerate(((all_any, all_ref), (tree_any, tree_ref), (sum1_any, sum1), (sum0_any, sum0))):
        loads.append(pltpu.make_async_copy(source, to, sems.at[2 + k]))
        loads[-1].start()

    def slab(source, to, at):
        part = pl.ds(pl.multiple_of(meta_ref[2 * WINDOW + at] * RANK, RANK), RANK)
        copy = pltpu.make_async_copy(source.at[part], to, sems.at[at])
        copy.start()
        return copy

    slabs = [slab(c2_any, c2_ref, 0), slab(c3_any, c3_ref, 1)]

    loads[0].wait()

    def lift(group, carry):
        total = jnp.zeros((RANK, LEAF), F32)
        for child in range(4):
            at = pl.multiple_of((group * 4 + child) * PACK, 16)
            packed = all_ref[pl.ds(at + RANK, 16)]
            matrix = jnp.concatenate([packed[:, k * RANK : (k + 1) * RANK] for k in range(4)], axis=0)
            total = total + dot(matrix, all_ref[pl.ds(at, RANK)])
        parents[pl.ds(pl.multiple_of(group * RANK, RANK), RANK)] = total.astype(BF)
        return carry

    lax.fori_loop(0, parents.shape[0] // RANK, lift, 0)

    def fill(start, source, stride):
        def one(i, carry):
            slot = meta_ref[start + i]
            to = pl.ds(pl.multiple_of(i * RANK, RANK), RANK)

            @pl.when(slot >= 0)
            def _():
                win[to] = source[pl.ds(pl.multiple_of(slot * stride, 16), RANK)]

            @pl.when(slot < 0)
            def _():
                win[to] = jnp.zeros((RANK, LEAF), BF)

            return carry

        lax.fori_loop(0, WINDOW, one, 0)

    fill(WINDOW, parents, RANK)
    slabs[1].wait()
    field3 = dot(c3_ref[...], win[...]).astype(BF)
    fill(0, all_ref, PACK)
    slabs[0].wait()
    for load in loads[1:]:
        load.wait()
    field2 = (dot(c2_ref[...], win[...]) + dot_first(tree_ref[TOP], field3)).astype(BF)
    field1 = []
    for at in range(4):
        field1.append(
            (sum1[at * RANK : (at + 1) * RANK] + dot_first(tree_ref[LEAVES + at], field2)).astype(BF)
        )
    for leaf in range(LEAVES):
        above = field1[leaf // SIDE // 2 * 2 + leaf % SIDE // 2]
        field_ref[leaf] = (sum0[leaf] + dot_first(tree_ref[leaf], above)).astype(BF)


def second_cycle(list_ref, leaf):
    found = jnp.int32(-1)
    for j in range(NEAR):
        code = list_ref[leaf * NEAR + j]
        y, x = code // 5, code % 5
        outer = (code >= 0) & ((y == 0) | (y == 4) | (x == 0) | (x == 4))
        found = jnp.where(outer, code, found)
    return found


def top_far(meta, gathered, tree, sum0, sum1):
    vmem = pl.BlockSpec(memory_space=pltpu.VMEM)
    smem = pl.BlockSpec(memory_space=pltpu.SMEM)
    anywhere = pl.BlockSpec(memory_space=pl.ANY)
    devices = gathered.shape[0] // PACK
    return pl.pallas_call(
        top_body,
        out_shape=jax.ShapeDtypeStruct((LEAVES, RANK, LEAF), BF),
        in_specs=[smem] + [anywhere] * 6,
        out_specs=vmem,
        scratch_shapes=[
            pltpu.VMEM((WINDOW * RANK, LEAF), BF),
            pltpu.VMEM((devices // 4 * RANK, LEAF), BF),
            pltpu.VMEM((RANK, WINDOW * RANK), BF),
            pltpu.VMEM((RANK, WINDOW * RANK), BF),
            pltpu.VMEM(gathered.shape, BF),
            pltpu.VMEM((TOP + 1, RANK, RANK), BF),
            pltpu.VMEM((LEAVES, RANK, LEAF), F32),
            pltpu.VMEM((4 * RANK, LEAF), F32),
            pltpu.SemaphoreType.DMA((6,)),
        ],
        compiler_params=pltpu.CompilerParams(vmem_limit_bytes=BIG),
        cost_estimate=pl.CostEstimate(flops=3_000_000_000, bytes_accessed=5_000_000, transcendentals=0),
        name="top_far",
    )(meta, gathered, jnp.asarray(window_coupling(2)), jnp.asarray(window_coupling(3)), tree, sum0, sum1)


def join_body(north_ref, south_ref, west_ref, east_ref, north_any, south_any, to_north, to_south, sems):
    copies = []

    def move(source, at, to, row, count):
        copy = pltpu.make_async_copy(source.at[pl.ds(at, count)], to.at[pl.ds(row, count)], sems.at[len(copies)])
        copy.start()
        copies.append(copy)

    for own, to, lower in ((north_ref, to_north, 0), (south_ref, to_south, 1)):
        move(own, 0, to, 0, SIDEWAYS)
        for side, base in ((west_ref, SIDEWAYS), (east_ref, SIDEWAYS + CORNER)):
            move(side, 4 * RANK * lower, to, base, 4 * RANK)
            move(side, 8 * RANK, to, base + 4 * RANK, CORNER - 4 * RANK)
    backs = []
    for k, (held, to) in enumerate(((to_north, north_any), (to_south, south_any))):
        for copy in copies[5 * k : 5 * k + 5]:
            copy.wait()
        backs.append(pltpu.make_async_copy(held, to, sems.at[10 + k]))
        backs[-1].start()
    for back in backs:
        back.wait()


def join(north, south, west, east):
    anywhere = pl.BlockSpec(memory_space=pl.ANY)
    message = jax.ShapeDtypeStruct((SIDEWAYS + 2 * CORNER, LEAF), BF)
    return pl.pallas_call(
        join_body,
        out_shape=(message, message),
        in_specs=[anywhere] * 4,
        out_specs=[anywhere] * 2,
        scratch_shapes=[pltpu.VMEM(message.shape, BF)] * 2 + [pltpu.SemaphoreType.DMA((12,))],
        compiler_params=pltpu.CompilerParams(vmem_limit_bytes=BIG),
        cost_estimate=pl.CostEstimate(flops=0, bytes_accessed=4_000_000, transcendentals=0),
        name="join",
    )(north, south, west, east)


def kernel_of(target_x, target_y, source_x, source_y):
    gap_x = target_x - source_x
    gap_y = target_y - source_y
    squared = jnp.maximum(gap_x * gap_x + gap_y * gap_y, 1e-12)
    length = squared * lax.rsqrt(squared)
    phase = length - ((length + rounder) - rounder)
    w = 0.25 - jnp.abs(phase)
    s = w * w
    wave = w * (SINE[0] + s * (SINE[1] + s * SINE[2]))
    return (jnp.exp2(squared * short_rate) + jnp.exp2(squared * long_rate) * wave).astype(BF)


def spread_columns(rows, columns):
    turned = rows.T
    for k in range(columns.shape[1] // 128):
        columns[:, 128 * k : 128 * (k + 1)] = jnp.broadcast_to(turned[:, k : k + 1], (LEAF, 128))


def block_into(to, columns, points, shift_y, shift_x):
    source_x = (points[0:1] + shift_x.astype(F32)) * waves
    source_y = (points[1:2] + shift_y.astype(F32)) * waves
    rows = 32
    for i in range(0, LEAF, rows):
        for j in (0, 128):
            to[i : i + rows, j : j + 128] = kernel_of(
                columns[i : i + rows, 0:128],
                columns[i : i + rows, 128:256],
                jnp.broadcast_to(source_x[:, j : j + 128], (rows, 128)),
                jnp.broadcast_to(source_y[:, j : j + 128], (rows, 128)),
            )


def turn_points(columns, leaf, position, noise):
    rows = jnp.concatenate([position * waves, noise, jnp.zeros((5, LEAF), F32)], axis=0)
    spread_columns(rows, columns.at[leaf])


def own_pairs(first, last):
    pairs = []
    for r in range(first, last):
        for c in range(SIDE):
            for dy, dx in ((0, 1), (1, -1), (1, 0), (1, 1)):
                if r + dy < SIDE and 0 <= c + dx < SIDE:
                    pairs.append((r * SIDE + c, (r + dy) * SIDE + c + dx, dy, dx))
    return pairs


def near_own_body(first, last, table_ref, q_any, pos_ref, noise_ref, *refs):
    before_any, out_any, columns, blocks, q_ref, before_ref, out_ref, sems = (None,) * (8 - len(refs)) + refs
    loads = [pltpu.make_async_copy(q_any, q_ref, sems.at[0])]
    if first:
        loads.append(pltpu.make_async_copy(before_any.at[pl.ds(SIDE, SIDE)], before_ref, sems.at[1]))
    for load in loads:
        load.start()
    pairs = own_pairs(first, last)
    start = first * SIDE
    count = (last - first) * SIDE

    def turn(leaf, carry):
        turn_points(columns, leaf, pos_ref[leaf], noise_ref[leaf])
        return carry

    lax.fori_loop(start, start + count, turn, 0)
    zero = jnp.int32(0)

    def selves(i, carry):
        for half in range(2):
            leaf = start + 2 * i + half
            block_into(blocks.at[2 * i + half], columns.at[leaf], pos_ref[leaf], zero, zero)
        return carry

    lax.fori_loop(0, count // 2, selves, 0)

    def pair(i):
        at = 4 * i
        place = count + 2 * i
        target, source = table_ref[at], table_ref[at + 1]
        block_into(blocks.at[place], columns.at[target], pos_ref[source], table_ref[at + 2], table_ref[at + 3])
        blocks[place + 1] = blocks[place].T

    def both(i, carry):
        pair(2 * i)
        pair(2 * i + 1)
        return carry

    lax.fori_loop(0, len(pairs) // 2, both, 0)
    if len(pairs) % 2:
        pair(len(pairs) - 1)
    for load in loads:
        load.wait()
    parts = {leaf: [(leaf - start, leaf)] for leaf in range(start, start + count)}
    for i, (target, source, _, _) in enumerate(pairs):
        parts[target].append((count + 2 * i, source))
        parts.setdefault(source, []).append((count + 1 + 2 * i, target))
    backs = []
    for leaf, terms in sorted(parts.items()):
        total = None
        for place, source in terms:
            part = dot(blocks[place], q_ref[source])
            total = part if total is None else total + part
        if leaf < start + count:
            noise = jnp.concatenate([columns[leaf, :, 256:384]] * 2, axis=1)
            total = total + noise * q_ref[leaf].astype(F32)
        if first and leaf < start + SIDE:
            total = total + before_ref[leaf - start]
        out_ref[leaf - start] = total
        backs.append(pltpu.make_async_copy(out_ref.at[leaf - start], out_any.at[leaf - start], sems.at[2 + leaf - start]))
        backs[-1].start()
    for back in backs:
        back.wait()


def near_own(first, last, q, points, noise, after, before):
    vmem = pl.BlockSpec(memory_space=pltpu.VMEM)
    smem = pl.BlockSpec(memory_space=pltpu.SMEM)
    anywhere = pl.BlockSpec(memory_space=pl.ANY)
    pairs = own_pairs(first, last)
    leaves = (min(last + 1, SIDE) - first) * SIDE

    def body(after_ref, *refs):
        near_own_body(first, last, *refs)

    return pl.pallas_call(
        body,
        out_shape=jax.ShapeDtypeStruct((leaves, LEAF, LEAF), F32),
        in_specs=[anywhere, smem, anywhere, vmem, vmem] + [anywhere] * len(before),
        out_specs=anywhere,
        scratch_shapes=[
            pltpu.VMEM((LEAVES, LEAF, 384), F32),
            pltpu.VMEM(((last - first) * SIDE + 2 * len(pairs), LEAF, LEAF), BF),
            pltpu.VMEM((LEAVES, LEAF, LEAF), BF),
            pltpu.VMEM((SIDE, LEAF, LEAF), F32),
            pltpu.VMEM((leaves, LEAF, LEAF), F32),
            pltpu.SemaphoreType.DMA((2 + leaves,)),
        ],
        compiler_params=pltpu.CompilerParams(vmem_limit_bytes=BIG),
        cost_estimate=pl.CostEstimate(flops=6_000_000_000, bytes_accessed=4_000_000, transcendentals=8_000_000),
        name="near_own",
    )(after, jnp.asarray(np.array(pairs, np.int32).reshape(-1)), q, points, noise, *before)


def edge_items():
    table = near_table(False)
    return [[leaf, *table[leaf, j]] for leaf in range(LEAVES) for j in range(5) if table[leaf, j, 0] >= 0]


ITEMS = edge_items()
EDGES = len(ITEMS)


def extra_of(list_ref, slot_ref, leaf):
    code = second_cycle(list_ref, leaf)
    place = (leaf // SIDE + code // 5) * 8 + leaf % SIDE + code % 5
    slot = slot_ref[jnp.where(code >= 0, place, 0)]
    return code, slot


def edge_body(
    half_at, list_ref, table_ref, slot_ref, after_ref, own_pos_ref, west_any, east_any, north_any, south_any, out_any,
    columns, parts, points, out_ref, sems,
):
    start = 8 * half_at
    copies = []
    sources = (
        (west_any, 12 * RANK),
        (east_any, 12 * RANK),
        (north_any, 12 * RANK),
        (north_any, SIDEWAYS + 8 * RANK),
        (north_any, SIDEWAYS + CORNER + 8 * RANK),
        (south_any, 12 * RANK),
        (south_any, SIDEWAYS + 8 * RANK),
        (south_any, SIDEWAYS + CORNER + 8 * RANK),
    )
    for k, (source, at) in enumerate(sources):
        copies.append(pltpu.make_async_copy(source.at[pl.ds(at, 48)], parts.at[k], sems.at[k]))
    for copy in copies:
        copy.start()

    def turn(leaf, carry):
        turn_points(columns, leaf, own_pos_ref[leaf], jnp.zeros((1, LEAF), F32))
        return carry

    lax.fori_loop(start, start + 8, turn, 0)
    points[0:LEAVES] = own_pos_ref[...]
    for copy in copies:
        copy.wait()
    slots = (16, 24, 32, 40, 44, 48, 56, 60)
    for k in range(8):
        whole = parts[k].astype(F32)
        whole = (whole[0:16] + whole[16:32]) + whole[32:48]
        first, count = {3: (4, 4), 4: (4, 4), 6: (0, 4), 7: (0, 4)}.get(k, (0, 8))
        for i in range(count):
            points[slots[k] + i] = whole[2 * (first + i) : 2 * (first + i) + 2]

    def fixed(i, carry):
        for half in range(2):
            at = 8 * i + 4 * half
            block_into(
                out_ref.at[2 * i + half],
                columns.at[table_ref[at]],
                points[table_ref[at + 1]],
                table_ref[at + 2],
                table_ref[at + 3],
            )
        return carry

    lax.fori_loop(0, EDGES // 4, fixed, 0)
    backs = []
    for k, part in enumerate((pl.ds(0, EDGES // 2), pl.ds(EDGES // 2, 8))):
        backs.append(pltpu.make_async_copy(out_ref.at[part], out_any.at[part], sems.at[8 + k]))
    backs[0].start()

    def extra(i, carry):
        for half in range(2):
            leaf = start + 2 * i + half
            code, slot = extra_of(list_ref, slot_ref, leaf)
            code = jnp.maximum(code, 0)
            block_into(out_ref.at[EDGES // 2 + 2 * i + half], columns.at[leaf], points[slot], code // 5 - 2, code % 5 - 2)
        return carry

    lax.fori_loop(0, 4, extra, 0)
    backs[1].start()
    for back in backs:
        back.wait()


def edge_blocks(half_at, near_list, after, own_points, west, east, north, south):
    vmem = pl.BlockSpec(memory_space=pltpu.VMEM)
    smem = pl.BlockSpec(memory_space=pltpu.SMEM)
    anywhere = pl.BlockSpec(memory_space=pl.ANY)
    items = [item for item in ITEMS if item[0] // 8 == half_at]
    assert len(items) * 2 == EDGES

    def body(*refs):
        edge_body(half_at, *refs)

    return pl.pallas_call(
        body,
        out_shape=jax.ShapeDtypeStruct((EDGES // 2 + 8, LEAF, LEAF), BF),
        in_specs=[smem, smem, smem, anywhere, vmem] + [anywhere] * 4,
        out_specs=anywhere,
        scratch_shapes=[
            pltpu.VMEM((LEAVES, LEAF, 384), F32),
            pltpu.VMEM((8, 48, LEAF), BF),
            pltpu.VMEM((64, 2, LEAF), F32),
            pltpu.VMEM((EDGES // 2 + 8, LEAF, LEAF), BF),
            pltpu.SemaphoreType.DMA((10,)),
        ],
        compiler_params=pltpu.CompilerParams(vmem_limit_bytes=BIG),
        cost_estimate=pl.CostEstimate(flops=6_000_000_000, bytes_accessed=8_000_000, transcendentals=12_000_000),
        name="edge_blocks",
    )(
        near_list, jnp.asarray(np.array(items, np.int32).reshape(-1)), jnp.asarray(SLOT_OF), after, own_points,
        west, east, north, south,
    )


def final_body(
    list_ref, slot_ref, q_any, west_any, east_any, north_any, north_corner_any, south_any, south_corner_any,
    upper_blocks_any, lower_blocks_any, row0_any, row1_any, row2_any, basis_ref, field_ref, out_any, held, blocks, sums, outs, sems,
):
    firsts = [min(at for at in range(EDGES) if ITEMS[at][0] // SIDE == r) for r in range(SIDE)] + [EDGES]
    stages = [[], [], [], []]
    count = 0

    def copy(stage, source, to):
        nonlocal count
        made = pltpu.make_async_copy(source, to, sems.at[count])
        count += 1
        stages[stage].append(made)

    for r in range(SIDE):
        if r == 0:
            for source, at in ((north_any, 32), (north_corner_any, 40)):
                copy(r, source, held.at[pl.ds(at, 8)])
        for source, at in ((west_any, 16), (east_any, 24)):
            for low, high in {0: ((0, 4),), 1: ((4, 6),), 2: ((6, 8),)}.get(r, ()):
                copy(r, source.at[pl.ds(low, high - low)], held.at[pl.ds(at + low, high - low)])
        if r == SIDE - 1:
            for source, at in ((south_any, 48), (south_corner_any, 56)):
                copy(r, source, held.at[pl.ds(at, 8)])
        part = pl.ds(firsts[r], firsts[r + 1] - firsts[r])
        source, back = (upper_blocks_any, 0) if r < 2 else (lower_blocks_any, EDGES // 2)
        copy(r, source.at[pl.ds(firsts[r] - back, firsts[r + 1] - firsts[r])], blocks.at[part])
        source = (row0_any, row1_any, row2_any, row2_any)[r].at[pl.ds(SIDE if r == 3 else 0, SIDE)]
        copy(r, source, sums.at[pl.ds(SIDE * r, SIDE)])
    copy(SIDE - 1, q_any, held.at[pl.ds(0, 16)])
    for half_at, source in enumerate((upper_blocks_any, lower_blocks_any)):
        copy(SIDE - 1, source.at[pl.ds(EDGES // 2, 8)], blocks.at[pl.ds(EDGES + 8 * half_at, 8)])
    for r in range(2):
        for made in stages[r]:
            made.start()
    for leaf in range(LEAVES):
        if leaf % SIDE == 0:
            for made in stages[leaf // SIDE]:
                made.wait()
            if leaf // SIDE + 2 < SIDE:
                for made in stages[leaf // SIDE + 2]:
                    made.start()
        total = dot_first(basis_ref[leaf], field_ref[leaf])
        for at in range(EDGES):
            if ITEMS[at][0] == leaf:
                total = total + dot(blocks[at], held[ITEMS[at][1]])
        sums[leaf] += total

    backs = []
    for r in range(SIDE):
        part = pl.ds(SIDE * r, SIDE)
        backs.append(pltpu.make_async_copy(outs.at[part], out_any.at[part], sems.at[count + r]))

    for r in range(SIDE):

        def finish(leaf, carry):
            code, slot = extra_of(list_ref, slot_ref, leaf)

            @pl.when(code >= 0)
            def _():
                outs[leaf] = (sums[leaf] + dot(blocks[EDGES + leaf], held[slot])).astype(BF)

            @pl.when(code < 0)
            def _():
                outs[leaf] = sums[leaf].astype(BF)

            return carry

        lax.fori_loop(SIDE * r, SIDE * (r + 1), finish, 0)
        backs[r].start()
    for back in backs:
        back.wait()


def finish(near_list, q, halos, upper_blocks, lower_blocks, sums, basis, field):
    vmem = pl.BlockSpec(memory_space=pltpu.VMEM)
    smem = pl.BlockSpec(memory_space=pltpu.SMEM)
    anywhere = pl.BlockSpec(memory_space=pl.ANY)

    return pl.pallas_call(
        final_body,
        out_shape=jax.ShapeDtypeStruct((LEAVES, LEAF, LEAF), BF),
        in_specs=[smem, smem] + [anywhere] * 12 + [vmem, vmem],
        out_specs=anywhere,
        scratch_shapes=[
            pltpu.VMEM((64, LEAF, LEAF), BF),
            pltpu.VMEM((EDGES + LEAVES, LEAF, LEAF), BF),
            pltpu.VMEM((LEAVES, LEAF, LEAF), F32),
            pltpu.VMEM((LEAVES, LEAF, LEAF), BF),
            pltpu.SemaphoreType.DMA((26,)),
        ],
        compiler_params=pltpu.CompilerParams(vmem_limit_bytes=BIG),
        cost_estimate=pl.CostEstimate(flops=4_000_000_000, bytes_accessed=24_000_000, transcendentals=0),
        name="finish",
    )(near_list, jnp.asarray(SLOT_OF), q, *halos, upper_blocks, lower_blocks, *sums, basis, field)


def window_slots(wide, narrow, steps):
    row, col = lax.axis_index("narrow"), lax.axis_index("wide")
    wy, wx = np.arange(WINDOW) // 6, np.arange(WINDOW) % 6

    def slots(target_y, target_x, scale):
        y = target_y // 2 * 2 - 2 + wy
        x = target_x // 2 * 2 - 2 + wx
        inside = (y >= 0) & (y < narrow // scale) & (x >= 0) & (x < wide // scale)
        apart = {"narrow": (y * scale) ^ row, "wide": (x * scale) ^ col}
        slot = 0
        for at, (axis, bit) in enumerate(steps):
            slot = slot + (apart[axis] // bit & 1) * (1 << at)
        return jnp.where(inside, slot if scale == 1 else slot // 4, -1)

    parity2 = row % 2 * 2 + col % 2
    parity3 = row // 2 % 2 * 2 + col // 2 % 2
    return jnp.concatenate(
        [slots(row, col, 1), slots(row // 2, col // 2, 2), jnp.stack([parity2, parity3])]
    ).astype(jnp.int32)


def per_device(wide, narrow, charges, positions, noise, leaf_basis, transfer, near_list):
    q = charges.reshape(LEAVES, LEAF, LEAF)
    points = positions.reshape(LEAVES, 2, LEAF)
    basis = leaf_basis.reshape(LEAVES, RANK, LEAF)
    tree = transfer[0, 0]
    listing = near_list.reshape(-1)
    steps = gather_steps(wide, narrow)
    meta = window_slots(wide, narrow, steps)

    east, west, north, south, coefs, give = go_up(q, basis, tree, points)
    from_west = shift(east, "wide", 1)
    from_east = shift(west, "wide", -1)
    q_north = shift(charges[2:4], "narrow", 1)
    q_south = shift(charges[0:2], "narrow", -1)

    noise_rows = noise.reshape(LEAVES, 1, LEAF)

    def step(value, at):
        axis, bit = steps[at]
        return lax.ppermute(value, axis, [(i, i ^ bit) for i in range(lax.axis_size(axis))])

    def tie(*values):
        return lax.optimization_barrier(values)

    gathered = give
    other = step(gathered, 0)
    row0 = near_own(0, 1, q, points, noise_rows, give, [])
    other, row0 = tie(other, row0)
    gathered = jnp.concatenate([gathered, other], axis=0)
    other = step(gathered, 1)
    row1 = near_own(1, 2, q, points, noise_rows, gathered, [row0])
    to_east, to_west = charges[:, 2:4], charges[:, 0:2]
    other, from_west, from_east, row1, to_east, to_west = tie(other, from_west, from_east, row1, to_east, to_west)
    gathered = jnp.concatenate([gathered, other], axis=0)
    other = step(gathered, 2)
    to_north, to_south = join(north, south, from_west, from_east)
    from_south = shift(to_north, "narrow", -1)
    from_north = shift(to_south, "narrow", 1)
    q_west = shift(to_east, "wide", 1)
    q_east = shift(to_west, "wide", -1)
    row2 = near_own(2, 4, q, points, noise_rows, to_north, [row1])
    other, from_south, from_north, row2 = tie(other, from_south, from_north, row2)
    gathered = jnp.concatenate([gathered, other], axis=0)
    other = step(gathered, 3)
    sums = local_far(listing, coefs, from_west, from_east, from_north, from_south)
    upper_blocks = edge_blocks(0, listing, sums[1], points, from_west, from_east, from_north, from_south)
    other, upper_blocks, q_west, q_east = tie(other, upper_blocks, q_west, q_east)
    for at in range(4, len(steps)):
        gathered = jnp.concatenate([gathered, other], axis=0)
        other = step(gathered, at)
        if at == 4:
            q_north_corner = shift(jnp.stack([q_west[2:4], q_east[2:4]]), "narrow", 1)
            q_south_corner = shift(jnp.stack([q_west[0:2], q_east[0:2]]), "narrow", -1)
            lower_blocks = edge_blocks(1, listing, upper_blocks, points, from_west, from_east, from_north, from_south)
            other, lower_blocks = tie(other, lower_blocks)
    gathered = jnp.concatenate([gathered, other], axis=0)
    field = top_far(meta, gathered, tree, *sums)
    q_north_corner, q_south_corner, field = tie(q_north_corner, q_south_corner, field)
    halos = [
        value.reshape(8, LEAF, LEAF)
        for value in (q_west, q_east, q_north, q_north_corner, q_south, q_south_corner)
    ]
    out = finish(listing, q, halos, upper_blocks, lower_blocks, (row0, row1, row2), basis, field)
    return out.reshape(SIDE, SIDE, LEAF, LEAF)


def solution(mesh):
    wide, narrow = mesh.shape["wide"], mesh.shape["narrow"]
    in_specs = (
        P("narrow", "wide", None, None),
        P("narrow", "wide", None, None),
        P("narrow", "wide", None),
        P("narrow", "wide", None, None),
        P("narrow", "wide", None, None, None),
        P("narrow", "wide", None),
    )
    out_specs = P("narrow", "wide", None, None)

    def step(*arrays):
        return per_device(wide, narrow, *arrays)

    return jax.shard_map(step, mesh=mesh, in_specs=in_specs, out_specs=out_specs, check_vma=False)
```

```python
import math

import jax
import jax.numpy as jnp
import ml_dtypes
import numpy as np
from jax import lax
from jax.experimental import pallas as pl
from jax.experimental.pallas import tpu as pltpu
from jax.sharding import PartitionSpec as P

LEAF = 256
CHEB = 8
RANK = 64
NEAR = 10
SIDE = 4
LEAVES = SIDE * SIDE
TOP = 20
WINDOW = 36
PACK = RANK + 16
SIDEWAYS = 8 * RANK + 4 * RANK + 48
CORNER = 4 * RANK + 4 * RANK + 48
BIG = 58 << 20
COPIES = 42
BF = jnp.bfloat16
F32 = jnp.float32

short_len = 0.125
long_weight = 0.03125
reach = 3.0 * SIDE
waves = 10.0
LOG2E = math.log2(math.e)
long_rate = -0.5 / (reach * reach) * LOG2E / (waves * waves)
short_rate = -0.5 / (short_len * short_len) * LOG2E / (waves * waves)
rounder = 1.5 * 2.0**23


def sine_terms(count):
    w = np.cos(np.pi * (np.arange(2000) + 0.5) / 2000) * 0.25
    powers = np.stack([w ** (2 * i + 1) for i in range(count)], 1)
    return [float(c) for c in np.linalg.lstsq(powers, np.sin(2 * np.pi * w) * long_weight, rcond=None)[0]]


SINE = sine_terms(3)


def coupling(height, shift_y, shift_x):
    points = 0.5 * (1.0 + np.cos((2.0 * np.arange(CHEB) + 1.0) * (math.pi / (2.0 * CHEB))))
    node_x = np.tile(points, CHEB)
    node_y = np.repeat(points, CHEB)
    gap_x = (node_x[:, None] - node_x[None, :] - shift_x) * 2.0**height
    gap_y = (node_y[:, None] - node_y[None, :] - shift_y) * 2.0**height
    squared = gap_x * gap_x + gap_y * gap_y
    return np.exp(squared * (-0.5 / (short_len * short_len))) + long_weight * np.exp(
        squared * (-0.5 / (reach * reach))
    ) * np.cos(2.0 * math.pi * waves * np.sqrt(squared))


def window_coupling(height):
    table = np.zeros((2, 2, RANK, 6, 6, RANK))
    for py in range(2):
        for px in range(2):
            for wy in range(6):
                for wx in range(6):
                    shift_y, shift_x = wy - 2 - py, wx - 2 - px
                    if max(abs(shift_y), abs(shift_x)) >= 2:
                        table[py, px, :, wy, wx] = coupling(height, shift_y, shift_x)
    return table.reshape(4 * RANK, WINDOW * RANK).astype(ml_dtypes.bfloat16)


def code_coupling():
    return np.stack([coupling(0, code // 5 - 2, code % 5 - 2) for code in range(25)]).astype(ml_dtypes.bfloat16)


def halo_slot(row, col):
    if 0 <= row < 4 and 0 <= col < 4:
        return row * 4 + col
    if 0 <= row < 4:
        return 16 + row * 2 + col + 2 if col < 0 else 24 + row * 2 + col - 4
    base, r = (32, row + 2) if row < 0 else (48, row - 4)
    if 0 <= col < 4:
        return base + r * 4 + col
    return base + 8 + r * 2 + col + 2 if col < 0 else base + 12 + r * 2 + col - 4


SLOT_OF = np.array([halo_slot(r - 2, c - 2) for r in range(8) for c in range(8)], np.int32)


def near_table(own):
    width = 9 if own else 5
    table = np.zeros((LEAVES, width, 3), np.int32)
    table[:, :, 0] = -1
    for r in range(SIDE):
        for c in range(SIDE):
            at = 0
            for dy in (-1, 0, 1):
                for dx in (-1, 0, 1):
                    slot = halo_slot(r + dy, c + dx)
                    if (slot < LEAVES) == own:
                        table[r * SIDE + c, at] = (slot, dy, dx)
                        at += 1
    return table


def bits(count):
    return [1 << i for i in range(count.bit_length() - 1)]


def gather_steps(wide, narrow):
    return (
        [("wide", 1), ("narrow", 1)]
        + [("wide", b) for b in reversed(bits(wide)[1:])]
        + [("narrow", b) for b in reversed(bits(narrow)[1:])]
    )


def shift(value, axis, steps):
    count = lax.axis_size(axis)
    return lax.ppermute(value, axis, [(i, i + steps) for i in range(count) if 0 <= i + steps < count])


def dot(a, b):
    return jnp.dot(a, b, preferred_element_type=F32)


def dot_first(a, b):
    return lax.dot_general(a, b, (((0,), (0,)), ((), ())), preferred_element_type=F32)


def up_body(
    q_any, basis_any, tree_any, pos_ref, east_ref, west_ref, north_ref, south_ref, coef_ref, give_ref, q_ref, basis_ref, tree_ref, sems
):
    loads = []
    for k in range(4):
        part = pl.ds(4 * k, 4)
        loads.append(pltpu.make_async_copy(basis_any.at[part], basis_ref.at[part], sems.at[2 * k]))
        loads.append(pltpu.make_async_copy(q_any.at[part], q_ref.at[part], sems.at[2 * k + 1]))
    loads.append(pltpu.make_async_copy(tree_any, tree_ref, sems.at[8]))
    for load in loads:
        load.start()
    level0 = []
    for leaf in range(LEAVES):
        if leaf % 4 == 0:
            loads[leaf // 2].wait()
            loads[leaf // 2 + 1].wait()
        coef = dot(basis_ref[leaf], q_ref[leaf]).astype(BF)
        level0.append(coef)
        r, c = leaf // SIDE, leaf % SIDE
        coef_ref[leaf * RANK : (leaf + 1) * RANK] = coef
        ref, at = (west_ref, r * 2 + c) if c < 2 else (east_ref, r * 2 + c - 2)
        ref[at * RANK : (at + 1) * RANK] = coef
        ref, at = (north_ref, r * 4 + c) if r < 2 else (south_ref, r * 4 + c - 8)
        ref[at * RANK : (at + 1) * RANK] = coef
    loads[8].wait()
    level1 = []
    for r in range(2):
        for c in range(2):
            total = None
            for dr in range(2):
                for dc in range(2):
                    leaf = (2 * r + dr) * SIDE + 2 * c + dc
                    part = dot(tree_ref[leaf], level0[leaf])
                    total = part if total is None else total + part
            coef = total.astype(BF)
            at = r * 2 + c
            level1.append(coef)
            coef_ref[(LEAVES + at) * RANK : (LEAVES + at + 1) * RANK] = coef
            for ref in (east_ref, west_ref, north_ref, south_ref):
                ref[(8 + at) * RANK : (9 + at) * RANK] = coef
    total = None
    for at in range(4):
        part = dot(tree_ref[LEAVES + at], level1[at])
        total = part if total is None else total + part
    give_ref[0:RANK] = total.astype(BF)
    top = tree_ref[TOP]
    give_ref[RANK:PACK] = jnp.concatenate([top[16 * k : 16 * k + 16] for k in range(4)], axis=1)
    for ref, leaves in (
        (west_ref, [r * 4 + c for r in range(4) for c in (0, 1)]),
        (east_ref, [r * 4 + c for r in range(4) for c in (2, 3)]),
        (north_ref, range(8)),
        (south_ref, range(8, 16)),
    ):
        rest = jnp.concatenate([pos_ref[leaf] for leaf in leaves], axis=0)
        for part in range(3):
            held = rest.astype(BF)
            at = 12 * RANK + 16 * part
            ref[at : at + 16] = held
            rest = rest - held.astype(F32)


def go_up(q, basis, tree, points):
    vmem = pl.BlockSpec(memory_space=pltpu.VMEM)
    side = jax.ShapeDtypeStruct((SIDEWAYS, LEAF), BF)
    return pl.pallas_call(
        up_body,
        out_shape=(
            side,
            side,
            side,
            side,
            jax.ShapeDtypeStruct(((LEAVES + 4) * RANK, LEAF), BF),
            jax.ShapeDtypeStruct((PACK, LEAF), BF),
        ),
        in_specs=[pl.BlockSpec(memory_space=pl.ANY)] * 3 + [vmem],
        out_specs=[vmem] * 6,
        scratch_shapes=[
            pltpu.VMEM((LEAVES, LEAF, LEAF), BF),
            pltpu.VMEM((LEAVES, RANK, LEAF), BF),
            pltpu.VMEM((TOP + 1, RANK, RANK), BF),
            pltpu.SemaphoreType.DMA((9,)),
        ],
        compiler_params=pltpu.CompilerParams(vmem_limit_bytes=BIG),
        cost_estimate=pl.CostEstimate(flops=300_000_000, bytes_accessed=5_000_000, transcendentals=0),
        name="upward",
    )(q, basis, tree, points)


def local_body(
    list_ref, coef_any, west_any, east_any, north_any, south_any, c0_any, c1_any, code_any, sum0, sum1, pad0, pad1, c0_ref, c1_ref, code_ref, sems
):
    loads = []

    def load(source, at, to, row, count):
        rows = pl.ds(at * RANK if at < 100 else at, count * RANK)
        copy = pltpu.make_async_copy(source.at[rows], to.at[pl.ds(row, count * RANK)], sems.at[len(loads)])
        copy.start()
        loads.append(copy)

    def put(pad, extent, row, col, ref, at, count):
        load(ref, at, pad, ((row + 2) * (extent + 4) + col + 2) * RANK, count)

    whole = []
    for k, (source, to) in enumerate(((c0_any, c0_ref), (c1_any, c1_ref), (code_any, code_ref))):
        whole.append(pltpu.make_async_copy(source, to, sems.at[COPIES + k]))
    whole[0].start()
    for r in range(4):
        put(pad0, 4, r, 0, coef_any, r * 4, 4)
        put(pad0, 4, r, -2, west_any, r * 2, 2)
        put(pad0, 4, r, 4, east_any, r * 2, 2)
    for ref, row in ((north_any, -2), (south_any, 4)):
        for r in range(2):
            put(pad0, 4, row + r, 0, ref, r * 4, 4)
            for col, base in ((-2, SIDEWAYS), (4, SIDEWAYS + CORNER)):
                load(ref, base + r * 2 * RANK, pad0, ((row + r + 2) * 8 + col + 2) * RANK, 2)
    split = len(loads)
    for copy in whole[1:]:
        copy.start()
    for r in range(2):
        put(pad1, 2, r, 0, coef_any, LEAVES + r * 2, 2)
        put(pad1, 2, r, -2, west_any, 8 + r * 2, 2)
        put(pad1, 2, r, 2, east_any, 8 + r * 2, 2)
    for ref, row in ((north_any, -2), (south_any, 2)):
        for r in range(2):
            put(pad1, 2, row + r, 0, ref, 8 + r * 2, 2)
            for col, base in ((-2, SIDEWAYS), (2, SIDEWAYS + CORNER)):
                load(ref, base + (4 + r * 2) * RANK, pad1, ((row + r + 2) * 6 + col + 2) * RANK, 2)
    whole[0].wait()
    for copy in loads[:split]:
        copy.wait()
    for a in range(2):
        for b in range(2):
            total = None
            for wy in range(6):
                at = ((2 * a + wy) * 8 + 2 * b) * RANK
                part = dot(c0_ref[:, wy * 6 * RANK : (wy + 1) * 6 * RANK], pad0[at : at + 6 * RANK])
                total = part if total is None else total + part
            for child in range(4):
                leaf = (2 * a + child // 2) * SIDE + 2 * b + child % 2
                sum0[leaf] = total[child * RANK : (child + 1) * RANK]
    for copy in loads[split:] + whole[1:]:
        copy.wait()

    def listed(leaf, carry):
        code = second_cycle(list_ref, leaf)

        @pl.when(code >= 0)
        def _():
            row = leaf // SIDE + code // 5
            col = leaf % SIDE + code % 5
            at = pl.multiple_of((row * 8 + col) * RANK, RANK)
            sum0[leaf] = sum0[leaf] - dot(code_ref[code], pad0[pl.ds(at, RANK)])

        return carry

    lax.fori_loop(0, LEAVES, listed, 0)
    sum1[...] = dot(c1_ref[...], pad1[...])


def local_far(near_list, coefs, west, east, north, south):
    vmem = pl.BlockSpec(memory_space=pltpu.VMEM)
    smem = pl.BlockSpec(memory_space=pltpu.SMEM)
    return pl.pallas_call(
        local_body,
        out_shape=(
            jax.ShapeDtypeStruct((LEAVES, RANK, LEAF), F32),
            jax.ShapeDtypeStruct((4 * RANK, LEAF), F32),
        ),
        in_specs=[smem] + [pl.BlockSpec(memory_space=pl.ANY)] * 8,
        out_specs=[vmem] * 2,
        scratch_shapes=[
            pltpu.VMEM((64 * RANK, LEAF), BF),
            pltpu.VMEM((WINDOW * RANK, LEAF), BF),
            pltpu.VMEM((4 * RANK, WINDOW * RANK), BF),
            pltpu.VMEM((4 * RANK, WINDOW * RANK), BF),
            pltpu.VMEM((25, RANK, RANK), BF),
            pltpu.SemaphoreType.DMA((COPIES + 3,)),
        ],
        compiler_params=pltpu.CompilerParams(vmem_limit_bytes=BIG),
        cost_estimate=pl.CostEstimate(flops=5_000_000_000, bytes_accessed=8_000_000, transcendentals=0),
        name="local_far",
    )(
        near_list,
        coefs,
        west,
        east,
        north,
        south,
        jnp.asarray(window_coupling(0)),
        jnp.asarray(window_coupling(1)),
        jnp.asarray(code_coupling()),
    )


def top_body(
    meta_ref, all_any, c2_any, c3_any, tree_any, sum0_any, sum1_any, field_ref, win, parents, c2_ref, c3_ref, all_ref, tree_ref, sum0, sum1, sems
):
    loads = []
    for k, (source, to) in enumerate(((all_any, all_ref), (tree_any, tree_ref), (sum1_any, sum1), (sum0_any, sum0))):
        loads.append(pltpu.make_async_copy(source, to, sems.at[2 + k]))
        loads[-1].start()

    def slab(source, to, at):
        part = pl.ds(pl.multiple_of(meta_ref[2 * WINDOW + at] * RANK, RANK), RANK)
        copy = pltpu.make_async_copy(source.at[part], to, sems.at[at])
        copy.start()
        return copy

    slabs = [slab(c2_any, c2_ref, 0), slab(c3_any, c3_ref, 1)]

    loads[0].wait()

    def lift(group, carry):
        total = jnp.zeros((RANK, LEAF), F32)
        for child in range(4):
            at = pl.multiple_of((group * 4 + child) * PACK, 16)
            packed = all_ref[pl.ds(at + RANK, 16)]
            matrix = jnp.concatenate([packed[:, k * RANK : (k + 1) * RANK] for k in range(4)], axis=0)
            total = total + dot(matrix, all_ref[pl.ds(at, RANK)])
        parents[pl.ds(pl.multiple_of(group * RANK, RANK), RANK)] = total.astype(BF)
        return carry

    lax.fori_loop(0, parents.shape[0] // RANK, lift, 0)

    def fill(start, source, stride):
        for i in range(WINDOW):
            slot = meta_ref[start + i]
            at = pl.multiple_of(jnp.maximum(slot, 0) * stride, 16)
            kept = jnp.where(slot >= 0, 1.0, 0.0).astype(BF)
            win[i * RANK : (i + 1) * RANK] = source[pl.ds(at, RANK)] * kept

    fill(WINDOW, parents, RANK)
    slabs[1].wait()
    field3 = dot(c3_ref[...], win[...]).astype(BF)
    fill(0, all_ref, PACK)
    slabs[0].wait()
    for load in loads[1:]:
        load.wait()
    field2 = (dot(c2_ref[...], win[...]) + dot_first(tree_ref[TOP], field3)).astype(BF)
    field1 = []
    for at in range(4):
        field1.append(
            (sum1[at * RANK : (at + 1) * RANK] + dot_first(tree_ref[LEAVES + at], field2)).astype(BF)
        )
    for leaf in range(LEAVES):
        above = field1[leaf // SIDE // 2 * 2 + leaf % SIDE // 2]
        field_ref[leaf] = (sum0[leaf] + dot_first(tree_ref[leaf], above)).astype(BF)


def second_cycle(list_ref, leaf):
    found = jnp.int32(-1)
    for j in range(NEAR):
        code = list_ref[leaf * NEAR + j]
        y, x = code // 5, code % 5
        outer = (code >= 0) & ((y == 0) | (y == 4) | (x == 0) | (x == 4))
        found = jnp.where(outer, code, found)
    return found


def top_far(meta, gathered, tree, sum0, sum1):
    vmem = pl.BlockSpec(memory_space=pltpu.VMEM)
    smem = pl.BlockSpec(memory_space=pltpu.SMEM)
    anywhere = pl.BlockSpec(memory_space=pl.ANY)
    devices = gathered.shape[0] // PACK
    return pl.pallas_call(
        top_body,
        out_shape=jax.ShapeDtypeStruct((LEAVES, RANK, LEAF), BF),
        in_specs=[smem] + [anywhere] * 6,
        out_specs=vmem,
        scratch_shapes=[
            pltpu.VMEM((WINDOW * RANK, LEAF), BF),
            pltpu.VMEM((devices // 4 * RANK, LEAF), BF),
            pltpu.VMEM((RANK, WINDOW * RANK), BF),
            pltpu.VMEM((RANK, WINDOW * RANK), BF),
            pltpu.VMEM(gathered.shape, BF),
            pltpu.VMEM((TOP + 1, RANK, RANK), BF),
            pltpu.VMEM((LEAVES, RANK, LEAF), F32),
            pltpu.VMEM((4 * RANK, LEAF), F32),
            pltpu.SemaphoreType.DMA((6,)),
        ],
        compiler_params=pltpu.CompilerParams(vmem_limit_bytes=BIG),
        cost_estimate=pl.CostEstimate(flops=3_000_000_000, bytes_accessed=5_000_000, transcendentals=0),
        name="top_far",
    )(meta, gathered, jnp.asarray(window_coupling(2)), jnp.asarray(window_coupling(3)), tree, sum0, sum1)


def join_body(north_ref, south_ref, west_ref, east_ref, north_any, south_any, to_north, to_south, sems):
    copies = []

    def move(source, at, to, row, count):
        copy = pltpu.make_async_copy(source.at[pl.ds(at, count)], to.at[pl.ds(row, count)], sems.at[len(copies)])
        copy.start()
        copies.append(copy)

    for own, to, lower in ((north_ref, to_north, 0), (south_ref, to_south, 1)):
        move(own, 0, to, 0, SIDEWAYS)
        for side, base in ((west_ref, SIDEWAYS), (east_ref, SIDEWAYS + CORNER)):
            move(side, 4 * RANK * lower, to, base, 4 * RANK)
            move(side, 8 * RANK, to, base + 4 * RANK, CORNER - 4 * RANK)
    backs = []
    for k, (held, to) in enumerate(((to_north, north_any), (to_south, south_any))):
        for copy in copies[5 * k : 5 * k + 5]:
            copy.wait()
        backs.append(pltpu.make_async_copy(held, to, sems.at[10 + k]))
        backs[-1].start()
    for back in backs:
        back.wait()


def join(north, south, west, east):
    anywhere = pl.BlockSpec(memory_space=pl.ANY)
    message = jax.ShapeDtypeStruct((SIDEWAYS + 2 * CORNER, LEAF), BF)
    return pl.pallas_call(
        join_body,
        out_shape=(message, message),
        in_specs=[anywhere] * 4,
        out_specs=[anywhere] * 2,
        scratch_shapes=[pltpu.VMEM(message.shape, BF)] * 2 + [pltpu.SemaphoreType.DMA((12,))],
        compiler_params=pltpu.CompilerParams(vmem_limit_bytes=BIG),
        cost_estimate=pl.CostEstimate(flops=0, bytes_accessed=4_000_000, transcendentals=0),
        name="join",
    )(north, south, west, east)


def kernel_of(target_x, target_y, source_x, source_y):
    gap_x = target_x - source_x
    gap_y = target_y - source_y
    squared = jnp.maximum(gap_x * gap_x + gap_y * gap_y, 1e-12)
    length = squared * lax.rsqrt(squared)
    phase = length - ((length + rounder) - rounder)
    w = 0.25 - jnp.abs(phase)
    s = w * w
    wave = w * (SINE[0] + s * (SINE[1] + s * SINE[2]))
    return (jnp.exp2(squared * short_rate) + jnp.exp2(squared * long_rate) * wave).astype(BF)


def spread_columns(rows, columns):
    turned = rows.T
    for k in range(columns.shape[1] // 128):
        columns[:, 128 * k : 128 * (k + 1)] = jnp.broadcast_to(turned[:, k : k + 1], (LEAF, 128))


def block_into(to, columns, points, shift_y, shift_x):
    source_x = (points[0:1] + shift_x.astype(F32)) * waves
    source_y = (points[1:2] + shift_y.astype(F32)) * waves
    rows = 32
    for i in range(0, LEAF, rows):
        for j in (0, 128):
            to[i : i + rows, j : j + 128] = kernel_of(
                columns[i : i + rows, 0:128],
                columns[i : i + rows, 128:256],
                jnp.broadcast_to(source_x[:, j : j + 128], (rows, 128)),
                jnp.broadcast_to(source_y[:, j : j + 128], (rows, 128)),
            )


def turn_points(columns, leaf, position, noise):
    rows = jnp.concatenate([position * waves, noise, jnp.zeros((5, LEAF), F32)], axis=0)
    spread_columns(rows, columns.at[leaf])


def own_pairs(first, last):
    pairs = []
    for r in range(first, last):
        for c in range(SIDE):
            for dy, dx in ((0, 1), (1, -1), (1, 0), (1, 1)):
                if r + dy < SIDE and 0 <= c + dx < SIDE:
                    pairs.append((r * SIDE + c, (r + dy) * SIDE + c + dx, dy, dx))
    return pairs


def near_own_body(first, last, table_ref, q_any, pos_ref, noise_ref, *refs):
    before_any, out_any, columns, blocks, q_ref, before_ref, out_ref, sems = (None,) * (8 - len(refs)) + refs
    loads = [pltpu.make_async_copy(q_any, q_ref, sems.at[0])]
    if first:
        loads.append(pltpu.make_async_copy(before_any.at[pl.ds(SIDE, SIDE)], before_ref, sems.at[1]))
    for load in loads:
        load.start()
    pairs = own_pairs(first, last)
    start = first * SIDE
    count = (last - first) * SIDE

    def turn(leaf, carry):
        turn_points(columns, leaf, pos_ref[leaf], noise_ref[leaf])
        return carry

    lax.fori_loop(start, start + count, turn, 0)
    zero = jnp.int32(0)

    def selves(i, carry):
        for half in range(2):
            leaf = start + 2 * i + half
            block_into(blocks.at[2 * i + half], columns.at[leaf], pos_ref[leaf], zero, zero)
        return carry

    lax.fori_loop(0, count // 2, selves, 0)

    def pair(i):
        at = 4 * i
        place = count + 2 * i
        target, source = table_ref[at], table_ref[at + 1]
        block_into(blocks.at[place], columns.at[target], pos_ref[source], table_ref[at + 2], table_ref[at + 3])
        blocks[place + 1] = blocks[place].T

    def both(i, carry):
        pair(2 * i)
        pair(2 * i + 1)
        return carry

    lax.fori_loop(0, len(pairs) // 2, both, 0)
    if len(pairs) % 2:
        pair(len(pairs) - 1)
    for load in loads:
        load.wait()
    parts = {leaf: [(leaf - start, leaf)] for leaf in range(start, start + count)}
    for i, (target, source, _, _) in enumerate(pairs):
        parts[target].append((count + 2 * i, source))
        parts.setdefault(source, []).append((count + 1 + 2 * i, target))
    backs = []
    for leaf, terms in sorted(parts.items()):
        total = None
        for place, source in terms:
            part = dot(blocks[place], q_ref[source])
            total = part if total is None else total + part
        if leaf < start + count:
            noise = jnp.concatenate([columns[leaf, :, 256:384]] * 2, axis=1)
            total = total + noise * q_ref[leaf].astype(F32)
        if first and leaf < start + SIDE:
            total = total + before_ref[leaf - start]
        out_ref[leaf - start] = total
        backs.append(pltpu.make_async_copy(out_ref.at[leaf - start], out_any.at[leaf - start], sems.at[2 + leaf - start]))
        backs[-1].start()
    for back in backs:
        back.wait()


def near_own(first, last, q, points, noise, after, before):
    vmem = pl.BlockSpec(memory_space=pltpu.VMEM)
    smem = pl.BlockSpec(memory_space=pltpu.SMEM)
    anywhere = pl.BlockSpec(memory_space=pl.ANY)
    pairs = own_pairs(first, last)
    leaves = (min(last + 1, SIDE) - first) * SIDE

    def body(after_ref, *refs):
        near_own_body(first, last, *refs)

    return pl.pallas_call(
        body,
        out_shape=jax.ShapeDtypeStruct((leaves, LEAF, LEAF), F32),
        in_specs=[anywhere, smem, anywhere, vmem, vmem] + [anywhere] * len(before),
        out_specs=anywhere,
        scratch_shapes=[
            pltpu.VMEM((LEAVES, LEAF, 384), F32),
            pltpu.VMEM(((last - first) * SIDE + 2 * len(pairs), LEAF, LEAF), BF),
            pltpu.VMEM((LEAVES, LEAF, LEAF), BF),
            pltpu.VMEM((SIDE, LEAF, LEAF), F32),
            pltpu.VMEM((leaves, LEAF, LEAF), F32),
            pltpu.SemaphoreType.DMA((2 + leaves,)),
        ],
        compiler_params=pltpu.CompilerParams(vmem_limit_bytes=BIG),
        cost_estimate=pl.CostEstimate(flops=6_000_000_000, bytes_accessed=4_000_000, transcendentals=8_000_000),
        name="near_own",
    )(after, jnp.asarray(np.array(pairs, np.int32).reshape(-1)), q, points, noise, *before)


def edge_items():
    table = near_table(False)
    return [[leaf, *table[leaf, j]] for leaf in range(LEAVES) for j in range(5) if table[leaf, j, 0] >= 0]


ITEMS = edge_items()
EDGES = len(ITEMS)


def extra_of(list_ref, slot_ref, leaf):
    code = second_cycle(list_ref, leaf)
    place = (leaf // SIDE + code // 5) * 8 + leaf % SIDE + code % 5
    slot = slot_ref[jnp.where(code >= 0, place, 0)]
    return code, slot


def edge_body(
    half_at, list_ref, table_ref, slot_ref, after_ref, own_pos_ref, west_any, east_any, north_any, south_any, out_any,
    columns, parts, points, out_ref, sems,
):
    start = 8 * half_at
    copies = []
    sources = (
        (west_any, 12 * RANK),
        (east_any, 12 * RANK),
        (north_any, 12 * RANK),
        (north_any, SIDEWAYS + 8 * RANK),
        (north_any, SIDEWAYS + CORNER + 8 * RANK),
        (south_any, 12 * RANK),
        (south_any, SIDEWAYS + 8 * RANK),
        (south_any, SIDEWAYS + CORNER + 8 * RANK),
    )
    for k, (source, at) in enumerate(sources):
        copies.append(pltpu.make_async_copy(source.at[pl.ds(at, 48)], parts.at[k], sems.at[k]))
    for copy in copies:
        copy.start()

    def turn(leaf, carry):
        turn_points(columns, leaf, own_pos_ref[leaf], jnp.zeros((1, LEAF), F32))
        return carry

    lax.fori_loop(start, start + 8, turn, 0)
    points[0:LEAVES] = own_pos_ref[...]
    for copy in copies:
        copy.wait()
    slots = (16, 24, 32, 40, 44, 48, 56, 60)
    for k in range(8):
        whole = parts[k].astype(F32)
        whole = (whole[0:16] + whole[16:32]) + whole[32:48]
        first, count = {3: (4, 4), 4: (4, 4), 6: (0, 4), 7: (0, 4)}.get(k, (0, 8))
        for i in range(count):
            points[slots[k] + i] = whole[2 * (first + i) : 2 * (first + i) + 2]

    def fixed(i, carry):
        for half in range(2):
            at = 8 * i + 4 * half
            block_into(
                out_ref.at[2 * i + half],
                columns.at[table_ref[at]],
                points[table_ref[at + 1]],
                table_ref[at + 2],
                table_ref[at + 3],
            )
        return carry

    lax.fori_loop(0, EDGES // 4, fixed, 0)
    backs = []
    for k, part in enumerate((pl.ds(0, EDGES // 2), pl.ds(EDGES // 2, 8))):
        backs.append(pltpu.make_async_copy(out_ref.at[part], out_any.at[part], sems.at[8 + k]))
    backs[0].start()

    def extra(i, carry):
        for half in range(2):
            leaf = start + 2 * i + half
            code, slot = extra_of(list_ref, slot_ref, leaf)
            code = jnp.maximum(code, 0)
            block_into(out_ref.at[EDGES // 2 + 2 * i + half], columns.at[leaf], points[slot], code // 5 - 2, code % 5 - 2)
        return carry

    lax.fori_loop(0, 4, extra, 0)
    backs[1].start()
    for back in backs:
        back.wait()


def edge_blocks(half_at, near_list, after, own_points, west, east, north, south):
    vmem = pl.BlockSpec(memory_space=pltpu.VMEM)
    smem = pl.BlockSpec(memory_space=pltpu.SMEM)
    anywhere = pl.BlockSpec(memory_space=pl.ANY)
    items = [item for item in ITEMS if item[0] // 8 == half_at]
    assert len(items) * 2 == EDGES

    def body(*refs):
        edge_body(half_at, *refs)

    return pl.pallas_call(
        body,
        out_shape=jax.ShapeDtypeStruct((EDGES // 2 + 8, LEAF, LEAF), BF),
        in_specs=[smem, smem, smem, anywhere, vmem] + [anywhere] * 4,
        out_specs=anywhere,
        scratch_shapes=[
            pltpu.VMEM((LEAVES, LEAF, 384), F32),
            pltpu.VMEM((8, 48, LEAF), BF),
            pltpu.VMEM((64, 2, LEAF), F32),
            pltpu.VMEM((EDGES // 2 + 8, LEAF, LEAF), BF),
            pltpu.SemaphoreType.DMA((10,)),
        ],
        compiler_params=pltpu.CompilerParams(vmem_limit_bytes=BIG),
        cost_estimate=pl.CostEstimate(flops=6_000_000_000, bytes_accessed=8_000_000, transcendentals=12_000_000),
        name="edge_blocks",
    )(
        near_list, jnp.asarray(np.array(items, np.int32).reshape(-1)), jnp.asarray(SLOT_OF), after, own_points,
        west, east, north, south,
    )


def final_body(
    list_ref, slot_ref, q_any, west_any, east_any, north_any, north_corner_any, south_any, south_corner_any,
    upper_blocks_any, lower_blocks_any, row0_any, row1_any, row2_any, basis_ref, field_ref, out_any, held, blocks, sums, outs, sems,
):
    firsts = [min(at for at in range(EDGES) if ITEMS[at][0] // SIDE == r) for r in range(SIDE)] + [EDGES]
    stages = [[], [], [], []]
    count = 0

    def copy(stage, source, to):
        nonlocal count
        made = pltpu.make_async_copy(source, to, sems.at[count])
        count += 1
        stages[stage].append(made)

    for r in range(SIDE):
        if r == 0:
            for source, at in ((north_any, 32), (north_corner_any, 40)):
                copy(r, source, held.at[pl.ds(at, 8)])
        for source, at in ((west_any, 16), (east_any, 24)):
            for low, high in {0: ((0, 4),), 1: ((4, 6),), 2: ((6, 8),)}.get(r, ()):
                copy(r, source.at[pl.ds(low, high - low)], held.at[pl.ds(at + low, high - low)])
        if r == SIDE - 1:
            for source, at in ((south_any, 48), (south_corner_any, 56)):
                copy(r, source, held.at[pl.ds(at, 8)])
        part = pl.ds(firsts[r], firsts[r + 1] - firsts[r])
        source, back = (upper_blocks_any, 0) if r < 2 else (lower_blocks_any, EDGES // 2)
        copy(r, source.at[pl.ds(firsts[r] - back, firsts[r + 1] - firsts[r])], blocks.at[part])
        source = (row0_any, row1_any, row2_any, row2_any)[r].at[pl.ds(SIDE if r == 3 else 0, SIDE)]
        copy(r, source, sums.at[pl.ds(SIDE * r, SIDE)])
    copy(SIDE - 1, q_any, held.at[pl.ds(0, 16)])
    for half_at, source in enumerate((upper_blocks_any, lower_blocks_any)):
        copy(SIDE - 1, source.at[pl.ds(EDGES // 2, 8)], blocks.at[pl.ds(EDGES + 8 * half_at, 8)])
    for r in range(2):
        for made in stages[r]:
            made.start()
    for leaf in range(LEAVES):
        if leaf % SIDE == 0:
            for made in stages[leaf // SIDE]:
                made.wait()
            if leaf // SIDE + 2 < SIDE:
                for made in stages[leaf // SIDE + 2]:
                    made.start()
        total = dot_first(basis_ref[leaf], field_ref[leaf])
        for at in range(EDGES):
            if ITEMS[at][0] == leaf:
                total = total + dot(blocks[at], held[ITEMS[at][1]])
        sums[leaf] += total

    backs = []
    for r in range(SIDE):
        part = pl.ds(SIDE * r, SIDE)
        backs.append(pltpu.make_async_copy(outs.at[part], out_any.at[part], sems.at[count + r]))

    for r in range(SIDE):

        def finish(leaf, carry):
            code, slot = extra_of(list_ref, slot_ref, leaf)

            @pl.when(code >= 0)
            def _():
                outs[leaf] = (sums[leaf] + dot(blocks[EDGES + leaf], held[slot])).astype(BF)

            @pl.when(code < 0)
            def _():
                outs[leaf] = sums[leaf].astype(BF)

            return carry

        lax.fori_loop(SIDE * r, SIDE * (r + 1), finish, 0)
        backs[r].start()
    for back in backs:
        back.wait()


def finish(near_list, q, halos, upper_blocks, lower_blocks, sums, basis, field):
    vmem = pl.BlockSpec(memory_space=pltpu.VMEM)
    smem = pl.BlockSpec(memory_space=pltpu.SMEM)
    anywhere = pl.BlockSpec(memory_space=pl.ANY)

    return pl.pallas_call(
        final_body,
        out_shape=jax.ShapeDtypeStruct((LEAVES, LEAF, LEAF), BF),
        in_specs=[smem, smem] + [anywhere] * 12 + [vmem, vmem],
        out_specs=anywhere,
        scratch_shapes=[
            pltpu.VMEM((64, LEAF, LEAF), BF),
            pltpu.VMEM((EDGES + LEAVES, LEAF, LEAF), BF),
            pltpu.VMEM((LEAVES, LEAF, LEAF), F32),
            pltpu.VMEM((LEAVES, LEAF, LEAF), BF),
            pltpu.SemaphoreType.DMA((26,)),
        ],
        compiler_params=pltpu.CompilerParams(vmem_limit_bytes=BIG),
        cost_estimate=pl.CostEstimate(flops=4_000_000_000, bytes_accessed=24_000_000, transcendentals=0),
        name="finish",
    )(near_list, jnp.asarray(SLOT_OF), q, *halos, upper_blocks, lower_blocks, *sums, basis, field)


def window_slots(wide, narrow, steps):
    row, col = lax.axis_index("narrow"), lax.axis_index("wide")
    wy, wx = np.arange(WINDOW) // 6, np.arange(WINDOW) % 6

    def slots(target_y, target_x, scale):
        y = target_y // 2 * 2 - 2 + wy
        x = target_x // 2 * 2 - 2 + wx
        inside = (y >= 0) & (y < narrow // scale) & (x >= 0) & (x < wide // scale)
        apart = {"narrow": (y * scale) ^ row, "wide": (x * scale) ^ col}
        slot = 0
        for at, (axis, bit) in enumerate(steps):
            slot = slot + (apart[axis] // bit & 1) * (1 << at)
        return jnp.where(inside, slot if scale == 1 else slot // 4, -1)

    parity2 = row % 2 * 2 + col % 2
    parity3 = row // 2 % 2 * 2 + col // 2 % 2
    return jnp.concatenate(
        [slots(row, col, 1), slots(row // 2, col // 2, 2), jnp.stack([parity2, parity3])]
    ).astype(jnp.int32)


def per_device(wide, narrow, charges, positions, noise, leaf_basis, transfer, near_list):
    q = charges.reshape(LEAVES, LEAF, LEAF)
    points = positions.reshape(LEAVES, 2, LEAF)
    basis = leaf_basis.reshape(LEAVES, RANK, LEAF)
    tree = transfer[0, 0]
    listing = near_list.reshape(-1)
    steps = gather_steps(wide, narrow)
    meta = window_slots(wide, narrow, steps)

    east, west, north, south, coefs, give = go_up(q, basis, tree, points)
    from_west = shift(east, "wide", 1)
    from_east = shift(west, "wide", -1)
    q_north = shift(charges[2:4], "narrow", 1)
    q_south = shift(charges[0:2], "narrow", -1)

    noise_rows = noise.reshape(LEAVES, 1, LEAF)

    def step(value, at):
        axis, bit = steps[at]
        return lax.ppermute(value, axis, [(i, i ^ bit) for i in range(lax.axis_size(axis))])

    def tie(*values):
        return lax.optimization_barrier(values)

    gathered = give
    other = step(gathered, 0)
    row0 = near_own(0, 1, q, points, noise_rows, give, [])
    other, row0 = tie(other, row0)
    gathered = jnp.concatenate([gathered, other], axis=0)
    other = step(gathered, 1)
    row1 = near_own(1, 2, q, points, noise_rows, gathered, [row0])
    to_east, to_west = charges[:, 2:4], charges[:, 0:2]
    other, from_west, from_east, row1, to_east, to_west, q_north, q_south = tie(
        other, from_west, from_east, row1, to_east, to_west, q_north, q_south
    )
    gathered = jnp.concatenate([gathered, other], axis=0)
    other = step(gathered, 2)
    to_north, to_south = join(north, south, from_west, from_east)
    from_south = shift(to_north, "narrow", -1)
    from_north = shift(to_south, "narrow", 1)
    q_west = shift(to_east, "wide", 1)
    q_east = shift(to_west, "wide", -1)
    row2 = near_own(2, 4, q, points, noise_rows, to_north, [row1])
    other, from_south, from_north, row2 = tie(other, from_south, from_north, row2)
    gathered = jnp.concatenate([gathered, other], axis=0)
    other = step(gathered, 3)
    sums = local_far(listing, coefs, from_west, from_east, from_north, from_south)
    upper_blocks = edge_blocks(0, listing, sums[1], points, from_west, from_east, from_north, from_south)
    other, upper_blocks = tie(other, upper_blocks)
    for at in range(4, len(steps)):
        gathered = jnp.concatenate([gathered, other], axis=0)
        other = step(gathered, at)
        if at == 4:
            lower_blocks = edge_blocks(1, listing, upper_blocks, points, from_west, from_east, from_north, from_south)
            other, lower_blocks, q_west, q_east = tie(other, lower_blocks, q_west, q_east)
            q_north_corner = shift(jnp.stack([q_west[2:4], q_east[2:4]]), "narrow", 1)
            q_south_corner = shift(jnp.stack([q_west[0:2], q_east[0:2]]), "narrow", -1)
    gathered = jnp.concatenate([gathered, other], axis=0)
    field = top_far(meta, gathered, tree, *sums)
    q_north_corner, q_south_corner, field = tie(q_north_corner, q_south_corner, field)
    halos = [
        value.reshape(8, LEAF, LEAF)
        for value in (q_west, q_east, q_north, q_north_corner, q_south, q_south_corner)
    ]
    out = finish(listing, q, halos, upper_blocks, lower_blocks, (row0, row1, row2), basis, field)
    return out.reshape(SIDE, SIDE, LEAF, LEAF)


def solution(mesh):
    wide, narrow = mesh.shape["wide"], mesh.shape["narrow"]
    in_specs = (
        P("narrow", "wide", None, None),
        P("narrow", "wide", None, None),
        P("narrow", "wide", None),
        P("narrow", "wide", None, None),
        P("narrow", "wide", None, None, None),
        P("narrow", "wide", None),
    )
    out_specs = P("narrow", "wide", None, None)

    def step(*arrays):
        return per_device(wide, narrow, *arrays)

    return jax.shard_map(step, mesh=mesh, in_specs=in_specs, out_specs=out_specs, check_vma=False)
```

```python
import math

import jax
import jax.numpy as jnp
import ml_dtypes
import numpy as np
from jax import lax
from jax.experimental import pallas as pl
from jax.experimental.pallas import tpu as pltpu
from jax.sharding import PartitionSpec as P

LEAF = 256
CHEB = 8
RANK = 64
NEAR = 10
SIDE = 4
LEAVES = SIDE * SIDE
TOP = 20
WINDOW = 36
PACK = RANK + 16
SIDEWAYS = 8 * RANK + 4 * RANK + 48
CORNER = 4 * RANK + 4 * RANK + 48
BIG = 58 << 20
COPIES = 42
BF = jnp.bfloat16
F32 = jnp.float32

short_len = 0.125
long_weight = 0.03125
reach = 3.0 * SIDE
waves = 10.0
LOG2E = math.log2(math.e)
long_rate = -0.5 / (reach * reach) * LOG2E / (waves * waves)
short_rate = -0.5 / (short_len * short_len) * LOG2E / (waves * waves)
rounder = 1.5 * 2.0**23


def sine_terms(count):
    w = np.cos(np.pi * (np.arange(2000) + 0.5) / 2000) * 0.25
    powers = np.stack([w ** (2 * i + 1) for i in range(count)], 1)
    return [float(c) for c in np.linalg.lstsq(powers, np.sin(2 * np.pi * w) * long_weight, rcond=None)[0]]


SINE = sine_terms(3)


def coupling(height, shift_y, shift_x):
    points = 0.5 * (1.0 + np.cos((2.0 * np.arange(CHEB) + 1.0) * (math.pi / (2.0 * CHEB))))
    node_x = np.tile(points, CHEB)
    node_y = np.repeat(points, CHEB)
    gap_x = (node_x[:, None] - node_x[None, :] - shift_x) * 2.0**height
    gap_y = (node_y[:, None] - node_y[None, :] - shift_y) * 2.0**height
    squared = gap_x * gap_x + gap_y * gap_y
    return np.exp(squared * (-0.5 / (short_len * short_len))) + long_weight * np.exp(
        squared * (-0.5 / (reach * reach))
    ) * np.cos(2.0 * math.pi * waves * np.sqrt(squared))


def window_coupling(height):
    table = np.zeros((2, 2, RANK, 6, 6, RANK))
    for py in range(2):
        for px in range(2):
            for wy in range(6):
                for wx in range(6):
                    shift_y, shift_x = wy - 2 - py, wx - 2 - px
                    if max(abs(shift_y), abs(shift_x)) >= 2:
                        table[py, px, :, wy, wx] = coupling(height, shift_y, shift_x)
    return table.reshape(4 * RANK, WINDOW * RANK).astype(ml_dtypes.bfloat16)


def code_coupling():
    return np.stack([coupling(0, code // 5 - 2, code % 5 - 2) for code in range(25)]).astype(ml_dtypes.bfloat16)


def halo_slot(row, col):
    if 0 <= row < 4 and 0 <= col < 4:
        return row * 4 + col
    if 0 <= row < 4:
        return 16 + row * 2 + col + 2 if col < 0 else 24 + row * 2 + col - 4
    base, r = (32, row + 2) if row < 0 else (48, row - 4)
    if 0 <= col < 4:
        return base + r * 4 + col
    return base + 8 + r * 2 + col + 2 if col < 0 else base + 12 + r * 2 + col - 4


SLOT_OF = np.array([halo_slot(r - 2, c - 2) for r in range(8) for c in range(8)], np.int32)


def near_table(own):
    width = 9 if own else 5
    table = np.zeros((LEAVES, width, 3), np.int32)
    table[:, :, 0] = -1
    for r in range(SIDE):
        for c in range(SIDE):
            at = 0
            for dy in (-1, 0, 1):
                for dx in (-1, 0, 1):
                    slot = halo_slot(r + dy, c + dx)
                    if (slot < LEAVES) == own:
                        table[r * SIDE + c, at] = (slot, dy, dx)
                        at += 1
    return table


def bits(count):
    return [1 << i for i in range(count.bit_length() - 1)]


def gather_steps(wide, narrow):
    return (
        [("wide", 1), ("narrow", 1)]
        + [("wide", b) for b in reversed(bits(wide)[1:])]
        + [("narrow", b) for b in reversed(bits(narrow)[1:])]
    )


def shift(value, axis, steps):
    count = lax.axis_size(axis)
    return lax.ppermute(value, axis, [(i, i + steps) for i in range(count) if 0 <= i + steps < count])


def dot(a, b):
    return jnp.dot(a, b, preferred_element_type=F32)


def dot_first(a, b):
    return lax.dot_general(a, b, (((0,), (0,)), ((), ())), preferred_element_type=F32)


def up_body(
    q_any, basis_any, tree_any, pos_ref, east_ref, west_ref, north_ref, south_ref, coef_ref, give_ref, q_ref, basis_ref, tree_ref, sems
):
    loads = []
    for k in range(4):
        part = pl.ds(4 * k, 4)
        loads.append(pltpu.make_async_copy(basis_any.at[part], basis_ref.at[part], sems.at[2 * k]))
        loads.append(pltpu.make_async_copy(q_any.at[part], q_ref.at[part], sems.at[2 * k + 1]))
    loads.append(pltpu.make_async_copy(tree_any, tree_ref, sems.at[8]))
    for load in loads:
        load.start()
    level0 = []
    for leaf in range(LEAVES):
        if leaf % 4 == 0:
            loads[leaf // 2].wait()
            loads[leaf // 2 + 1].wait()
        coef = dot(basis_ref[leaf], q_ref[leaf]).astype(BF)
        level0.append(coef)
        r, c = leaf // SIDE, leaf % SIDE
        coef_ref[leaf * RANK : (leaf + 1) * RANK] = coef
        ref, at = (west_ref, r * 2 + c) if c < 2 else (east_ref, r * 2 + c - 2)
        ref[at * RANK : (at + 1) * RANK] = coef
        ref, at = (north_ref, r * 4 + c) if r < 2 else (south_ref, r * 4 + c - 8)
        ref[at * RANK : (at + 1) * RANK] = coef
    loads[8].wait()
    level1 = []
    for r in range(2):
        for c in range(2):
            total = None
            for dr in range(2):
                for dc in range(2):
                    leaf = (2 * r + dr) * SIDE + 2 * c + dc
                    part = dot(tree_ref[leaf], level0[leaf])
                    total = part if total is None else total + part
            coef = total.astype(BF)
            at = r * 2 + c
            level1.append(coef)
            coef_ref[(LEAVES + at) * RANK : (LEAVES + at + 1) * RANK] = coef
            for ref in (east_ref, west_ref, north_ref, south_ref):
                ref[(8 + at) * RANK : (9 + at) * RANK] = coef
    total = None
    for at in range(4):
        part = dot(tree_ref[LEAVES + at], level1[at])
        total = part if total is None else total + part
    give_ref[0:RANK] = total.astype(BF)
    top = tree_ref[TOP]
    give_ref[RANK:PACK] = jnp.concatenate([top[16 * k : 16 * k + 16] for k in range(4)], axis=1)
    for ref, leaves in (
        (west_ref, [r * 4 + c for r in range(4) for c in (0, 1)]),
        (east_ref, [r * 4 + c for r in range(4) for c in (2, 3)]),
        (north_ref, range(8)),
        (south_ref, range(8, 16)),
    ):
        rest = jnp.concatenate([pos_ref[leaf] for leaf in leaves], axis=0)
        for part in range(3):
            held = rest.astype(BF)
            at = 12 * RANK + 16 * part
            ref[at : at + 16] = held
            rest = rest - held.astype(F32)


def go_up(q, basis, tree, points):
    vmem = pl.BlockSpec(memory_space=pltpu.VMEM)
    side = jax.ShapeDtypeStruct((SIDEWAYS, LEAF), BF)
    return pl.pallas_call(
        up_body,
        out_shape=(
            side,
            side,
            side,
            side,
            jax.ShapeDtypeStruct(((LEAVES + 4) * RANK, LEAF), BF),
            jax.ShapeDtypeStruct((PACK, LEAF), BF),
        ),
        in_specs=[pl.BlockSpec(memory_space=pl.ANY)] * 3 + [vmem],
        out_specs=[vmem] * 6,
        scratch_shapes=[
            pltpu.VMEM((LEAVES, LEAF, LEAF), BF),
            pltpu.VMEM((LEAVES, RANK, LEAF), BF),
            pltpu.VMEM((TOP + 1, RANK, RANK), BF),
            pltpu.SemaphoreType.DMA((9,)),
        ],
        compiler_params=pltpu.CompilerParams(vmem_limit_bytes=BIG),
        cost_estimate=pl.CostEstimate(flops=300_000_000, bytes_accessed=5_000_000, transcendentals=0),
        name="upward",
    )(q, basis, tree, points)


def local_body(
    list_ref, coef_any, west_any, east_any, north_any, south_any, c0_any, c1_any, code_any, sum0, sum1, pad0, pad1, c0_ref, c1_ref, code_ref, sems
):
    loads = []

    def load(source, at, to, row, count):
        rows = pl.ds(at * RANK if at < 100 else at, count * RANK)
        copy = pltpu.make_async_copy(source.at[rows], to.at[pl.ds(row, count * RANK)], sems.at[len(loads)])
        copy.start()
        loads.append(copy)

    def put(pad, extent, row, col, ref, at, count):
        load(ref, at, pad, ((row + 2) * (extent + 4) + col + 2) * RANK, count)

    whole = []
    for k, (source, to) in enumerate(((c0_any, c0_ref), (c1_any, c1_ref), (code_any, code_ref))):
        whole.append(pltpu.make_async_copy(source, to, sems.at[COPIES + k]))
    whole[0].start()
    for r in range(4):
        put(pad0, 4, r, 0, coef_any, r * 4, 4)
        put(pad0, 4, r, -2, west_any, r * 2, 2)
        put(pad0, 4, r, 4, east_any, r * 2, 2)
    for ref, row in ((north_any, -2), (south_any, 4)):
        for r in range(2):
            put(pad0, 4, row + r, 0, ref, r * 4, 4)
            for col, base in ((-2, SIDEWAYS), (4, SIDEWAYS + CORNER)):
                load(ref, base + r * 2 * RANK, pad0, ((row + r + 2) * 8 + col + 2) * RANK, 2)
    split = len(loads)
    for copy in whole[1:]:
        copy.start()
    for r in range(2):
        put(pad1, 2, r, 0, coef_any, LEAVES + r * 2, 2)
        put(pad1, 2, r, -2, west_any, 8 + r * 2, 2)
        put(pad1, 2, r, 2, east_any, 8 + r * 2, 2)
    for ref, row in ((north_any, -2), (south_any, 2)):
        for r in range(2):
            put(pad1, 2, row + r, 0, ref, 8 + r * 2, 2)
            for col, base in ((-2, SIDEWAYS), (2, SIDEWAYS + CORNER)):
                load(ref, base + (4 + r * 2) * RANK, pad1, ((row + r + 2) * 6 + col + 2) * RANK, 2)
    whole[0].wait()
    for copy in loads[:split]:
        copy.wait()
    for a in range(2):
        for b in range(2):
            total = None
            for wy in range(6):
                at = ((2 * a + wy) * 8 + 2 * b) * RANK
                part = dot(c0_ref[:, wy * 6 * RANK : (wy + 1) * 6 * RANK], pad0[at : at + 6 * RANK])
                total = part if total is None else total + part
            for child in range(4):
                leaf = (2 * a + child // 2) * SIDE + 2 * b + child % 2
                sum0[leaf] = total[child * RANK : (child + 1) * RANK]
    for copy in loads[split:] + whole[1:]:
        copy.wait()

    def listed(leaf, carry):
        code = second_cycle(list_ref, leaf)

        @pl.when(code >= 0)
        def _():
            row = leaf // SIDE + code // 5
            col = leaf % SIDE + code % 5
            at = pl.multiple_of((row * 8 + col) * RANK, RANK)
            sum0[leaf] = sum0[leaf] - dot(code_ref[code], pad0[pl.ds(at, RANK)])

        return carry

    lax.fori_loop(0, LEAVES, listed, 0)
    sum1[...] = dot(c1_ref[...], pad1[...])


def local_far(near_list, coefs, west, east, north, south):
    vmem = pl.BlockSpec(memory_space=pltpu.VMEM)
    smem = pl.BlockSpec(memory_space=pltpu.SMEM)
    return pl.pallas_call(
        local_body,
        out_shape=(
            jax.ShapeDtypeStruct((LEAVES, RANK, LEAF), F32),
            jax.ShapeDtypeStruct((4 * RANK, LEAF), F32),
        ),
        in_specs=[smem] + [pl.BlockSpec(memory_space=pl.ANY)] * 8,
        out_specs=[vmem] * 2,
        scratch_shapes=[
            pltpu.VMEM((64 * RANK, LEAF), BF),
            pltpu.VMEM((WINDOW * RANK, LEAF), BF),
            pltpu.VMEM((4 * RANK, WINDOW * RANK), BF),
            pltpu.VMEM((4 * RANK, WINDOW * RANK), BF),
            pltpu.VMEM((25, RANK, RANK), BF),
            pltpu.SemaphoreType.DMA((COPIES + 3,)),
        ],
        compiler_params=pltpu.CompilerParams(vmem_limit_bytes=BIG),
        cost_estimate=pl.CostEstimate(flops=5_000_000_000, bytes_accessed=8_000_000, transcendentals=0),
        name="local_far",
    )(
        near_list,
        coefs,
        west,
        east,
        north,
        south,
        jnp.asarray(window_coupling(0)),
        jnp.asarray(window_coupling(1)),
        jnp.asarray(code_coupling()),
    )


def top_body(
    meta_ref, all_any, c2_any, c3_any, tree_any, sum0_any, sum1_any, field_ref, win, parents, c2_ref, c3_ref, all_ref, tree_ref, sum0, sum1, sems
):
    loads = []
    for k, (source, to) in enumerate(((all_any, all_ref), (tree_any, tree_ref), (sum1_any, sum1), (sum0_any, sum0))):
        loads.append(pltpu.make_async_copy(source, to, sems.at[2 + k]))
        loads[-1].start()

    def slab(source, to, at):
        part = pl.ds(pl.multiple_of(meta_ref[2 * WINDOW + at] * RANK, RANK), RANK)
        copy = pltpu.make_async_copy(source.at[part], to, sems.at[at])
        copy.start()
        return copy

    slabs = [slab(c2_any, c2_ref, 0), slab(c3_any, c3_ref, 1)]

    loads[0].wait()

    def lift(group, carry):
        total = jnp.zeros((RANK, LEAF), F32)
        for child in range(4):
            at = pl.multiple_of((group * 4 + child) * PACK, 16)
            packed = all_ref[pl.ds(at + RANK, 16)]
            matrix = jnp.concatenate([packed[:, k * RANK : (k + 1) * RANK] for k in range(4)], axis=0)
            total = total + dot(matrix, all_ref[pl.ds(at, RANK)])
        parents[pl.ds(pl.multiple_of(group * RANK, RANK), RANK)] = total.astype(BF)
        return carry

    lax.fori_loop(0, parents.shape[0] // RANK, lift, 0)

    def fill(start, source, stride):
        for i in range(WINDOW):
            slot = meta_ref[start + i]
            at = pl.multiple_of(jnp.maximum(slot, 0) * stride, 16)
            kept = jnp.where(slot >= 0, 1.0, 0.0).astype(BF)
            win[i * RANK : (i + 1) * RANK] = source[pl.ds(at, RANK)] * kept

    fill(WINDOW, parents, RANK)
    slabs[1].wait()
    field3 = dot(c3_ref[...], win[...]).astype(BF)
    fill(0, all_ref, PACK)
    slabs[0].wait()
    for load in loads[1:]:
        load.wait()
    field2 = (dot(c2_ref[...], win[...]) + dot_first(tree_ref[TOP], field3)).astype(BF)
    field1 = []
    for at in range(4):
        field1.append(
            (sum1[at * RANK : (at + 1) * RANK] + dot_first(tree_ref[LEAVES + at], field2)).astype(BF)
        )
    for leaf in range(LEAVES):
        above = field1[leaf // SIDE // 2 * 2 + leaf % SIDE // 2]
        field_ref[leaf] = (sum0[leaf] + dot_first(tree_ref[leaf], above)).astype(BF)


def second_cycle(list_ref, leaf):
    return list_ref[leaf]


def top_far(meta, gathered, tree, sum0, sum1):
    vmem = pl.BlockSpec(memory_space=pltpu.VMEM)
    smem = pl.BlockSpec(memory_space=pltpu.SMEM)
    anywhere = pl.BlockSpec(memory_space=pl.ANY)
    devices = gathered.shape[0] // PACK
    return pl.pallas_call(
        top_body,
        out_shape=jax.ShapeDtypeStruct((LEAVES, RANK, LEAF), BF),
        in_specs=[smem] + [anywhere] * 6,
        out_specs=vmem,
        scratch_shapes=[
            pltpu.VMEM((WINDOW * RANK, LEAF), BF),
            pltpu.VMEM((devices // 4 * RANK, LEAF), BF),
            pltpu.VMEM((RANK, WINDOW * RANK), BF),
            pltpu.VMEM((RANK, WINDOW * RANK), BF),
            pltpu.VMEM(gathered.shape, BF),
            pltpu.VMEM((TOP + 1, RANK, RANK), BF),
            pltpu.VMEM((LEAVES, RANK, LEAF), F32),
            pltpu.VMEM((4 * RANK, LEAF), F32),
            pltpu.SemaphoreType.DMA((6,)),
        ],
        compiler_params=pltpu.CompilerParams(vmem_limit_bytes=BIG),
        cost_estimate=pl.CostEstimate(flops=3_000_000_000, bytes_accessed=5_000_000, transcendentals=0),
        name="top_far",
    )(meta, gathered, jnp.asarray(window_coupling(2)), jnp.asarray(window_coupling(3)), tree, sum0, sum1)


def join_body(north_ref, south_ref, west_ref, east_ref, north_any, south_any, to_north, to_south, sems):
    copies = []

    def move(source, at, to, row, count):
        copy = pltpu.make_async_copy(source.at[pl.ds(at, count)], to.at[pl.ds(row, count)], sems.at[len(copies)])
        copy.start()
        copies.append(copy)

    for own, to, lower in ((north_ref, to_north, 0), (south_ref, to_south, 1)):
        move(own, 0, to, 0, SIDEWAYS)
        for side, base in ((west_ref, SIDEWAYS), (east_ref, SIDEWAYS + CORNER)):
            move(side, 4 * RANK * lower, to, base, 4 * RANK)
            move(side, 8 * RANK, to, base + 4 * RANK, CORNER - 4 * RANK)
    backs = []
    for k, (held, to) in enumerate(((to_north, north_any), (to_south, south_any))):
        for copy in copies[5 * k : 5 * k + 5]:
            copy.wait()
        backs.append(pltpu.make_async_copy(held, to, sems.at[10 + k]))
        backs[-1].start()
    for back in backs:
        back.wait()


def join(north, south, west, east):
    anywhere = pl.BlockSpec(memory_space=pl.ANY)
    message = jax.ShapeDtypeStruct((SIDEWAYS + 2 * CORNER, LEAF), BF)
    return pl.pallas_call(
        join_body,
        out_shape=(message, message),
        in_specs=[anywhere] * 4,
        out_specs=[anywhere] * 2,
        scratch_shapes=[pltpu.VMEM(message.shape, BF)] * 2 + [pltpu.SemaphoreType.DMA((12,))],
        compiler_params=pltpu.CompilerParams(vmem_limit_bytes=BIG),
        cost_estimate=pl.CostEstimate(flops=0, bytes_accessed=4_000_000, transcendentals=0),
        name="join",
    )(north, south, west, east)


def kernel_of(target_x, target_y, source_x, source_y):
    gap_x = target_x - source_x
    gap_y = target_y - source_y
    squared = jnp.maximum(gap_x * gap_x + gap_y * gap_y, 1e-12)
    length = squared * lax.rsqrt(squared)
    phase = length - ((length + rounder) - rounder)
    w = 0.25 - jnp.abs(phase)
    s = w * w
    wave = w * (SINE[0] + s * (SINE[1] + s * SINE[2]))
    return (jnp.exp2(squared * short_rate) + jnp.exp2(squared * long_rate) * wave).astype(BF)


def spread_columns(rows, columns):
    turned = rows.T
    for k in range(columns.shape[1] // 128):
        columns[:, 128 * k : 128 * (k + 1)] = jnp.broadcast_to(turned[:, k : k + 1], (LEAF, 128))


def block_into(to, columns, points, shift_y, shift_x):
    source_x = (points[0:1] + shift_x.astype(F32)) * waves
    source_y = (points[1:2] + shift_y.astype(F32)) * waves
    rows = 32
    for i in range(0, LEAF, rows):
        for j in (0, 128):
            to[i : i + rows, j : j + 128] = kernel_of(
                columns[i : i + rows, 0:128],
                columns[i : i + rows, 128:256],
                jnp.broadcast_to(source_x[:, j : j + 128], (rows, 128)),
                jnp.broadcast_to(source_y[:, j : j + 128], (rows, 128)),
            )


def turn_points(columns, leaf, position, noise):
    rows = jnp.concatenate([position * waves, noise, jnp.zeros((5, LEAF), F32)], axis=0)
    spread_columns(rows, columns.at[leaf])


def own_pairs(first, last):
    pairs = []
    for r in range(first, last):
        for c in range(SIDE):
            for dy, dx in ((0, 1), (1, -1), (1, 0), (1, 1)):
                if r + dy < SIDE and 0 <= c + dx < SIDE:
                    pairs.append((r * SIDE + c, (r + dy) * SIDE + c + dx, dy, dx))
    return pairs


def near_own_body(first, last, table_ref, q_any, pos_ref, noise_ref, *refs):
    before_any, out_any, columns, blocks, q_ref, before_ref, out_ref, sems = (None,) * (8 - len(refs)) + refs
    loads = [pltpu.make_async_copy(q_any, q_ref, sems.at[0])]
    if first:
        loads.append(pltpu.make_async_copy(before_any.at[pl.ds(SIDE, SIDE)], before_ref, sems.at[1]))
    for load in loads:
        load.start()
    pairs = own_pairs(first, last)
    start = first * SIDE
    count = (last - first) * SIDE

    def turn(leaf, carry):
        turn_points(columns, leaf, pos_ref[leaf], noise_ref[leaf])
        return carry

    lax.fori_loop(start, start + count, turn, 0)
    zero = jnp.int32(0)

    def selves(i, carry):
        for half in range(2):
            leaf = start + 2 * i + half
            block_into(blocks.at[2 * i + half], columns.at[leaf], pos_ref[leaf], zero, zero)
        return carry

    lax.fori_loop(0, count // 2, selves, 0)

    def pair(i):
        at = 4 * i
        place = count + 2 * i
        target, source = table_ref[at], table_ref[at + 1]
        block_into(blocks.at[place], columns.at[target], pos_ref[source], table_ref[at + 2], table_ref[at + 3])
        blocks[place + 1] = blocks[place].T

    def both(i, carry):
        pair(2 * i)
        pair(2 * i + 1)
        return carry

    lax.fori_loop(0, len(pairs) // 2, both, 0)
    if len(pairs) % 2:
        pair(len(pairs) - 1)
    for load in loads:
        load.wait()
    parts = {leaf: [(leaf - start, leaf)] for leaf in range(start, start + count)}
    for i, (target, source, _, _) in enumerate(pairs):
        parts[target].append((count + 2 * i, source))
        parts.setdefault(source, []).append((count + 1 + 2 * i, target))
    backs = []
    for leaf, terms in sorted(parts.items()):
        total = None
        for place, source in terms:
            part = dot(blocks[place], q_ref[source])
            total = part if total is None else total + part
        if leaf < start + count:
            noise = jnp.concatenate([columns[leaf, :, 256:384]] * 2, axis=1)
            total = total + noise * q_ref[leaf].astype(F32)
        if first and leaf < start + SIDE:
            total = total + before_ref[leaf - start]
        out_ref[leaf - start] = total
        backs.append(pltpu.make_async_copy(out_ref.at[leaf - start], out_any.at[leaf - start], sems.at[2 + leaf - start]))
        backs[-1].start()
    for back in backs:
        back.wait()


def near_own(first, last, q, points, noise, after, before):
    vmem = pl.BlockSpec(memory_space=pltpu.VMEM)
    smem = pl.BlockSpec(memory_space=pltpu.SMEM)
    anywhere = pl.BlockSpec(memory_space=pl.ANY)
    pairs = own_pairs(first, last)
    leaves = (min(last + 1, SIDE) - first) * SIDE

    def body(after_ref, *refs):
        near_own_body(first, last, *refs)

    return pl.pallas_call(
        body,
        out_shape=jax.ShapeDtypeStruct((leaves, LEAF, LEAF), F32),
        in_specs=[anywhere, smem, anywhere, vmem, vmem] + [anywhere] * len(before),
        out_specs=anywhere,
        scratch_shapes=[
            pltpu.VMEM((LEAVES, LEAF, 384), F32),
            pltpu.VMEM(((last - first) * SIDE + 2 * len(pairs), LEAF, LEAF), BF),
            pltpu.VMEM((LEAVES, LEAF, LEAF), BF),
            pltpu.VMEM((SIDE, LEAF, LEAF), F32),
            pltpu.VMEM((leaves, LEAF, LEAF), F32),
            pltpu.SemaphoreType.DMA((2 + leaves,)),
        ],
        compiler_params=pltpu.CompilerParams(vmem_limit_bytes=BIG),
        cost_estimate=pl.CostEstimate(flops=6_000_000_000, bytes_accessed=4_000_000, transcendentals=8_000_000),
        name="near_own",
    )(after, jnp.asarray(np.array(pairs, np.int32).reshape(-1)), q, points, noise, *before)


def edge_items():
    table = near_table(False)
    return [[leaf, *table[leaf, j]] for leaf in range(LEAVES) for j in range(5) if table[leaf, j, 0] >= 0]


ITEMS = edge_items()
EDGES = len(ITEMS)


def extra_of(list_ref, slot_ref, leaf):
    code = second_cycle(list_ref, leaf)
    place = (leaf // SIDE + code // 5) * 8 + leaf % SIDE + code % 5
    slot = slot_ref[jnp.where(code >= 0, place, 0)]
    return code, slot


def edge_body(
    half_at, list_ref, table_ref, slot_ref, after_ref, own_pos_ref, west_any, east_any, north_any, south_any, out_any,
    columns, parts, points, out_ref, sems,
):
    start = 8 * half_at
    copies = []
    sources = (
        (west_any, 12 * RANK),
        (east_any, 12 * RANK),
        (north_any, 12 * RANK),
        (north_any, SIDEWAYS + 8 * RANK),
        (north_any, SIDEWAYS + CORNER + 8 * RANK),
        (south_any, 12 * RANK),
        (south_any, SIDEWAYS + 8 * RANK),
        (south_any, SIDEWAYS + CORNER + 8 * RANK),
    )
    for k, (source, at) in enumerate(sources):
        copies.append(pltpu.make_async_copy(source.at[pl.ds(at, 48)], parts.at[k], sems.at[k]))
    for copy in copies:
        copy.start()

    def turn(leaf, carry):
        turn_points(columns, leaf, own_pos_ref[leaf], jnp.zeros((1, LEAF), F32))
        return carry

    lax.fori_loop(start, start + 8, turn, 0)
    points[0:LEAVES] = own_pos_ref[...]
    for copy in copies:
        copy.wait()
    slots = (16, 24, 32, 40, 44, 48, 56, 60)
    for k in range(8):
        whole = parts[k].astype(F32)
        whole = (whole[0:16] + whole[16:32]) + whole[32:48]
        first, count = {3: (4, 4), 4: (4, 4), 6: (0, 4), 7: (0, 4)}.get(k, (0, 8))
        for i in range(count):
            points[slots[k] + i] = whole[2 * (first + i) : 2 * (first + i) + 2]

    def fixed(i, carry):
        for half in range(2):
            at = 8 * i + 4 * half
            block_into(
                out_ref.at[2 * i + half],
                columns.at[table_ref[at]],
                points[table_ref[at + 1]],
                table_ref[at + 2],
                table_ref[at + 3],
            )
        return carry

    lax.fori_loop(0, EDGES // 4, fixed, 0)
    backs = []
    for k, part in enumerate((pl.ds(0, EDGES // 2), pl.ds(EDGES // 2, 8))):
        backs.append(pltpu.make_async_copy(out_ref.at[part], out_any.at[part], sems.at[8 + k]))
    backs[0].start()

    def extra(i, carry):
        for half in range(2):
            leaf = start + 2 * i + half
            code, slot = extra_of(list_ref, slot_ref, leaf)
            code = jnp.maximum(code, 0)
            block_into(out_ref.at[EDGES // 2 + 2 * i + half], columns.at[leaf], points[slot], code // 5 - 2, code % 5 - 2)
        return carry

    lax.fori_loop(0, 4, extra, 0)
    backs[1].start()
    for back in backs:
        back.wait()


def edge_blocks(half_at, near_list, after, own_points, west, east, north, south):
    vmem = pl.BlockSpec(memory_space=pltpu.VMEM)
    smem = pl.BlockSpec(memory_space=pltpu.SMEM)
    anywhere = pl.BlockSpec(memory_space=pl.ANY)
    items = [item for item in ITEMS if item[0] // 8 == half_at]
    assert len(items) * 2 == EDGES

    def body(*refs):
        edge_body(half_at, *refs)

    return pl.pallas_call(
        body,
        out_shape=jax.ShapeDtypeStruct((EDGES // 2 + 8, LEAF, LEAF), BF),
        in_specs=[smem, smem, smem, anywhere, vmem] + [anywhere] * 4,
        out_specs=anywhere,
        scratch_shapes=[
            pltpu.VMEM((LEAVES, LEAF, 384), F32),
            pltpu.VMEM((8, 48, LEAF), BF),
            pltpu.VMEM((64, 2, LEAF), F32),
            pltpu.VMEM((EDGES // 2 + 8, LEAF, LEAF), BF),
            pltpu.SemaphoreType.DMA((10,)),
        ],
        compiler_params=pltpu.CompilerParams(vmem_limit_bytes=BIG),
        cost_estimate=pl.CostEstimate(flops=6_000_000_000, bytes_accessed=8_000_000, transcendentals=12_000_000),
        name="edge_blocks",
    )(
        near_list, jnp.asarray(np.array(items, np.int32).reshape(-1)), jnp.asarray(SLOT_OF), after, own_points,
        west, east, north, south,
    )


def final_body(
    list_ref, slot_ref, q_any, west_any, east_any, north_any, north_corner_any, south_any, south_corner_any,
    upper_blocks_any, lower_blocks_any, row0_any, row1_any, row2_any, basis_ref, field_ref, out_any, held, blocks, sums, outs, sems,
):
    firsts = [min(at for at in range(EDGES) if ITEMS[at][0] // SIDE == r) for r in range(SIDE)] + [EDGES]
    stages = [[], [], [], []]
    count = 0

    def copy(stage, source, at, rows, to, row):
        nonlocal count
        made = pltpu.make_async_copy(source.at[pl.ds(at, rows)], to.at[pl.ds(row, rows)], sems.at[count])
        count += 1
        stages[stage].append(made)

    copy(0, north_any, 0, 8, held, 32)
    copy(0, north_corner_any, 0, 8, held, 40)
    for stage, low, high in ((0, 0, 3), (1, 3, 4)):
        copy(stage, west_any, 2 * low, 2 * (high - low), held, 16 + 2 * low)
        copy(stage, east_any, 2 * low, 2 * (high - low), held, 24 + 2 * low)
        copy(stage, q_any, 4 * low, 4 * (high - low), held, 4 * low)
    copy(2, south_any, 0, 8, held, 48)
    copy(2, south_corner_any, 0, 8, held, 56)
    for r in range(SIDE):
        source = upper_blocks_any if r < 2 else lower_blocks_any
        back = 0 if r < 2 else EDGES // 2
        copy(r, source, firsts[r] - back, firsts[r + 1] - firsts[r], blocks, firsts[r])
        copy(r, source, EDGES // 2 + SIDE * (r % 2), SIDE, blocks, EDGES + SIDE * r)
        copy(r, (row0_any, row1_any, row2_any, row2_any)[r], SIDE if r == 3 else 0, SIDE, sums, SIDE * r)
    backs = []
    for r in range(SIDE):
        part = pl.ds(SIDE * r, SIDE)
        backs.append(pltpu.make_async_copy(outs.at[part], out_any.at[part], sems.at[count + r]))
    for r in range(2):
        for made in stages[r]:
            made.start()
    for leaf in range(LEAVES):
        if leaf % SIDE == 0:
            for made in stages[leaf // SIDE]:
                made.wait()
            if leaf // SIDE + 2 < SIDE:
                for made in stages[leaf // SIDE + 2]:
                    made.start()
        total = dot_first(basis_ref[leaf], field_ref[leaf])
        for at in range(EDGES):
            if ITEMS[at][0] == leaf:
                total = total + dot(blocks[at], held[ITEMS[at][1]])
        total = total + sums[leaf]
        sums[leaf] = total
        outs[leaf] = total.astype(BF)
        code, slot = extra_of(list_ref, slot_ref, leaf)

        @pl.when(code >= 0)
        def _(leaf=leaf, slot=slot):
            outs[leaf] = (sums[leaf] + dot(blocks[EDGES + leaf], held[slot])).astype(BF)

        if leaf % SIDE == SIDE - 1:
            backs[leaf // SIDE].start()
    for back in backs:
        back.wait()


def finish(near_list, q, halos, upper_blocks, lower_blocks, sums, basis, field):
    vmem = pl.BlockSpec(memory_space=pltpu.VMEM)
    smem = pl.BlockSpec(memory_space=pltpu.SMEM)
    anywhere = pl.BlockSpec(memory_space=pl.ANY)

    return pl.pallas_call(
        final_body,
        out_shape=jax.ShapeDtypeStruct((LEAVES, LEAF, LEAF), BF),
        in_specs=[smem, smem] + [anywhere] * 12 + [vmem, vmem],
        out_specs=anywhere,
        scratch_shapes=[
            pltpu.VMEM((64, LEAF, LEAF), BF),
            pltpu.VMEM((EDGES + LEAVES, LEAF, LEAF), BF),
            pltpu.VMEM((LEAVES, LEAF, LEAF), F32),
            pltpu.VMEM((LEAVES, LEAF, LEAF), BF),
            pltpu.SemaphoreType.DMA((28,)),
        ],
        compiler_params=pltpu.CompilerParams(vmem_limit_bytes=BIG),
        cost_estimate=pl.CostEstimate(flops=4_000_000_000, bytes_accessed=24_000_000, transcendentals=0),
        name="finish",
    )(near_list, jnp.asarray(SLOT_OF), q, *halos, upper_blocks, lower_blocks, *sums, basis, field)


def window_slots(wide, narrow, steps):
    row, col = lax.axis_index("narrow"), lax.axis_index("wide")
    wy, wx = np.arange(WINDOW) // 6, np.arange(WINDOW) % 6

    def slots(target_y, target_x, scale):
        y = target_y // 2 * 2 - 2 + wy
        x = target_x // 2 * 2 - 2 + wx
        inside = (y >= 0) & (y < narrow // scale) & (x >= 0) & (x < wide // scale)
        apart = {"narrow": (y * scale) ^ row, "wide": (x * scale) ^ col}
        slot = 0
        for at, (axis, bit) in enumerate(steps):
            slot = slot + (apart[axis] // bit & 1) * (1 << at)
        return jnp.where(inside, slot if scale == 1 else slot // 4, -1)

    parity2 = row % 2 * 2 + col % 2
    parity3 = row // 2 % 2 * 2 + col // 2 % 2
    return jnp.concatenate(
        [slots(row, col, 1), slots(row // 2, col // 2, 2), jnp.stack([parity2, parity3])]
    ).astype(jnp.int32)


def per_device(wide, narrow, charges, positions, noise, leaf_basis, transfer, near_list):
    q = charges.reshape(LEAVES, LEAF, LEAF)
    points = positions.reshape(LEAVES, 2, LEAF)
    basis = leaf_basis.reshape(LEAVES, RANK, LEAF)
    tree = transfer[0, 0]
    code_y, code_x = near_list // 5, near_list % 5
    outer = (near_list >= 0) & ((code_y == 0) | (code_y == 4) | (code_x == 0) | (code_x == 4))
    listing = jnp.max(jnp.where(outer, near_list, -1), axis=-1).reshape(-1)
    steps = gather_steps(wide, narrow)
    meta = window_slots(wide, narrow, steps)

    east, west, north, south, coefs, give = go_up(q, basis, tree, points)
    from_west = shift(east, "wide", 1)
    from_east = shift(west, "wide", -1)
    q_north = shift(charges[2:4], "narrow", 1)
    q_south = shift(charges[0:2], "narrow", -1)

    noise_rows = noise.reshape(LEAVES, 1, LEAF)

    def step(value, at):
        axis, bit = steps[at]
        return lax.ppermute(value, axis, [(i, i ^ bit) for i in range(lax.axis_size(axis))])

    def tie(*values):
        return lax.optimization_barrier(values)

    gathered = give
    other = step(gathered, 0)
    row0 = near_own(0, 1, q, points, noise_rows, give, [])
    other, row0 = tie(other, row0)
    gathered = jnp.concatenate([gathered, other], axis=0)
    other = step(gathered, 1)
    row1 = near_own(1, 2, q, points, noise_rows, gathered, [row0])
    to_east, to_west = charges[:, 2:4], charges[:, 0:2]
    other, from_west, from_east, row1, to_east, to_west, q_north, q_south = tie(
        other, from_west, from_east, row1, to_east, to_west, q_north, q_south
    )
    gathered = jnp.concatenate([gathered, other], axis=0)
    other = step(gathered, 2)
    to_north, to_south = join(north, south, from_west, from_east)
    from_south = shift(to_north, "narrow", -1)
    from_north = shift(to_south, "narrow", 1)
    q_west = shift(to_east, "wide", 1)
    q_east = shift(to_west, "wide", -1)
    row2 = near_own(2, 4, q, points, noise_rows, to_north, [row1])
    other, from_south, from_north, row2 = tie(other, from_south, from_north, row2)
    gathered = jnp.concatenate([gathered, other], axis=0)
    other = step(gathered, 3)
    sums = local_far(listing, coefs, from_west, from_east, from_north, from_south)
    upper_blocks = edge_blocks(0, listing, sums[1], points, from_west, from_east, from_north, from_south)
    other, upper_blocks = tie(other, upper_blocks)
    for at in range(4, len(steps)):
        gathered = jnp.concatenate([gathered, other], axis=0)
        other = step(gathered, at)
        if at == 4:
            lower_blocks = edge_blocks(1, listing, upper_blocks, points, from_west, from_east, from_north, from_south)
            other, lower_blocks, q_west, q_east = tie(other, lower_blocks, q_west, q_east)
            q_north_corner = shift(jnp.stack([q_west[2:4], q_east[2:4]]), "narrow", 1)
            q_south_corner = shift(jnp.stack([q_west[0:2], q_east[0:2]]), "narrow", -1)
    gathered = jnp.concatenate([gathered, other], axis=0)
    field = top_far(meta, gathered, tree, *sums)
    q_north_corner, q_south_corner, field = tie(q_north_corner, q_south_corner, field)
    halos = [
        value.reshape(8, LEAF, LEAF)
        for value in (q_west, q_east, q_north, q_north_corner, q_south, q_south_corner)
    ]
    out = finish(listing, q, halos, upper_blocks, lower_blocks, (row0, row1, row2), basis, field)
    return out.reshape(SIDE, SIDE, LEAF, LEAF)


def solution(mesh):
    wide, narrow = mesh.shape["wide"], mesh.shape["narrow"]
    in_specs = (
        P("narrow", "wide", None, None),
        P("narrow", "wide", None, None),
        P("narrow", "wide", None),
        P("narrow", "wide", None, None),
        P("narrow", "wide", None, None, None),
        P("narrow", "wide", None),
    )
    out_specs = P("narrow", "wide", None, None)

    def step(*arrays):
        return per_device(wide, narrow, *arrays)

    return jax.shard_map(step, mesh=mesh, in_specs=in_specs, out_specs=out_specs, check_vma=False)
```

```python
import math

import jax
import jax.numpy as jnp
import ml_dtypes
import numpy as np
from jax import lax
from jax.experimental import pallas as pl
from jax.experimental.pallas import tpu as pltpu
from jax.sharding import PartitionSpec as P

LEAF = 256
CHEB = 8
RANK = 64
NEAR = 10
SIDE = 4
LEAVES = SIDE * SIDE
TOP = 20
WINDOW = 36
PACK = RANK + 16
SIDEWAYS = 8 * RANK + 4 * RANK + 48
CORNER = 4 * RANK + 4 * RANK + 48
BIG = 58 << 20
COPIES = 42
BF = jnp.bfloat16
F32 = jnp.float32

short_len = 0.125
long_weight = 0.03125
reach = 3.0 * SIDE
waves = 10.0
LOG2E = math.log2(math.e)
long_rate = -0.5 / (reach * reach) * LOG2E / (waves * waves)
short_rate = -0.5 / (short_len * short_len) * LOG2E / (waves * waves)
rounder = 1.5 * 2.0**23


def sine_terms(count):
    w = np.cos(np.pi * (np.arange(2000) + 0.5) / 2000) * 0.25
    powers = np.stack([w ** (2 * i + 1) for i in range(count)], 1)
    return [float(c) for c in np.linalg.lstsq(powers, np.sin(2 * np.pi * w) * long_weight, rcond=None)[0]]


SINE = sine_terms(3)


def coupling(height, shift_y, shift_x):
    points = 0.5 * (1.0 + np.cos((2.0 * np.arange(CHEB) + 1.0) * (math.pi / (2.0 * CHEB))))
    node_x = np.tile(points, CHEB)
    node_y = np.repeat(points, CHEB)
    gap_x = (node_x[:, None] - node_x[None, :] - shift_x) * 2.0**height
    gap_y = (node_y[:, None] - node_y[None, :] - shift_y) * 2.0**height
    squared = gap_x * gap_x + gap_y * gap_y
    return np.exp(squared * (-0.5 / (short_len * short_len))) + long_weight * np.exp(
        squared * (-0.5 / (reach * reach))
    ) * np.cos(2.0 * math.pi * waves * np.sqrt(squared))


def window_coupling(height):
    table = np.zeros((2, 2, RANK, 6, 6, RANK))
    for py in range(2):
        for px in range(2):
            for wy in range(6):
                for wx in range(6):
                    shift_y, shift_x = wy - 2 - py, wx - 2 - px
                    if max(abs(shift_y), abs(shift_x)) >= 2:
                        table[py, px, :, wy, wx] = coupling(height, shift_y, shift_x)
    return table.reshape(4 * RANK, WINDOW * RANK).astype(ml_dtypes.bfloat16)


def code_coupling():
    return np.stack([coupling(0, code // 5 - 2, code % 5 - 2) for code in range(25)]).astype(ml_dtypes.bfloat16)


def halo_slot(row, col):
    if 0 <= row < 4 and 0 <= col < 4:
        return row * 4 + col
    if 0 <= row < 4:
        return 16 + row * 2 + col + 2 if col < 0 else 24 + row * 2 + col - 4
    base, r = (32, row + 2) if row < 0 else (48, row - 4)
    if 0 <= col < 4:
        return base + r * 4 + col
    return base + 8 + r * 2 + col + 2 if col < 0 else base + 12 + r * 2 + col - 4


SLOT_OF = np.array([halo_slot(r - 2, c - 2) for r in range(8) for c in range(8)], np.int32)


def near_table(own):
    width = 9 if own else 5
    table = np.zeros((LEAVES, width, 3), np.int32)
    table[:, :, 0] = -1
    for r in range(SIDE):
        for c in range(SIDE):
            at = 0
            for dy in (-1, 0, 1):
                for dx in (-1, 0, 1):
                    slot = halo_slot(r + dy, c + dx)
                    if (slot < LEAVES) == own:
                        table[r * SIDE + c, at] = (slot, dy, dx)
                        at += 1
    return table


def bits(count):
    return [1 << i for i in range(count.bit_length() - 1)]


def gather_steps(wide, narrow):
    return (
        [("wide", 1), ("narrow", 1)]
        + [("wide", b) for b in reversed(bits(wide)[1:])]
        + [("narrow", b) for b in reversed(bits(narrow)[1:])]
    )


def shift(value, axis, steps):
    count = lax.axis_size(axis)
    return lax.ppermute(value, axis, [(i, i + steps) for i in range(count) if 0 <= i + steps < count])


def dot(a, b):
    return jnp.dot(a, b, preferred_element_type=F32)


def dot_first(a, b):
    return lax.dot_general(a, b, (((0,), (0,)), ((), ())), preferred_element_type=F32)


def up_body(
    q_any, basis_any, tree_any, pos_ref, east_ref, west_ref, north_ref, south_ref, coef_ref, give_ref, to_east, to_west, to_north, to_south,
    q_ref, basis_ref, tree_ref, sems
):
    loads = []
    for k in range(4):
        part = pl.ds(4 * k, 4)
        loads.append(pltpu.make_async_copy(basis_any.at[part], basis_ref.at[part], sems.at[2 * k]))
        loads.append(pltpu.make_async_copy(q_any.at[part], q_ref.at[part], sems.at[2 * k + 1]))
    loads.append(pltpu.make_async_copy(tree_any, tree_ref, sems.at[8]))
    for load in loads:
        load.start()
    backs = []
    level0 = []
    for leaf in range(LEAVES):
        if leaf % 4 == 0:
            loads[leaf // 2].wait()
            loads[leaf // 2 + 1].wait()
            half = pl.ds(leaf // 2, 2)
            for to, low in ((to_west, leaf), (to_east, leaf + 2)):
                backs.append(pltpu.make_async_copy(q_ref.at[pl.ds(low, 2)], to.at[half], sems.at[9 + len(backs)]))
                backs[-1].start()
            to, row = (to_north, leaf) if leaf < 8 else (to_south, leaf - 8)
            backs.append(pltpu.make_async_copy(q_ref.at[pl.ds(leaf, 4)], to.at[pl.ds(row, 4)], sems.at[9 + len(backs)]))
            backs[-1].start()
        coef = dot(basis_ref[leaf], q_ref[leaf]).astype(BF)
        level0.append(coef)
        r, c = leaf // SIDE, leaf % SIDE
        coef_ref[leaf * RANK : (leaf + 1) * RANK] = coef
        ref, at = (west_ref, r * 2 + c) if c < 2 else (east_ref, r * 2 + c - 2)
        ref[at * RANK : (at + 1) * RANK] = coef
        ref, at = (north_ref, r * 4 + c) if r < 2 else (south_ref, r * 4 + c - 8)
        ref[at * RANK : (at + 1) * RANK] = coef
    loads[8].wait()
    level1 = []
    for r in range(2):
        for c in range(2):
            total = None
            for dr in range(2):
                for dc in range(2):
                    leaf = (2 * r + dr) * SIDE + 2 * c + dc
                    part = dot(tree_ref[leaf], level0[leaf])
                    total = part if total is None else total + part
            coef = total.astype(BF)
            at = r * 2 + c
            level1.append(coef)
            coef_ref[(LEAVES + at) * RANK : (LEAVES + at + 1) * RANK] = coef
            for ref in (east_ref, west_ref, north_ref, south_ref):
                ref[(8 + at) * RANK : (9 + at) * RANK] = coef
    total = None
    for at in range(4):
        part = dot(tree_ref[LEAVES + at], level1[at])
        total = part if total is None else total + part
    give_ref[0:RANK] = total.astype(BF)
    top = tree_ref[TOP]
    give_ref[RANK:PACK] = jnp.concatenate([top[16 * k : 16 * k + 16] for k in range(4)], axis=1)
    for ref, leaves in (
        (west_ref, [r * 4 + c for r in range(4) for c in (0, 1)]),
        (east_ref, [r * 4 + c for r in range(4) for c in (2, 3)]),
        (north_ref, range(8)),
        (south_ref, range(8, 16)),
    ):
        rest = jnp.concatenate([pos_ref[leaf] for leaf in leaves], axis=0)
        for part in range(3):
            held = rest.astype(BF)
            at = 12 * RANK + 16 * part
            ref[at : at + 16] = held
            rest = rest - held.astype(F32)
    for back in backs:
        back.wait()


def go_up(q, basis, tree, points):
    vmem = pl.BlockSpec(memory_space=pltpu.VMEM)
    side = jax.ShapeDtypeStruct((SIDEWAYS, LEAF), BF)
    return pl.pallas_call(
        up_body,
        out_shape=(
            side,
            side,
            side,
            side,
            jax.ShapeDtypeStruct(((LEAVES + 4) * RANK, LEAF), BF),
            jax.ShapeDtypeStruct((PACK, LEAF), BF),
        )
        + (jax.ShapeDtypeStruct((8, LEAF, LEAF), BF),) * 4,
        in_specs=[pl.BlockSpec(memory_space=pl.ANY)] * 3 + [vmem],
        out_specs=[vmem] * 6 + [pl.BlockSpec(memory_space=pl.ANY)] * 4,
        scratch_shapes=[
            pltpu.VMEM((LEAVES, LEAF, LEAF), BF),
            pltpu.VMEM((LEAVES, RANK, LEAF), BF),
            pltpu.VMEM((TOP + 1, RANK, RANK), BF),
            pltpu.SemaphoreType.DMA((21,)),
        ],
        compiler_params=pltpu.CompilerParams(vmem_limit_bytes=BIG),
        cost_estimate=pl.CostEstimate(flops=300_000_000, bytes_accessed=5_000_000, transcendentals=0),
        name="upward",
    )(q, basis, tree, points)


def local_body(
    list_ref, coef_any, west_any, east_any, north_any, south_any, c0_any, c1_any, code_any, sum0, sum1, pad0, pad1, c0_ref, c1_ref, code_ref, sems
):
    loads = []

    def load(source, at, to, row, count):
        rows = pl.ds(at * RANK if at < 100 else at, count * RANK)
        copy = pltpu.make_async_copy(source.at[rows], to.at[pl.ds(row, count * RANK)], sems.at[len(loads)])
        copy.start()
        loads.append(copy)

    def put(pad, extent, row, col, ref, at, count):
        load(ref, at, pad, ((row + 2) * (extent + 4) + col + 2) * RANK, count)

    whole = []
    for k, (source, to) in enumerate(((c0_any, c0_ref), (c1_any, c1_ref), (code_any, code_ref))):
        whole.append(pltpu.make_async_copy(source, to, sems.at[COPIES + k]))
    whole[0].start()
    for r in range(4):
        put(pad0, 4, r, 0, coef_any, r * 4, 4)
        put(pad0, 4, r, -2, west_any, r * 2, 2)
        put(pad0, 4, r, 4, east_any, r * 2, 2)
    for ref, row in ((north_any, -2), (south_any, 4)):
        for r in range(2):
            put(pad0, 4, row + r, 0, ref, r * 4, 4)
            for col, base in ((-2, SIDEWAYS), (4, SIDEWAYS + CORNER)):
                load(ref, base + r * 2 * RANK, pad0, ((row + r + 2) * 8 + col + 2) * RANK, 2)
    split = len(loads)
    for copy in whole[1:]:
        copy.start()
    for r in range(2):
        put(pad1, 2, r, 0, coef_any, LEAVES + r * 2, 2)
        put(pad1, 2, r, -2, west_any, 8 + r * 2, 2)
        put(pad1, 2, r, 2, east_any, 8 + r * 2, 2)
    for ref, row in ((north_any, -2), (south_any, 2)):
        for r in range(2):
            put(pad1, 2, row + r, 0, ref, 8 + r * 2, 2)
            for col, base in ((-2, SIDEWAYS), (2, SIDEWAYS + CORNER)):
                load(ref, base + (4 + r * 2) * RANK, pad1, ((row + r + 2) * 6 + col + 2) * RANK, 2)
    whole[0].wait()
    for copy in loads[:split]:
        copy.wait()
    for a in range(2):
        for b in range(2):
            total = None
            for wy in range(6):
                at = ((2 * a + wy) * 8 + 2 * b) * RANK
                part = dot(c0_ref[:, wy * 6 * RANK : (wy + 1) * 6 * RANK], pad0[at : at + 6 * RANK])
                total = part if total is None else total + part
            for child in range(4):
                leaf = (2 * a + child // 2) * SIDE + 2 * b + child % 2
                sum0[leaf] = total[child * RANK : (child + 1) * RANK]
    for copy in loads[split:] + whole[1:]:
        copy.wait()

    def listed(leaf, carry):
        code = second_cycle(list_ref, leaf)

        @pl.when(code >= 0)
        def _():
            row = leaf // SIDE + code // 5
            col = leaf % SIDE + code % 5
            at = pl.multiple_of((row * 8 + col) * RANK, RANK)
            sum0[leaf] = sum0[leaf] - dot(code_ref[code], pad0[pl.ds(at, RANK)])

        return carry

    lax.fori_loop(0, LEAVES, listed, 0)
    sum1[...] = dot(c1_ref[...], pad1[...])


def local_far(near_list, coefs, west, east, north, south):
    vmem = pl.BlockSpec(memory_space=pltpu.VMEM)
    smem = pl.BlockSpec(memory_space=pltpu.SMEM)
    return pl.pallas_call(
        local_body,
        out_shape=(
            jax.ShapeDtypeStruct((LEAVES, RANK, LEAF), F32),
            jax.ShapeDtypeStruct((4 * RANK, LEAF), F32),
        ),
        in_specs=[smem] + [pl.BlockSpec(memory_space=pl.ANY)] * 8,
        out_specs=[vmem] * 2,
        scratch_shapes=[
            pltpu.VMEM((64 * RANK, LEAF), BF),
            pltpu.VMEM((WINDOW * RANK, LEAF), BF),
            pltpu.VMEM((4 * RANK, WINDOW * RANK), BF),
            pltpu.VMEM((4 * RANK, WINDOW * RANK), BF),
            pltpu.VMEM((25, RANK, RANK), BF),
            pltpu.SemaphoreType.DMA((COPIES + 3,)),
        ],
        compiler_params=pltpu.CompilerParams(vmem_limit_bytes=BIG),
        cost_estimate=pl.CostEstimate(flops=5_000_000_000, bytes_accessed=8_000_000, transcendentals=0),
        name="local_far",
    )(
        near_list,
        coefs,
        west,
        east,
        north,
        south,
        jnp.asarray(window_coupling(0)),
        jnp.asarray(window_coupling(1)),
        jnp.asarray(code_coupling()),
    )


def top_body(
    meta_ref, mine_any, other_any, c2_any, c3_any, tree_any, sum0_any, sum1_any, field_ref, win, parents, c2_ref, c3_ref, all_ref, tree_ref, sum0, sum1, sems
):
    loads = []
    for k, (source, to) in enumerate(((mine_any, all_ref.at[pl.ds(0, mine_any.shape[0])]), (other_any, all_ref.at[pl.ds(mine_any.shape[0], mine_any.shape[0])]), (tree_any, tree_ref), (sum1_any, sum1), (sum0_any, sum0))):
        loads.append(pltpu.make_async_copy(source, to, sems.at[2 + k]))
        loads[-1].start()

    def slab(source, to, at):
        part = pl.ds(pl.multiple_of(meta_ref[2 * WINDOW + at] * RANK, RANK), RANK)
        copy = pltpu.make_async_copy(source.at[part], to, sems.at[at])
        copy.start()
        return copy

    slabs = [slab(c2_any, c2_ref, 0), slab(c3_any, c3_ref, 1)]

    loads[0].wait()
    loads[1].wait()

    def lift(group, carry):
        total = jnp.zeros((RANK, LEAF), F32)
        for child in range(4):
            at = pl.multiple_of((group * 4 + child) * PACK, 16)
            packed = all_ref[pl.ds(at + RANK, 16)]
            matrix = jnp.concatenate([packed[:, k * RANK : (k + 1) * RANK] for k in range(4)], axis=0)
            total = total + dot(matrix, all_ref[pl.ds(at, RANK)])
        parents[pl.ds(pl.multiple_of(group * RANK, RANK), RANK)] = total.astype(BF)
        return carry

    lax.fori_loop(0, parents.shape[0] // RANK, lift, 0)

    def fill(start, source, stride):
        for i in range(WINDOW):
            slot = meta_ref[start + i]
            at = pl.multiple_of(jnp.maximum(slot, 0) * stride, 16)
            kept = jnp.where(slot >= 0, 1.0, 0.0).astype(BF)
            win[i * RANK : (i + 1) * RANK] = source[pl.ds(at, RANK)] * kept

    fill(WINDOW, parents, RANK)
    slabs[1].wait()
    field3 = dot(c3_ref[...], win[...]).astype(BF)
    fill(0, all_ref, PACK)
    slabs[0].wait()
    for load in loads[2:]:
        load.wait()
    field2 = (dot(c2_ref[...], win[...]) + dot_first(tree_ref[TOP], field3)).astype(BF)
    field1 = []
    for at in range(4):
        field1.append(
            (sum1[at * RANK : (at + 1) * RANK] + dot_first(tree_ref[LEAVES + at], field2)).astype(BF)
        )
    for leaf in range(LEAVES):
        above = field1[leaf // SIDE // 2 * 2 + leaf % SIDE // 2]
        field_ref[leaf] = (sum0[leaf] + dot_first(tree_ref[leaf], above)).astype(BF)


def second_cycle(list_ref, leaf):
    return list_ref[leaf]


def top_far(meta, mine, other, tree, sum0, sum1):
    vmem = pl.BlockSpec(memory_space=pltpu.VMEM)
    smem = pl.BlockSpec(memory_space=pltpu.SMEM)
    anywhere = pl.BlockSpec(memory_space=pl.ANY)
    rows = 2 * mine.shape[0]
    devices = rows // PACK
    return pl.pallas_call(
        top_body,
        out_shape=jax.ShapeDtypeStruct((LEAVES, RANK, LEAF), BF),
        in_specs=[smem] + [anywhere] * 7,
        out_specs=vmem,
        scratch_shapes=[
            pltpu.VMEM((WINDOW * RANK, LEAF), BF),
            pltpu.VMEM((devices // 4 * RANK, LEAF), BF),
            pltpu.VMEM((RANK, WINDOW * RANK), BF),
            pltpu.VMEM((RANK, WINDOW * RANK), BF),
            pltpu.VMEM((rows, LEAF), BF),
            pltpu.VMEM((TOP + 1, RANK, RANK), BF),
            pltpu.VMEM((LEAVES, RANK, LEAF), F32),
            pltpu.VMEM((4 * RANK, LEAF), F32),
            pltpu.SemaphoreType.DMA((7,)),
        ],
        compiler_params=pltpu.CompilerParams(vmem_limit_bytes=BIG),
        cost_estimate=pl.CostEstimate(flops=3_000_000_000, bytes_accessed=5_000_000, transcendentals=0),
        name="top_far",
    )(meta, mine, other, jnp.asarray(window_coupling(2)), jnp.asarray(window_coupling(3)), tree, sum0, sum1)


def join_body(north_ref, south_ref, west_ref, east_ref, north_any, south_any, to_north, to_south, sems):
    copies = []

    def move(source, at, to, row, count):
        copy = pltpu.make_async_copy(source.at[pl.ds(at, count)], to.at[pl.ds(row, count)], sems.at[len(copies)])
        copy.start()
        copies.append(copy)

    for own, to, lower in ((north_ref, to_north, 0), (south_ref, to_south, 1)):
        move(own, 0, to, 0, SIDEWAYS)
        for side, base in ((west_ref, SIDEWAYS), (east_ref, SIDEWAYS + CORNER)):
            move(side, 4 * RANK * lower, to, base, 4 * RANK)
            move(side, 8 * RANK, to, base + 4 * RANK, CORNER - 4 * RANK)
    backs = []
    for k, (held, to) in enumerate(((to_north, north_any), (to_south, south_any))):
        for copy in copies[5 * k : 5 * k + 5]:
            copy.wait()
        backs.append(pltpu.make_async_copy(held, to, sems.at[10 + k]))
        backs[-1].start()
    for back in backs:
        back.wait()


def join(north, south, west, east):
    anywhere = pl.BlockSpec(memory_space=pl.ANY)
    message = jax.ShapeDtypeStruct((SIDEWAYS + 2 * CORNER, LEAF), BF)
    return pl.pallas_call(
        join_body,
        out_shape=(message, message),
        in_specs=[anywhere] * 4,
        out_specs=[anywhere] * 2,
        scratch_shapes=[pltpu.VMEM(message.shape, BF)] * 2 + [pltpu.SemaphoreType.DMA((12,))],
        compiler_params=pltpu.CompilerParams(vmem_limit_bytes=BIG),
        cost_estimate=pl.CostEstimate(flops=0, bytes_accessed=4_000_000, transcendentals=0),
        name="join",
    )(north, south, west, east)


def kernel_of(target_x, target_y, source_x, source_y):
    gap_x = target_x - source_x
    gap_y = target_y - source_y
    squared = jnp.maximum(gap_x * gap_x + gap_y * gap_y, 1e-12)
    length = squared * lax.rsqrt(squared)
    phase = length - ((length + rounder) - rounder)
    w = 0.25 - jnp.abs(phase)
    s = w * w
    wave = w * (SINE[0] + s * (SINE[1] + s * SINE[2]))
    return (jnp.exp2(squared * short_rate) + jnp.exp2(squared * long_rate) * wave).astype(BF)


def spread_columns(rows, columns):
    turned = rows.T
    for k in range(columns.shape[1] // 128):
        columns[:, 128 * k : 128 * (k + 1)] = jnp.broadcast_to(turned[:, k : k + 1], (LEAF, 128))


def block_into(to, columns, points, shift_y, shift_x):
    source_x = (points[0:1] + shift_x.astype(F32)) * waves
    source_y = (points[1:2] + shift_y.astype(F32)) * waves
    rows = 32
    for i in range(0, LEAF, rows):
        for j in (0, 128):
            to[i : i + rows, j : j + 128] = kernel_of(
                columns[i : i + rows, 0:128],
                columns[i : i + rows, 128:256],
                jnp.broadcast_to(source_x[:, j : j + 128], (rows, 128)),
                jnp.broadcast_to(source_y[:, j : j + 128], (rows, 128)),
            )


def turn_points(columns, leaf, position, noise):
    rows = jnp.concatenate([position * waves, noise, jnp.zeros((5, LEAF), F32)], axis=0)
    spread_columns(rows, columns.at[leaf])


def repeat(count, at_once, step):
    def several(i, carry):
        for k in range(at_once):
            step(i * at_once + k)
        return carry

    lax.fori_loop(0, count // at_once, several, 0)
    for i in range(count // at_once * at_once, count):
        step(i)


def own_pairs(first, last):
    pairs = []
    for r in range(first, last):
        for c in range(SIDE):
            for dy, dx in ((0, 1), (1, -1), (1, 0), (1, 1)):
                if r + dy < SIDE and 0 <= c + dx < SIDE:
                    pairs.append((r * SIDE + c, (r + dy) * SIDE + c + dx, dy, dx))
    return pairs


def near_own_body(first, last, table_ref, q_any, pos_ref, noise_ref, *refs):
    before_any, out_any, columns, blocks, q_ref, before_ref, out_ref, sems = (None,) * (8 - len(refs)) + refs
    loads = [pltpu.make_async_copy(q_any, q_ref, sems.at[0])]
    if first:
        loads.append(pltpu.make_async_copy(before_any.at[pl.ds(SIDE, SIDE)], before_ref, sems.at[1]))
    for load in loads:
        load.start()
    pairs = own_pairs(first, last)
    start = first * SIDE
    count = (last - first) * SIDE

    def turn(leaf, carry):
        turn_points(columns, leaf, pos_ref[leaf], noise_ref[leaf])
        return carry

    lax.fori_loop(start, start + count, turn, 0)
    zero = jnp.int32(0)

    def single(i):
        block_into(blocks.at[i], columns.at[start + i], pos_ref[start + i], zero, zero)

    repeat(count, 4, single)

    def turned(i):
        blocks[count + 2 * i + 1] = blocks[count + 2 * i].T

    def pair(i):
        at = 4 * i
        place = count + 2 * i
        target, source = table_ref[at], table_ref[at + 1]
        block_into(blocks.at[place], columns.at[target], pos_ref[source], table_ref[at + 2], table_ref[at + 3])

    for i in range(4):
        pair(i)

    def four(i, carry):
        for k in range(4):
            turned(4 * i + k - 4)
        for k in range(4):
            pair(4 * i + k)
        return carry

    steps = len(pairs) // 4
    lax.fori_loop(1, steps, four, 0)
    for i in range(4 * steps - 4, 4 * steps):
        turned(i)
    for i in range(4 * steps, len(pairs)):
        pair(i)
        turned(i)
    for load in loads:
        load.wait()
    parts = {leaf: [(leaf - start, leaf)] for leaf in range(start, start + count)}
    for i, (target, source, _, _) in enumerate(pairs):
        parts[target].append((count + 2 * i, source))
        parts.setdefault(source, []).append((count + 1 + 2 * i, target))
    backs = []
    for leaf, terms in sorted(parts.items()):
        total = None
        for place, source in terms:
            part = dot(blocks[place], q_ref[source])
            total = part if total is None else total + part
        if leaf < start + count:
            noise = jnp.concatenate([columns[leaf, :, 256:384]] * 2, axis=1)
            total = total + noise * q_ref[leaf].astype(F32)
        if first and leaf < start + SIDE:
            total = total + before_ref[leaf - start]
        out_ref[leaf - start] = total
        backs.append(pltpu.make_async_copy(out_ref.at[leaf - start], out_any.at[leaf - start], sems.at[2 + leaf - start]))
        backs[-1].start()
    for back in backs:
        back.wait()


def near_own(first, last, q, points, noise, after, before):
    vmem = pl.BlockSpec(memory_space=pltpu.VMEM)
    smem = pl.BlockSpec(memory_space=pltpu.SMEM)
    anywhere = pl.BlockSpec(memory_space=pl.ANY)
    pairs = own_pairs(first, last)
    leaves = (min(last + 1, SIDE) - first) * SIDE

    def body(after_ref, *refs):
        near_own_body(first, last, *refs)

    return pl.pallas_call(
        body,
        out_shape=jax.ShapeDtypeStruct((leaves, LEAF, LEAF), F32),
        in_specs=[anywhere, smem, anywhere, vmem, vmem] + [anywhere] * len(before),
        out_specs=anywhere,
        scratch_shapes=[
            pltpu.VMEM((LEAVES, LEAF, 384), F32),
            pltpu.VMEM(((last - first) * SIDE + 2 * len(pairs), LEAF, LEAF), BF),
            pltpu.VMEM((LEAVES, LEAF, LEAF), BF),
            pltpu.VMEM((SIDE, LEAF, LEAF), F32),
            pltpu.VMEM((leaves, LEAF, LEAF), F32),
            pltpu.SemaphoreType.DMA((2 + leaves,)),
        ],
        compiler_params=pltpu.CompilerParams(vmem_limit_bytes=BIG),
        cost_estimate=pl.CostEstimate(flops=6_000_000_000, bytes_accessed=4_000_000, transcendentals=8_000_000),
        name="near_own",
    )(after, jnp.asarray(np.array(pairs, np.int32).reshape(-1)), q, points, noise, *before)


def edge_items():
    table = near_table(False)
    return [[leaf, *table[leaf, j]] for leaf in range(LEAVES) for j in range(5) if table[leaf, j, 0] >= 0]


ITEMS = edge_items()
EDGES = len(ITEMS)


def extra_of(list_ref, slot_ref, leaf):
    code = second_cycle(list_ref, leaf)
    place = (leaf // SIDE + code // 5) * 8 + leaf % SIDE + code % 5
    slot = slot_ref[jnp.where(code >= 0, place, 0)]
    return code, slot


def edge_body(
    half_at, list_ref, table_ref, slot_ref, after_ref, own_pos_ref, west_any, east_any, north_any, south_any, out_any,
    columns, parts, points, out_ref, sems,
):
    start = 8 * half_at
    copies = []
    sources = (
        (west_any, 12 * RANK),
        (east_any, 12 * RANK),
        (north_any, 12 * RANK),
        (north_any, SIDEWAYS + 8 * RANK),
        (north_any, SIDEWAYS + CORNER + 8 * RANK),
        (south_any, 12 * RANK),
        (south_any, SIDEWAYS + 8 * RANK),
        (south_any, SIDEWAYS + CORNER + 8 * RANK),
    )
    for k, (source, at) in enumerate(sources):
        copies.append(pltpu.make_async_copy(source.at[pl.ds(at, 48)], parts.at[k], sems.at[k]))
    for copy in copies:
        copy.start()

    def turn(leaf, carry):
        turn_points(columns, leaf, own_pos_ref[leaf], jnp.zeros((1, LEAF), F32))
        return carry

    lax.fori_loop(start, start + 8, turn, 0)
    points[0:LEAVES] = own_pos_ref[...]
    for copy in copies:
        copy.wait()
    slots = (16, 24, 32, 40, 44, 48, 56, 60)
    for k in range(8):
        whole = parts[k].astype(F32)
        whole = (whole[0:16] + whole[16:32]) + whole[32:48]
        first, count = {3: (4, 4), 4: (4, 4), 6: (0, 4), 7: (0, 4)}.get(k, (0, 8))
        for i in range(count):
            points[slots[k] + i] = whole[2 * (first + i) : 2 * (first + i) + 2]

    def fixed(i):
        at = 4 * i
        block_into(
            out_ref.at[i],
            columns.at[table_ref[at]],
            points[table_ref[at + 1]],
            table_ref[at + 2],
            table_ref[at + 3],
        )

    repeat(EDGES // 2, 4, fixed)
    backs = []
    for k, part in enumerate((pl.ds(0, EDGES // 2), pl.ds(EDGES // 2, 8))):
        backs.append(pltpu.make_async_copy(out_ref.at[part], out_any.at[part], sems.at[8 + k]))
    backs[0].start()

    def extra(i):
        code, slot = extra_of(list_ref, slot_ref, start + i)
        code = jnp.maximum(code, 0)
        block_into(out_ref.at[EDGES // 2 + i], columns.at[start + i], points[slot], code // 5 - 2, code % 5 - 2)

    repeat(8, 4, extra)
    backs[1].start()
    for back in backs:
        back.wait()


def edge_blocks(half_at, near_list, after, own_points, west, east, north, south):
    vmem = pl.BlockSpec(memory_space=pltpu.VMEM)
    smem = pl.BlockSpec(memory_space=pltpu.SMEM)
    anywhere = pl.BlockSpec(memory_space=pl.ANY)
    items = [item for item in ITEMS if item[0] // 8 == half_at]
    assert len(items) * 2 == EDGES

    def body(*refs):
        edge_body(half_at, *refs)

    return pl.pallas_call(
        body,
        out_shape=jax.ShapeDtypeStruct((EDGES // 2 + 8, LEAF, LEAF), BF),
        in_specs=[smem, smem, smem, anywhere, vmem] + [anywhere] * 4,
        out_specs=anywhere,
        scratch_shapes=[
            pltpu.VMEM((LEAVES, LEAF, 384), F32),
            pltpu.VMEM((8, 48, LEAF), BF),
            pltpu.VMEM((64, 2, LEAF), F32),
            pltpu.VMEM((EDGES // 2 + 8, LEAF, LEAF), BF),
            pltpu.SemaphoreType.DMA((10,)),
        ],
        compiler_params=pltpu.CompilerParams(vmem_limit_bytes=BIG),
        cost_estimate=pl.CostEstimate(flops=6_000_000_000, bytes_accessed=8_000_000, transcendentals=12_000_000),
        name="edge_blocks",
    )(
        near_list, jnp.asarray(np.array(items, np.int32).reshape(-1)), jnp.asarray(SLOT_OF), after, own_points,
        west, east, north, south,
    )


def final_body(
    list_ref, slot_ref, q_any, west_any, east_any, north_any, north_corner_any, south_any, south_corner_any,
    upper_blocks_any, lower_blocks_any, row0_any, row1_any, row2_any, basis_ref, field_ref, out_any, held, blocks, sums, outs, sems,
):
    firsts = [min(at for at in range(EDGES) if ITEMS[at][0] // SIDE == r) for r in range(SIDE)] + [EDGES]
    stages = [[], [], [], []]
    count = 0

    def copy(stage, source, at, rows, to, row):
        nonlocal count
        made = pltpu.make_async_copy(source.at[pl.ds(at, rows)], to.at[pl.ds(row, rows)], sems.at[count])
        count += 1
        stages[stage].append(made)

    copy(0, north_any, 0, 8, held, 32)
    copy(0, north_corner_any, 0, 8, held, 40)
    for stage, low, high in ((0, 0, 3), (1, 3, 4)):
        copy(stage, west_any, 2 * low, 2 * (high - low), held, 16 + 2 * low)
        copy(stage, east_any, 2 * low, 2 * (high - low), held, 24 + 2 * low)
        copy(stage, q_any, 4 * low, 4 * (high - low), held, 4 * low)
    copy(2, south_any, 0, 8, held, 48)
    copy(2, south_corner_any, 0, 8, held, 56)
    for r in range(SIDE):
        source = upper_blocks_any if r < 2 else lower_blocks_any
        back = 0 if r < 2 else EDGES // 2
        copy(r, source, firsts[r] - back, firsts[r + 1] - firsts[r], blocks, firsts[r])
        copy(r, source, EDGES // 2 + SIDE * (r % 2), SIDE, blocks, EDGES + SIDE * r)
        copy(r, (row0_any, row1_any, row2_any, row2_any)[r], SIDE if r == 3 else 0, SIDE, sums, SIDE * r)
    backs = []
    for r in range(SIDE):
        part = pl.ds(SIDE * r, SIDE)
        backs.append(pltpu.make_async_copy(outs.at[part], out_any.at[part], sems.at[count + r]))
    for r in range(2):
        for made in stages[r]:
            made.start()
    for leaf in range(LEAVES):
        if leaf % SIDE == 0:
            for made in stages[leaf // SIDE]:
                made.wait()
            if leaf // SIDE + 2 < SIDE:
                for made in stages[leaf // SIDE + 2]:
                    made.start()
        total = dot_first(basis_ref[leaf], field_ref[leaf])
        for at in range(EDGES):
            if ITEMS[at][0] == leaf:
                total = total + dot(blocks[at], held[ITEMS[at][1]])
        total = total + sums[leaf]
        sums[leaf] = total
        outs[leaf] = total.astype(BF)
        code, slot = extra_of(list_ref, slot_ref, leaf)

        @pl.when(code >= 0)
        def _(leaf=leaf, slot=slot):
            outs[leaf] = (sums[leaf] + dot(blocks[EDGES + leaf], held[slot])).astype(BF)

        if leaf % SIDE == SIDE - 1:
            backs[leaf // SIDE].start()
    for back in backs:
        back.wait()


def finish(near_list, q, halos, upper_blocks, lower_blocks, sums, basis, field):
    vmem = pl.BlockSpec(memory_space=pltpu.VMEM)
    smem = pl.BlockSpec(memory_space=pltpu.SMEM)
    anywhere = pl.BlockSpec(memory_space=pl.ANY)

    return pl.pallas_call(
        final_body,
        out_shape=jax.ShapeDtypeStruct((LEAVES, LEAF, LEAF), BF),
        in_specs=[smem, smem] + [anywhere] * 12 + [vmem, vmem],
        out_specs=anywhere,
        scratch_shapes=[
            pltpu.VMEM((64, LEAF, LEAF), BF),
            pltpu.VMEM((EDGES + LEAVES, LEAF, LEAF), BF),
            pltpu.VMEM((LEAVES, LEAF, LEAF), F32),
            pltpu.VMEM((LEAVES, LEAF, LEAF), BF),
            pltpu.SemaphoreType.DMA((28,)),
        ],
        compiler_params=pltpu.CompilerParams(vmem_limit_bytes=BIG),
        cost_estimate=pl.CostEstimate(flops=4_000_000_000, bytes_accessed=24_000_000, transcendentals=0),
        name="finish",
    )(near_list, jnp.asarray(SLOT_OF), q, *halos, upper_blocks, lower_blocks, *sums, basis, field)


def window_slots(wide, narrow, steps):
    row, col = lax.axis_index("narrow"), lax.axis_index("wide")
    wy, wx = np.arange(WINDOW) // 6, np.arange(WINDOW) % 6

    def slots(target_y, target_x, scale):
        y = target_y // 2 * 2 - 2 + wy
        x = target_x // 2 * 2 - 2 + wx
        inside = (y >= 0) & (y < narrow // scale) & (x >= 0) & (x < wide // scale)
        apart = {"narrow": (y * scale) ^ row, "wide": (x * scale) ^ col}
        slot = 0
        for at, (axis, bit) in enumerate(steps):
            slot = slot + (apart[axis] // bit & 1) * (1 << at)
        return jnp.where(inside, slot if scale == 1 else slot // 4, -1)

    parity2 = row % 2 * 2 + col % 2
    parity3 = row // 2 % 2 * 2 + col // 2 % 2
    return jnp.concatenate(
        [slots(row, col, 1), slots(row // 2, col // 2, 2), jnp.stack([parity2, parity3])]
    ).astype(jnp.int32)


def per_device(wide, narrow, charges, positions, noise, leaf_basis, transfer, near_list):
    q = charges.reshape(LEAVES, LEAF, LEAF)
    points = positions.reshape(LEAVES, 2, LEAF)
    basis = leaf_basis.reshape(LEAVES, RANK, LEAF)
    tree = transfer[0, 0]
    code_y, code_x = near_list // 5, near_list % 5
    outer = (near_list >= 0) & ((code_y == 0) | (code_y == 4) | (code_x == 0) | (code_x == 4))
    listing = jnp.max(jnp.where(outer, near_list, -1), axis=-1).reshape(-1)
    steps = gather_steps(wide, narrow)
    meta = window_slots(wide, narrow, steps)

    east, west, north, south, coefs, give, to_east, to_west, q_up, q_down = go_up(q, basis, tree, points)
    from_west = shift(east, "wide", 1)
    from_east = shift(west, "wide", -1)
    q_north = shift(q_down, "narrow", 1)
    q_south = shift(q_up, "narrow", -1)

    noise_rows = noise.reshape(LEAVES, 1, LEAF)

    def step(value, at):
        axis, bit = steps[at]
        return lax.ppermute(value, axis, [(i, i ^ bit) for i in range(lax.axis_size(axis))])

    def tie(*values):
        return lax.optimization_barrier(values)

    gathered = give
    other = step(gathered, 0)
    row0 = near_own(0, 1, q, points, noise_rows, give, [])
    other, row0 = tie(other, row0)
    gathered = jnp.concatenate([gathered, other], axis=0)
    other = step(gathered, 1)
    row1 = near_own(1, 2, q, points, noise_rows, gathered, [row0])
    other, from_west, from_east, row1, to_east, to_west, q_north, q_south = tie(
        other, from_west, from_east, row1, to_east, to_west, q_north, q_south
    )
    gathered = jnp.concatenate([gathered, other], axis=0)
    other = step(gathered, 2)
    to_north, to_south = join(north, south, from_west, from_east)
    from_south = shift(to_north, "narrow", -1)
    from_north = shift(to_south, "narrow", 1)
    q_west = shift(to_east, "wide", 1)
    q_east = shift(to_west, "wide", -1)
    row2 = near_own(2, 4, q, points, noise_rows, to_north, [row1])
    other, from_south, from_north, row2 = tie(other, from_south, from_north, row2)
    gathered = jnp.concatenate([gathered, other], axis=0)
    other = step(gathered, 3)
    sums = local_far(listing, coefs, from_west, from_east, from_north, from_south)
    upper_blocks = edge_blocks(0, listing, sums[1], points, from_west, from_east, from_north, from_south)
    other, upper_blocks = tie(other, upper_blocks)
    for at in range(4, len(steps)):
        gathered = jnp.concatenate([gathered, other], axis=0)
        other = step(gathered, at)
        if at == 4:
            lower_blocks = edge_blocks(1, listing, upper_blocks, points, from_west, from_east, from_north, from_south)
            other, lower_blocks, q_west, q_east = tie(other, lower_blocks, q_west, q_east)
            q_north_corner = shift(jnp.stack([q_west[4:8], q_east[4:8]]), "narrow", 1)
            q_south_corner = shift(jnp.stack([q_west[0:4], q_east[0:4]]), "narrow", -1)
    field = top_far(meta, gathered, other, tree, *sums)
    q_north_corner, q_south_corner, field = tie(q_north_corner, q_south_corner, field)
    halos = [
        value.reshape(8, LEAF, LEAF)
        for value in (q_west, q_east, q_north, q_north_corner, q_south, q_south_corner)
    ]
    out = finish(listing, q, halos, upper_blocks, lower_blocks, (row0, row1, row2), basis, field)
    return out.reshape(SIDE, SIDE, LEAF, LEAF)


def solution(mesh):
    wide, narrow = mesh.shape["wide"], mesh.shape["narrow"]
    in_specs = (
        P("narrow", "wide", None, None),
        P("narrow", "wide", None, None),
        P("narrow", "wide", None),
        P("narrow", "wide", None, None),
        P("narrow", "wide", None, None, None),
        P("narrow", "wide", None),
    )
    out_specs = P("narrow", "wide", None, None)

    def step(*arrays):
        return per_device(wide, narrow, *arrays)

    return jax.shard_map(step, mesh=mesh, in_specs=in_specs, out_specs=out_specs, check_vma=False)
```

```python
import math

import jax
import jax.numpy as jnp
import ml_dtypes
import numpy as np
from jax import lax
from jax.experimental import pallas as pl
from jax.experimental.pallas import tpu as pltpu
from jax.sharding import PartitionSpec as P

LEAF = 256
CHEB = 8
RANK = 64
NEAR = 10
SIDE = 4
LEAVES = SIDE * SIDE
TOP = 20
WINDOW = 36
PACK = RANK + 16
SIDEWAYS = 8 * RANK + 4 * RANK + 48
CORNER = 4 * RANK + 4 * RANK + 48
BIG = 58 << 20
COPIES = 42
BF = jnp.bfloat16
F32 = jnp.float32

short_len = 0.125
long_weight = 0.03125
reach = 3.0 * SIDE
waves = 10.0
LOG2E = math.log2(math.e)
long_rate = -0.5 / (reach * reach) * LOG2E / (waves * waves)
short_rate = -0.5 / (short_len * short_len) * LOG2E / (waves * waves)
rounder = 1.5 * 2.0**23


def sine_terms(count):
    w = np.cos(np.pi * (np.arange(2000) + 0.5) / 2000) * 0.25
    powers = np.stack([w ** (2 * i + 1) for i in range(count)], 1)
    return [float(c) for c in np.linalg.lstsq(powers, np.sin(2 * np.pi * w) * long_weight, rcond=None)[0]]


SINE = sine_terms(3)


def coupling(height, shift_y, shift_x):
    points = 0.5 * (1.0 + np.cos((2.0 * np.arange(CHEB) + 1.0) * (math.pi / (2.0 * CHEB))))
    node_x = np.tile(points, CHEB)
    node_y = np.repeat(points, CHEB)
    gap_x = (node_x[:, None] - node_x[None, :] - shift_x) * 2.0**height
    gap_y = (node_y[:, None] - node_y[None, :] - shift_y) * 2.0**height
    squared = gap_x * gap_x + gap_y * gap_y
    return np.exp(squared * (-0.5 / (short_len * short_len))) + long_weight * np.exp(
        squared * (-0.5 / (reach * reach))
    ) * np.cos(2.0 * math.pi * waves * np.sqrt(squared))


def window_coupling(height):
    table = np.zeros((2, 2, RANK, 6, 6, RANK))
    for py in range(2):
        for px in range(2):
            for wy in range(6):
                for wx in range(6):
                    shift_y, shift_x = wy - 2 - py, wx - 2 - px
                    if max(abs(shift_y), abs(shift_x)) >= 2:
                        table[py, px, :, wy, wx] = coupling(height, shift_y, shift_x)
    return table.reshape(4 * RANK, WINDOW * RANK).astype(ml_dtypes.bfloat16)


def code_coupling():
    return np.stack([coupling(0, code // 5 - 2, code % 5 - 2) for code in range(25)]).astype(ml_dtypes.bfloat16)


def halo_slot(row, col):
    if 0 <= row < 4 and 0 <= col < 4:
        return row * 4 + col
    if 0 <= row < 4:
        return 16 + row * 2 + col + 2 if col < 0 else 24 + row * 2 + col - 4
    base, r = (32, row + 2) if row < 0 else (48, row - 4)
    if 0 <= col < 4:
        return base + r * 4 + col
    return base + 8 + r * 2 + col + 2 if col < 0 else base + 12 + r * 2 + col - 4


SLOT_OF = np.array([halo_slot(r - 2, c - 2) for r in range(8) for c in range(8)], np.int32)


def near_table(own):
    width = 9 if own else 5
    table = np.zeros((LEAVES, width, 3), np.int32)
    table[:, :, 0] = -1
    for r in range(SIDE):
        for c in range(SIDE):
            at = 0
            for dy in (-1, 0, 1):
                for dx in (-1, 0, 1):
                    slot = halo_slot(r + dy, c + dx)
                    if (slot < LEAVES) == own:
                        table[r * SIDE + c, at] = (slot, dy, dx)
                        at += 1
    return table


def bits(count):
    return [1 << i for i in range(count.bit_length() - 1)]


def gather_steps(wide, narrow):
    return (
        [("wide", 1), ("narrow", 1)]
        + [("wide", b) for b in reversed(bits(wide)[1:])]
        + [("narrow", b) for b in reversed(bits(narrow)[1:])]
    )


def shift(value, axis, steps):
    count = lax.axis_size(axis)
    return lax.ppermute(value, axis, [(i, i + steps) for i in range(count) if 0 <= i + steps < count])


def dot(a, b):
    return jnp.dot(a, b, preferred_element_type=F32)


def dot_first(a, b):
    return lax.dot_general(a, b, (((0,), (0,)), ((), ())), preferred_element_type=F32)


def up_body(
    q_any, basis_any, tree_any, pos_ref, east_ref, west_ref, north_ref, south_ref, coef_ref, give_ref, to_east, to_west, to_north, to_south,
    q_ref, basis_ref, tree_ref, sems
):
    loads = []
    for k in range(4):
        part = pl.ds(4 * k, 4)
        loads.append(pltpu.make_async_copy(basis_any.at[part], basis_ref.at[part], sems.at[2 * k]))
        loads.append(pltpu.make_async_copy(q_any.at[part], q_ref.at[part], sems.at[2 * k + 1]))
    loads.append(pltpu.make_async_copy(tree_any, tree_ref, sems.at[8]))
    for load in loads:
        load.start()
    backs = []
    level0 = []
    for leaf in range(LEAVES):
        if leaf % 4 == 0:
            loads[leaf // 2].wait()
            loads[leaf // 2 + 1].wait()
            half = pl.ds(leaf // 2, 2)
            for to, low in ((to_west, leaf), (to_east, leaf + 2)):
                backs.append(pltpu.make_async_copy(q_ref.at[pl.ds(low, 2)], to.at[half], sems.at[9 + len(backs)]))
                backs[-1].start()
            to, row = (to_north, leaf) if leaf < 8 else (to_south, leaf - 8)
            backs.append(pltpu.make_async_copy(q_ref.at[pl.ds(leaf, 4)], to.at[pl.ds(row, 4)], sems.at[9 + len(backs)]))
            backs[-1].start()
        coef = dot(basis_ref[leaf], q_ref[leaf]).astype(BF)
        level0.append(coef)
        r, c = leaf // SIDE, leaf % SIDE
        coef_ref[leaf * RANK : (leaf + 1) * RANK] = coef
        ref, at = (west_ref, r * 2 + c) if c < 2 else (east_ref, r * 2 + c - 2)
        ref[at * RANK : (at + 1) * RANK] = coef
        ref, at = (north_ref, r * 4 + c) if r < 2 else (south_ref, r * 4 + c - 8)
        ref[at * RANK : (at + 1) * RANK] = coef
    loads[8].wait()
    level1 = []
    for r in range(2):
        for c in range(2):
            total = None
            for dr in range(2):
                for dc in range(2):
                    leaf = (2 * r + dr) * SIDE + 2 * c + dc
                    part = dot(tree_ref[leaf], level0[leaf])
                    total = part if total is None else total + part
            coef = total.astype(BF)
            at = r * 2 + c
            level1.append(coef)
            coef_ref[(LEAVES + at) * RANK : (LEAVES + at + 1) * RANK] = coef
            for ref in (east_ref, west_ref, north_ref, south_ref):
                ref[(8 + at) * RANK : (9 + at) * RANK] = coef
    total = None
    for at in range(4):
        part = dot(tree_ref[LEAVES + at], level1[at])
        total = part if total is None else total + part
    give_ref[0:RANK] = total.astype(BF)
    top = tree_ref[TOP]
    give_ref[RANK:PACK] = jnp.concatenate([top[16 * k : 16 * k + 16] for k in range(4)], axis=1)
    for ref, leaves in (
        (west_ref, [r * 4 + c for r in range(4) for c in (0, 1)]),
        (east_ref, [r * 4 + c for r in range(4) for c in (2, 3)]),
        (north_ref, range(8)),
        (south_ref, range(8, 16)),
    ):
        rest = jnp.concatenate([pos_ref[leaf] for leaf in leaves], axis=0)
        for part in range(3):
            held = rest.astype(BF)
            at = 12 * RANK + 16 * part
            ref[at : at + 16] = held
            rest = rest - held.astype(F32)
    for back in backs:
        back.wait()


def go_up(q, basis, tree, points):
    vmem = pl.BlockSpec(memory_space=pltpu.VMEM)
    side = jax.ShapeDtypeStruct((SIDEWAYS, LEAF), BF)
    return pl.pallas_call(
        up_body,
        out_shape=(
            side,
            side,
            side,
            side,
            jax.ShapeDtypeStruct(((LEAVES + 4) * RANK, LEAF), BF),
            jax.ShapeDtypeStruct((PACK, LEAF), BF),
        )
        + (jax.ShapeDtypeStruct((8, LEAF, LEAF), BF),) * 4,
        in_specs=[pl.BlockSpec(memory_space=pl.ANY)] * 3 + [vmem],
        out_specs=[vmem] * 6 + [pl.BlockSpec(memory_space=pl.ANY)] * 4,
        scratch_shapes=[
            pltpu.VMEM((LEAVES, LEAF, LEAF), BF),
            pltpu.VMEM((LEAVES, RANK, LEAF), BF),
            pltpu.VMEM((TOP + 1, RANK, RANK), BF),
            pltpu.SemaphoreType.DMA((21,)),
        ],
        compiler_params=pltpu.CompilerParams(vmem_limit_bytes=BIG),
        cost_estimate=pl.CostEstimate(flops=300_000_000, bytes_accessed=5_000_000, transcendentals=0),
        name="upward",
    )(q, basis, tree, points)


def local_body(
    list_ref, coef_any, west_any, east_any, north_any, south_any, c0_any, c1_any, code_any, sum0, sum1, pad0, pad1, c0_ref, c1_ref, code_ref, sems
):
    loads = []

    def load(source, at, to, row, count):
        rows = pl.ds(at * RANK if at < 100 else at, count * RANK)
        copy = pltpu.make_async_copy(source.at[rows], to.at[pl.ds(row, count * RANK)], sems.at[len(loads)])
        copy.start()
        loads.append(copy)

    def put(pad, extent, row, col, ref, at, count):
        load(ref, at, pad, ((row + 2) * (extent + 4) + col + 2) * RANK, count)

    whole = []
    for k, (source, to) in enumerate(((c0_any, c0_ref), (c1_any, c1_ref), (code_any, code_ref))):
        whole.append(pltpu.make_async_copy(source, to, sems.at[COPIES + k]))
    whole[0].start()
    for r in range(4):
        put(pad0, 4, r, 0, coef_any, r * 4, 4)
        put(pad0, 4, r, -2, west_any, r * 2, 2)
        put(pad0, 4, r, 4, east_any, r * 2, 2)
    for ref, row in ((north_any, -2), (south_any, 4)):
        for r in range(2):
            put(pad0, 4, row + r, 0, ref, r * 4, 4)
            for col, base in ((-2, SIDEWAYS), (4, SIDEWAYS + CORNER)):
                load(ref, base + r * 2 * RANK, pad0, ((row + r + 2) * 8 + col + 2) * RANK, 2)
    split = len(loads)
    for copy in whole[1:]:
        copy.start()
    for r in range(2):
        put(pad1, 2, r, 0, coef_any, LEAVES + r * 2, 2)
        put(pad1, 2, r, -2, west_any, 8 + r * 2, 2)
        put(pad1, 2, r, 2, east_any, 8 + r * 2, 2)
    for ref, row in ((north_any, -2), (south_any, 2)):
        for r in range(2):
            put(pad1, 2, row + r, 0, ref, 8 + r * 2, 2)
            for col, base in ((-2, SIDEWAYS), (2, SIDEWAYS + CORNER)):
                load(ref, base + (4 + r * 2) * RANK, pad1, ((row + r + 2) * 6 + col + 2) * RANK, 2)
    whole[0].wait()
    for copy in loads[:split]:
        copy.wait()
    for a in range(2):
        for b in range(2):
            total = None
            for wy in range(6):
                at = ((2 * a + wy) * 8 + 2 * b) * RANK
                part = dot(c0_ref[:, wy * 6 * RANK : (wy + 1) * 6 * RANK], pad0[at : at + 6 * RANK])
                total = part if total is None else total + part
            for child in range(4):
                leaf = (2 * a + child // 2) * SIDE + 2 * b + child % 2
                sum0[leaf] = total[child * RANK : (child + 1) * RANK]
    for copy in loads[split:] + whole[1:]:
        copy.wait()

    def listed(leaf, carry):
        code = second_cycle(list_ref, leaf)

        @pl.when(code >= 0)
        def _():
            row = leaf // SIDE + code // 5
            col = leaf % SIDE + code % 5
            at = pl.multiple_of((row * 8 + col) * RANK, RANK)
            sum0[leaf] = sum0[leaf] - dot(code_ref[code], pad0[pl.ds(at, RANK)])

        return carry

    lax.fori_loop(0, LEAVES, listed, 0)
    sum1[...] = dot(c1_ref[...], pad1[...])


def local_far(near_list, coefs, west, east, north, south):
    vmem = pl.BlockSpec(memory_space=pltpu.VMEM)
    smem = pl.BlockSpec(memory_space=pltpu.SMEM)
    return pl.pallas_call(
        local_body,
        out_shape=(
            jax.ShapeDtypeStruct((LEAVES, RANK, LEAF), F32),
            jax.ShapeDtypeStruct((4 * RANK, LEAF), F32),
        ),
        in_specs=[smem] + [pl.BlockSpec(memory_space=pl.ANY)] * 8,
        out_specs=[vmem] * 2,
        scratch_shapes=[
            pltpu.VMEM((64 * RANK, LEAF), BF),
            pltpu.VMEM((WINDOW * RANK, LEAF), BF),
            pltpu.VMEM((4 * RANK, WINDOW * RANK), BF),
            pltpu.VMEM((4 * RANK, WINDOW * RANK), BF),
            pltpu.VMEM((25, RANK, RANK), BF),
            pltpu.SemaphoreType.DMA((COPIES + 3,)),
        ],
        compiler_params=pltpu.CompilerParams(vmem_limit_bytes=BIG),
        cost_estimate=pl.CostEstimate(flops=5_000_000_000, bytes_accessed=8_000_000, transcendentals=0),
        name="local_far",
    )(
        near_list,
        coefs,
        west,
        east,
        north,
        south,
        jnp.asarray(window_coupling(0)),
        jnp.asarray(window_coupling(1)),
        jnp.asarray(code_coupling()),
    )


def top_body(
    meta_ref, mine_any, other_any, c2_any, c3_any, tree_any, sum0_any, sum1_any, field_ref, win, parents, c2_ref, c3_ref, all_ref, tree_ref, sum0, sum1, sems
):
    loads = []
    for k, (source, to) in enumerate(((mine_any, all_ref.at[pl.ds(0, mine_any.shape[0])]), (other_any, all_ref.at[pl.ds(mine_any.shape[0], mine_any.shape[0])]), (tree_any, tree_ref), (sum1_any, sum1), (sum0_any, sum0))):
        loads.append(pltpu.make_async_copy(source, to, sems.at[2 + k]))
        loads[-1].start()

    def slab(source, to, at):
        part = pl.ds(pl.multiple_of(meta_ref[2 * WINDOW + at] * RANK, RANK), RANK)
        copy = pltpu.make_async_copy(source.at[part], to, sems.at[at])
        copy.start()
        return copy

    slabs = [slab(c2_any, c2_ref, 0), slab(c3_any, c3_ref, 1)]

    loads[0].wait()
    loads[1].wait()

    def lift(group, carry):
        total = jnp.zeros((RANK, LEAF), F32)
        for child in range(4):
            at = pl.multiple_of((group * 4 + child) * PACK, 16)
            packed = all_ref[pl.ds(at + RANK, 16)]
            matrix = jnp.concatenate([packed[:, k * RANK : (k + 1) * RANK] for k in range(4)], axis=0)
            total = total + dot(matrix, all_ref[pl.ds(at, RANK)])
        parents[pl.ds(pl.multiple_of(group * RANK, RANK), RANK)] = total.astype(BF)
        return carry

    lax.fori_loop(0, parents.shape[0] // RANK, lift, 0)

    def fill(start, source, stride):
        for i in range(WINDOW):
            slot = meta_ref[start + i]
            at = pl.multiple_of(jnp.maximum(slot, 0) * stride, 16)
            kept = jnp.where(slot >= 0, 1.0, 0.0).astype(BF)
            win[i * RANK : (i + 1) * RANK] = source[pl.ds(at, RANK)] * kept

    fill(WINDOW, parents, RANK)
    slabs[1].wait()
    field3 = dot(c3_ref[...], win[...]).astype(BF)
    fill(0, all_ref, PACK)
    slabs[0].wait()
    for load in loads[2:]:
        load.wait()
    field2 = (dot(c2_ref[...], win[...]) + dot_first(tree_ref[TOP], field3)).astype(BF)
    field1 = []
    for at in range(4):
        field1.append(
            (sum1[at * RANK : (at + 1) * RANK] + dot_first(tree_ref[LEAVES + at], field2)).astype(BF)
        )
    for leaf in range(LEAVES):
        above = field1[leaf // SIDE // 2 * 2 + leaf % SIDE // 2]
        field_ref[leaf] = (sum0[leaf] + dot_first(tree_ref[leaf], above)).astype(BF)


def second_cycle(list_ref, leaf):
    return list_ref[leaf]


def top_far(meta, mine, other, tree, sum0, sum1):
    vmem = pl.BlockSpec(memory_space=pltpu.VMEM)
    smem = pl.BlockSpec(memory_space=pltpu.SMEM)
    anywhere = pl.BlockSpec(memory_space=pl.ANY)
    rows = 2 * mine.shape[0]
    devices = rows // PACK
    return pl.pallas_call(
        top_body,
        out_shape=jax.ShapeDtypeStruct((LEAVES, RANK, LEAF), BF),
        in_specs=[smem] + [anywhere] * 7,
        out_specs=vmem,
        scratch_shapes=[
            pltpu.VMEM((WINDOW * RANK, LEAF), BF),
            pltpu.VMEM((devices // 4 * RANK, LEAF), BF),
            pltpu.VMEM((RANK, WINDOW * RANK), BF),
            pltpu.VMEM((RANK, WINDOW * RANK), BF),
            pltpu.VMEM((rows, LEAF), BF),
            pltpu.VMEM((TOP + 1, RANK, RANK), BF),
            pltpu.VMEM((LEAVES, RANK, LEAF), F32),
            pltpu.VMEM((4 * RANK, LEAF), F32),
            pltpu.SemaphoreType.DMA((7,)),
        ],
        compiler_params=pltpu.CompilerParams(vmem_limit_bytes=BIG),
        cost_estimate=pl.CostEstimate(flops=3_000_000_000, bytes_accessed=5_000_000, transcendentals=0),
        name="top_far",
    )(meta, mine, other, jnp.asarray(window_coupling(2)), jnp.asarray(window_coupling(3)), tree, sum0, sum1)


def join_body(north_ref, south_ref, west_ref, east_ref, north_any, south_any, to_north, to_south, sems):
    copies = []

    def move(source, at, to, row, count):
        copy = pltpu.make_async_copy(source.at[pl.ds(at, count)], to.at[pl.ds(row, count)], sems.at[len(copies)])
        copy.start()
        copies.append(copy)

    for own, to, lower in ((north_ref, to_north, 0), (south_ref, to_south, 1)):
        move(own, 0, to, 0, SIDEWAYS)
        for side, base in ((west_ref, SIDEWAYS), (east_ref, SIDEWAYS + CORNER)):
            move(side, 4 * RANK * lower, to, base, 4 * RANK)
            move(side, 8 * RANK, to, base + 4 * RANK, CORNER - 4 * RANK)
    backs = []
    for k, (held, to) in enumerate(((to_north, north_any), (to_south, south_any))):
        for copy in copies[5 * k : 5 * k + 5]:
            copy.wait()
        backs.append(pltpu.make_async_copy(held, to, sems.at[10 + k]))
        backs[-1].start()
    for back in backs:
        back.wait()


def join(north, south, west, east):
    anywhere = pl.BlockSpec(memory_space=pl.ANY)
    message = jax.ShapeDtypeStruct((SIDEWAYS + 2 * CORNER, LEAF), BF)
    return pl.pallas_call(
        join_body,
        out_shape=(message, message),
        in_specs=[anywhere] * 4,
        out_specs=[anywhere] * 2,
        scratch_shapes=[pltpu.VMEM(message.shape, BF)] * 2 + [pltpu.SemaphoreType.DMA((12,))],
        compiler_params=pltpu.CompilerParams(vmem_limit_bytes=BIG),
        cost_estimate=pl.CostEstimate(flops=0, bytes_accessed=4_000_000, transcendentals=0),
        name="join",
    )(north, south, west, east)


def kernel_of(target_x, target_y, source_x, source_y):
    gap_x = target_x - source_x
    gap_y = target_y - source_y
    squared = jnp.maximum(gap_x * gap_x + gap_y * gap_y, 1e-12)
    length = squared * lax.rsqrt(squared)
    phase = length - ((length + rounder) - rounder)
    w = 0.25 - jnp.abs(phase)
    s = w * w
    wave = w * (SINE[0] + s * (SINE[1] + s * SINE[2]))
    return (jnp.exp2(squared * short_rate) + jnp.exp2(squared * long_rate) * wave).astype(BF)


def spread_columns(rows, columns):
    turned = rows.T
    for k in range(columns.shape[1] // 128):
        columns[:, 128 * k : 128 * (k + 1)] = jnp.broadcast_to(turned[:, k : k + 1], (LEAF, 128))


def block_into(to, columns, points, shift_y, shift_x):
    source_x = (points[0:1] + shift_x.astype(F32)) * waves
    source_y = (points[1:2] + shift_y.astype(F32)) * waves
    rows = 32
    for i in range(0, LEAF, rows):
        for j in (0, 128):
            to[i : i + rows, j : j + 128] = kernel_of(
                columns[i : i + rows, 0:128],
                columns[i : i + rows, 128:256],
                jnp.broadcast_to(source_x[:, j : j + 128], (rows, 128)),
                jnp.broadcast_to(source_y[:, j : j + 128], (rows, 128)),
            )


def turn_points(columns, leaf, position, noise):
    rows = jnp.concatenate([position * waves, noise, jnp.zeros((5, LEAF), F32)], axis=0)
    spread_columns(rows, columns.at[leaf])


def repeat(count, at_once, step):
    def several(i, carry):
        for k in range(at_once):
            step(i * at_once + k)
        return carry

    lax.fori_loop(0, count // at_once, several, 0)
    for i in range(count // at_once * at_once, count):
        step(i)


def own_pairs(first, last):
    pairs = []
    for r in range(first, last):
        for c in range(SIDE):
            for dy, dx in ((0, 1), (1, -1), (1, 0), (1, 1)):
                if r + dy < SIDE and 0 <= c + dx < SIDE:
                    pairs.append((r * SIDE + c, (r + dy) * SIDE + c + dx, dy, dx))
    return pairs


def near_own_body(first, last, table_ref, q_any, pos_ref, noise_ref, *refs):
    before_any, out_any, columns, blocks, q_ref, before_ref, out_ref, sems = (None,) * (8 - len(refs)) + refs
    loads = [pltpu.make_async_copy(q_any, q_ref, sems.at[0])]
    if first:
        loads.append(pltpu.make_async_copy(before_any.at[pl.ds(SIDE, SIDE)], before_ref, sems.at[1]))
    for load in loads:
        load.start()
    pairs = own_pairs(first, last)
    start = first * SIDE
    count = (last - first) * SIDE

    def turn(leaf, carry):
        turn_points(columns, leaf, pos_ref[leaf], noise_ref[leaf])
        return carry

    lax.fori_loop(start, start + count, turn, 0)
    zero = jnp.int32(0)

    def single(i):
        block_into(blocks.at[i], columns.at[start + i], pos_ref[start + i], zero, zero)

    repeat(count, 4, single)

    def turned(i):
        blocks[count + 2 * i + 1] = blocks[count + 2 * i].T

    def pair(i):
        at = 4 * i
        place = count + 2 * i
        target, source = table_ref[at], table_ref[at + 1]
        block_into(blocks.at[place], columns.at[target], pos_ref[source], table_ref[at + 2], table_ref[at + 3])

    for i in range(4):
        pair(i)

    def four(i, carry):
        for k in range(4):
            turned(4 * i + k - 4)
        for k in range(4):
            pair(4 * i + k)
        return carry

    steps = len(pairs) // 4
    lax.fori_loop(1, steps, four, 0)
    for i in range(4 * steps - 4, 4 * steps):
        turned(i)
    for i in range(4 * steps, len(pairs)):
        pair(i)
        turned(i)
    for load in loads:
        load.wait()
    parts = {leaf: [(leaf - start, leaf)] for leaf in range(start, start + count)}
    for i, (target, source, _, _) in enumerate(pairs):
        parts[target].append((count + 2 * i, source))
        parts.setdefault(source, []).append((count + 1 + 2 * i, target))
    backs = []
    for leaf, terms in sorted(parts.items()):
        total = None
        for place, source in terms:
            part = dot(blocks[place], q_ref[source])
            total = part if total is None else total + part
        if leaf < start + count:
            noise = jnp.concatenate([columns[leaf, :, 256:384]] * 2, axis=1)
            total = total + noise * q_ref[leaf].astype(F32)
        if first and leaf < start + SIDE:
            total = total + before_ref[leaf - start]
        out_ref[leaf - start] = total
        backs.append(pltpu.make_async_copy(out_ref.at[leaf - start], out_any.at[leaf - start], sems.at[2 + leaf - start]))
        backs[-1].start()
    for back in backs:
        back.wait()


def near_own(first, last, q, points, noise, after, before):
    vmem = pl.BlockSpec(memory_space=pltpu.VMEM)
    smem = pl.BlockSpec(memory_space=pltpu.SMEM)
    anywhere = pl.BlockSpec(memory_space=pl.ANY)
    pairs = own_pairs(first, last)
    leaves = (min(last + 1, SIDE) - first) * SIDE

    def body(after_ref, *refs):
        near_own_body(first, last, *refs)

    return pl.pallas_call(
        body,
        out_shape=jax.ShapeDtypeStruct((leaves, LEAF, LEAF), F32),
        in_specs=[anywhere, smem, anywhere, vmem, vmem] + [anywhere] * len(before),
        out_specs=anywhere,
        scratch_shapes=[
            pltpu.VMEM((LEAVES, LEAF, 384), F32),
            pltpu.VMEM(((last - first) * SIDE + 2 * len(pairs), LEAF, LEAF), BF),
            pltpu.VMEM((LEAVES, LEAF, LEAF), BF),
            pltpu.VMEM((SIDE, LEAF, LEAF), F32),
            pltpu.VMEM((leaves, LEAF, LEAF), F32),
            pltpu.SemaphoreType.DMA((2 + leaves,)),
        ],
        compiler_params=pltpu.CompilerParams(vmem_limit_bytes=BIG),
        cost_estimate=pl.CostEstimate(flops=6_000_000_000, bytes_accessed=4_000_000, transcendentals=8_000_000),
        name="near_own",
    )(after, jnp.asarray(np.array(pairs, np.int32).reshape(-1)), q, points, noise, *before)


def edge_items():
    table = near_table(False)
    return [[leaf, *table[leaf, j]] for leaf in range(LEAVES) for j in range(5) if table[leaf, j, 0] >= 0]


ITEMS = edge_items()
EDGES = len(ITEMS)


def extra_of(list_ref, slot_ref, leaf):
    code = second_cycle(list_ref, leaf)
    place = (leaf // SIDE + code // 5) * 8 + leaf % SIDE + code % 5
    slot = slot_ref[jnp.where(code >= 0, place, 0)]
    return code, slot


def edge_body(
    half_at, list_ref, table_ref, slot_ref, after_ref, own_pos_ref, west_any, east_any, north_any, south_any, out_any,
    columns, parts, points, out_ref, sems,
):
    start = 8 * half_at
    copies = []
    sources = (
        (west_any, 12 * RANK),
        (east_any, 12 * RANK),
        (north_any, 12 * RANK),
        (north_any, SIDEWAYS + 8 * RANK),
        (north_any, SIDEWAYS + CORNER + 8 * RANK),
        (south_any, 12 * RANK),
        (south_any, SIDEWAYS + 8 * RANK),
        (south_any, SIDEWAYS + CORNER + 8 * RANK),
    )
    for k, (source, at) in enumerate(sources):
        copies.append(pltpu.make_async_copy(source.at[pl.ds(at, 48)], parts.at[k], sems.at[k]))
    for copy in copies:
        copy.start()

    def turn(leaf, carry):
        turn_points(columns, leaf, own_pos_ref[leaf], jnp.zeros((1, LEAF), F32))
        return carry

    lax.fori_loop(start, start + 8, turn, 0)
    points[0:LEAVES] = own_pos_ref[...]
    for copy in copies:
        copy.wait()
    slots = (16, 24, 32, 40, 44, 48, 56, 60)
    for k in range(8):
        whole = parts[k].astype(F32)
        whole = (whole[0:16] + whole[16:32]) + whole[32:48]
        first, count = {3: (4, 4), 4: (4, 4), 6: (0, 4), 7: (0, 4)}.get(k, (0, 8))
        for i in range(count):
            points[slots[k] + i] = whole[2 * (first + i) : 2 * (first + i) + 2]

    def fixed(i):
        at = 4 * i
        block_into(
            out_ref.at[i],
            columns.at[table_ref[at]],
            points[table_ref[at + 1]],
            table_ref[at + 2],
            table_ref[at + 3],
        )

    repeat(EDGES // 2, 4, fixed)
    backs = []
    for k, part in enumerate((pl.ds(0, EDGES // 2), pl.ds(EDGES // 2, 8))):
        backs.append(pltpu.make_async_copy(out_ref.at[part], out_any.at[part], sems.at[8 + k]))
    backs[0].start()

    def extra(i):
        code, slot = extra_of(list_ref, slot_ref, start + i)
        code = jnp.maximum(code, 0)
        block_into(out_ref.at[EDGES // 2 + i], columns.at[start + i], points[slot], code // 5 - 2, code % 5 - 2)

    repeat(8, 4, extra)
    backs[1].start()
    for back in backs:
        back.wait()


def edge_blocks(half_at, near_list, after, own_points, west, east, north, south):
    vmem = pl.BlockSpec(memory_space=pltpu.VMEM)
    smem = pl.BlockSpec(memory_space=pltpu.SMEM)
    anywhere = pl.BlockSpec(memory_space=pl.ANY)
    items = [item for item in ITEMS if item[0] // 8 == half_at]
    assert len(items) * 2 == EDGES

    def body(*refs):
        edge_body(half_at, *refs)

    return pl.pallas_call(
        body,
        out_shape=jax.ShapeDtypeStruct((EDGES // 2 + 8, LEAF, LEAF), BF),
        in_specs=[smem, smem, smem, anywhere, vmem] + [anywhere] * 4,
        out_specs=anywhere,
        scratch_shapes=[
            pltpu.VMEM((LEAVES, LEAF, 384), F32),
            pltpu.VMEM((8, 48, LEAF), BF),
            pltpu.VMEM((64, 2, LEAF), F32),
            pltpu.VMEM((EDGES // 2 + 8, LEAF, LEAF), BF),
            pltpu.SemaphoreType.DMA((10,)),
        ],
        compiler_params=pltpu.CompilerParams(vmem_limit_bytes=BIG),
        cost_estimate=pl.CostEstimate(flops=6_000_000_000, bytes_accessed=8_000_000, transcendentals=12_000_000),
        name="edge_blocks",
    )(
        near_list, jnp.asarray(np.array(items, np.int32).reshape(-1)), jnp.asarray(SLOT_OF), after, own_points,
        west, east, north, south,
    )


def final_body(
    list_ref, slot_ref, q_any, west_any, east_any, north_any, north_corner_any, south_any, south_corner_any,
    upper_blocks_any, lower_blocks_any, row0_any, row1_any, row2_any, basis_ref, field_ref, out_any, held, blocks, sums, outs, sems,
):
    firsts = [min(at for at in range(EDGES) if ITEMS[at][0] // SIDE == r) for r in range(SIDE)] + [EDGES]
    stages = [[], [], [], []]
    count = 0

    def copy(stage, source, at, rows, to, row):
        nonlocal count
        made = pltpu.make_async_copy(source.at[pl.ds(at, rows)], to.at[pl.ds(row, rows)], sems.at[count])
        count += 1
        stages[stage].append(made)

    copy(0, north_any, 0, 8, held, 32)
    copy(0, north_corner_any, 0, 8, held, 40)
    for stage, low, high in ((0, 0, 3), (1, 3, 4)):
        copy(stage, west_any, 2 * low, 2 * (high - low), held, 16 + 2 * low)
        copy(stage, east_any, 2 * low, 2 * (high - low), held, 24 + 2 * low)
        copy(stage, q_any, 4 * low, 4 * (high - low), held, 4 * low)
    copy(2, south_any, 0, 8, held, 48)
    copy(2, south_corner_any, 0, 8, held, 56)
    for r in range(SIDE):
        source = upper_blocks_any if r < 2 else lower_blocks_any
        back = 0 if r < 2 else EDGES // 2
        copy(r, source, firsts[r] - back, firsts[r + 1] - firsts[r], blocks, firsts[r])
        copy(r, source, EDGES // 2 + SIDE * (r % 2), SIDE, blocks, EDGES + SIDE * r)
        copy(r, (row0_any, row1_any, row2_any, row2_any)[r], SIDE if r == 3 else 0, SIDE, sums, SIDE * r)
    backs = []
    for r in range(SIDE):
        part = pl.ds(SIDE * r, SIDE)
        backs.append(pltpu.make_async_copy(outs.at[part], out_any.at[part], sems.at[count + r]))
    for r in range(2):
        for made in stages[r]:
            made.start()
    for leaf in range(LEAVES):
        if leaf % SIDE == 0:
            for made in stages[leaf // SIDE]:
                made.wait()
            if leaf // SIDE + 2 < SIDE:
                for made in stages[leaf // SIDE + 2]:
                    made.start()
        total = dot_first(basis_ref[leaf], field_ref[leaf])
        for at in range(EDGES):
            if ITEMS[at][0] == leaf:
                total = total + dot(blocks[at], held[ITEMS[at][1]])
        total = total + sums[leaf]
        sums[leaf] = total
        outs[leaf] = total.astype(BF)
        code, slot = extra_of(list_ref, slot_ref, leaf)

        @pl.when(code >= 0)
        def _(leaf=leaf, slot=slot):
            outs[leaf] = (sums[leaf] + dot(blocks[EDGES + leaf], held[slot])).astype(BF)

        if leaf % SIDE == SIDE - 1:
            backs[leaf // SIDE].start()
    for back in backs:
        back.wait()


def finish(near_list, q, halos, upper_blocks, lower_blocks, sums, basis, field):
    vmem = pl.BlockSpec(memory_space=pltpu.VMEM)
    smem = pl.BlockSpec(memory_space=pltpu.SMEM)
    anywhere = pl.BlockSpec(memory_space=pl.ANY)

    return pl.pallas_call(
        final_body,
        out_shape=jax.ShapeDtypeStruct((LEAVES, LEAF, LEAF), BF),
        in_specs=[smem, smem] + [anywhere] * 12 + [vmem, vmem],
        out_specs=anywhere,
        scratch_shapes=[
            pltpu.VMEM((64, LEAF, LEAF), BF),
            pltpu.VMEM((EDGES + LEAVES, LEAF, LEAF), BF),
            pltpu.VMEM((LEAVES, LEAF, LEAF), F32),
            pltpu.VMEM((LEAVES, LEAF, LEAF), BF),
            pltpu.SemaphoreType.DMA((28,)),
        ],
        compiler_params=pltpu.CompilerParams(vmem_limit_bytes=BIG),
        cost_estimate=pl.CostEstimate(flops=4_000_000_000, bytes_accessed=24_000_000, transcendentals=0),
        name="finish",
    )(near_list, jnp.asarray(SLOT_OF), q, *halos, upper_blocks, lower_blocks, *sums, basis, field)


def window_slots(wide, narrow, steps):
    row, col = lax.axis_index("narrow"), lax.axis_index("wide")
    wy, wx = np.arange(WINDOW) // 6, np.arange(WINDOW) % 6

    def slots(target_y, target_x, scale):
        y = target_y // 2 * 2 - 2 + wy
        x = target_x // 2 * 2 - 2 + wx
        inside = (y >= 0) & (y < narrow // scale) & (x >= 0) & (x < wide // scale)
        apart = {"narrow": (y * scale) ^ row, "wide": (x * scale) ^ col}
        slot = 0
        for at, (axis, bit) in enumerate(steps):
            slot = slot + (apart[axis] // bit & 1) * (1 << at)
        return jnp.where(inside, slot if scale == 1 else slot // 4, -1)

    parity2 = row % 2 * 2 + col % 2
    parity3 = row // 2 % 2 * 2 + col // 2 % 2
    return jnp.concatenate(
        [slots(row, col, 1), slots(row // 2, col // 2, 2), jnp.stack([parity2, parity3])]
    ).astype(jnp.int32)


def per_device(wide, narrow, charges, positions, noise, leaf_basis, transfer, near_list):
    q = charges.reshape(LEAVES, LEAF, LEAF)
    points = positions.reshape(LEAVES, 2, LEAF)
    basis = leaf_basis.reshape(LEAVES, RANK, LEAF)
    tree = transfer[0, 0]
    code_y, code_x = near_list // 5, near_list % 5
    outer = (near_list >= 0) & ((code_y == 0) | (code_y == 4) | (code_x == 0) | (code_x == 4))
    listing = jnp.max(jnp.where(outer, near_list, -1), axis=-1).reshape(-1)
    steps = gather_steps(wide, narrow)
    meta = window_slots(wide, narrow, steps)

    east, west, north, south, coefs, give, to_east, to_west, q_up, q_down = go_up(q, basis, tree, points)
    from_west = shift(east, "wide", 1)
    from_east = shift(west, "wide", -1)
    q_north = shift(q_down, "narrow", 1)
    q_south = shift(q_up, "narrow", -1)

    noise_rows = noise.reshape(LEAVES, 1, LEAF)

    def step(value, at):
        axis, bit = steps[at]
        return lax.ppermute(value, axis, [(i, i ^ bit) for i in range(lax.axis_size(axis))])

    def tie(*values):
        return lax.optimization_barrier(values)

    gathered = give
    other = step(gathered, 0)
    row0 = near_own(0, 1, q, points, noise_rows, give, [])
    other, row0, to_east, to_west, q_north, q_south = tie(other, row0, to_east, to_west, q_north, q_south)
    q_west = shift(to_east, "wide", 1)
    q_east = shift(to_west, "wide", -1)
    gathered = jnp.concatenate([gathered, other], axis=0)
    other = step(gathered, 1)
    row1 = near_own(1, 2, q, points, noise_rows, gathered, [row0])
    other, from_west, from_east, row1 = tie(other, from_west, from_east, row1)
    gathered = jnp.concatenate([gathered, other], axis=0)
    other = step(gathered, 2)
    to_north, to_south = join(north, south, from_west, from_east)
    from_south = shift(to_north, "narrow", -1)
    from_north = shift(to_south, "narrow", 1)
    row2 = near_own(2, 4, q, points, noise_rows, to_north, [row1])
    other, from_south, from_north, row2 = tie(other, from_south, from_north, row2)
    gathered = jnp.concatenate([gathered, other], axis=0)
    other = step(gathered, 3)
    sums = local_far(listing, coefs, from_west, from_east, from_north, from_south)
    upper_blocks = edge_blocks(0, listing, sums[1], points, from_west, from_east, from_north, from_south)
    other, upper_blocks = tie(other, upper_blocks)
    for at in range(4, len(steps)):
        gathered = jnp.concatenate([gathered, other], axis=0)
        other = step(gathered, at)
        if at == 4:
            lower_blocks = edge_blocks(1, listing, upper_blocks, points, from_west, from_east, from_north, from_south)
            other, lower_blocks, q_west, q_east = tie(other, lower_blocks, q_west, q_east)
            q_north_corner = shift(jnp.stack([q_west[4:8], q_east[4:8]]), "narrow", 1)
            q_south_corner = shift(jnp.stack([q_west[0:4], q_east[0:4]]), "narrow", -1)
    field = top_far(meta, gathered, other, tree, *sums)
    q_north_corner, q_south_corner, field = tie(q_north_corner, q_south_corner, field)
    halos = [
        value.reshape(8, LEAF, LEAF)
        for value in (q_west, q_east, q_north, q_north_corner, q_south, q_south_corner)
    ]
    out = finish(listing, q, halos, upper_blocks, lower_blocks, (row0, row1, row2), basis, field)
    return out.reshape(SIDE, SIDE, LEAF, LEAF)


def solution(mesh):
    wide, narrow = mesh.shape["wide"], mesh.shape["narrow"]
    in_specs = (
        P("narrow", "wide", None, None),
        P("narrow", "wide", None, None),
        P("narrow", "wide", None),
        P("narrow", "wide", None, None),
        P("narrow", "wide", None, None, None),
        P("narrow", "wide", None),
    )
    out_specs = P("narrow", "wide", None, None)

    def step(*arrays):
        return per_device(wide, narrow, *arrays)

    return jax.shard_map(step, mesh=mesh, in_specs=in_specs, out_specs=out_specs, check_vma=False)
```

```python
import math

import jax
import jax.numpy as jnp
import ml_dtypes
import numpy as np
from jax import lax
from jax.experimental import pallas as pl
from jax.experimental.pallas import tpu as pltpu
from jax.sharding import PartitionSpec as P

LEAF = 256
CHEB = 8
RANK = 64
NEAR = 10
SIDE = 4
LEAVES = SIDE * SIDE
TOP = 20
WINDOW = 36
PACK = RANK + 16
SIDEWAYS = 8 * RANK + 4 * RANK + 48
CORNER = 4 * RANK + 4 * RANK + 48
BIG = 58 << 20
COPIES = 42
BF = jnp.bfloat16
F32 = jnp.float32

short_len = 0.125
long_weight = 0.03125
reach = 3.0 * SIDE
waves = 10.0
LOG2E = math.log2(math.e)
long_rate = -0.5 / (reach * reach) * LOG2E / (waves * waves)
short_rate = -0.5 / (short_len * short_len) * LOG2E / (waves * waves)
rounder = 1.5 * 2.0**23


def sine_terms(count):
    w = np.cos(np.pi * (np.arange(2000) + 0.5) / 2000) * 0.25
    powers = np.stack([w ** (2 * i + 1) for i in range(count)], 1)
    return [float(c) for c in np.linalg.lstsq(powers, np.sin(2 * np.pi * w) * long_weight, rcond=None)[0]]


SINE = sine_terms(3)


def coupling(height, shift_y, shift_x):
    points = 0.5 * (1.0 + np.cos((2.0 * np.arange(CHEB) + 1.0) * (math.pi / (2.0 * CHEB))))
    node_x = np.tile(points, CHEB)
    node_y = np.repeat(points, CHEB)
    gap_x = (node_x[:, None] - node_x[None, :] - shift_x) * 2.0**height
    gap_y = (node_y[:, None] - node_y[None, :] - shift_y) * 2.0**height
    squared = gap_x * gap_x + gap_y * gap_y
    return np.exp(squared * (-0.5 / (short_len * short_len))) + long_weight * np.exp(
        squared * (-0.5 / (reach * reach))
    ) * np.cos(2.0 * math.pi * waves * np.sqrt(squared))


def window_coupling(height):
    table = np.zeros((2, 2, RANK, 6, 6, RANK))
    for py in range(2):
        for px in range(2):
            for wy in range(6):
                for wx in range(6):
                    shift_y, shift_x = wy - 2 - py, wx - 2 - px
                    if max(abs(shift_y), abs(shift_x)) >= 2:
                        table[py, px, :, wy, wx] = coupling(height, shift_y, shift_x)
    return table.reshape(4 * RANK, WINDOW * RANK).astype(ml_dtypes.bfloat16)


def code_coupling():
    return np.stack([coupling(0, code // 5 - 2, code % 5 - 2) for code in range(25)]).astype(ml_dtypes.bfloat16)


def halo_slot(row, col):
    if 0 <= row < 4 and 0 <= col < 4:
        return row * 4 + col
    if 0 <= row < 4:
        return 16 + row * 2 + col + 2 if col < 0 else 24 + row * 2 + col - 4
    base, r = (32, row + 2) if row < 0 else (48, row - 4)
    if 0 <= col < 4:
        return base + r * 4 + col
    return base + 8 + r * 2 + col + 2 if col < 0 else base + 12 + r * 2 + col - 4


SLOT_OF = np.array([halo_slot(r - 2, c - 2) for r in range(8) for c in range(8)], np.int32)


def near_table(own):
    width = 9 if own else 5
    table = np.zeros((LEAVES, width, 3), np.int32)
    table[:, :, 0] = -1
    for r in range(SIDE):
        for c in range(SIDE):
            at = 0
            for dy in (-1, 0, 1):
                for dx in (-1, 0, 1):
                    slot = halo_slot(r + dy, c + dx)
                    if (slot < LEAVES) == own:
                        table[r * SIDE + c, at] = (slot, dy, dx)
                        at += 1
    return table


def bits(count):
    return [1 << i for i in range(count.bit_length() - 1)]


def gather_steps(wide, narrow):
    return (
        [("wide", 1), ("narrow", 1)]
        + [("wide", b) for b in reversed(bits(wide)[1:])]
        + [("narrow", b) for b in reversed(bits(narrow)[1:])]
    )


def shift(value, axis, steps):
    count = lax.axis_size(axis)
    return lax.ppermute(value, axis, [(i, i + steps) for i in range(count) if 0 <= i + steps < count])


def dot(a, b):
    return jnp.dot(a, b, preferred_element_type=F32)


def dot_first(a, b):
    return lax.dot_general(a, b, (((0,), (0,)), ((), ())), preferred_element_type=F32)


def up_body(
    q_any, basis_any, tree_any, pos_ref, east_ref, west_ref, north_ref, south_ref, coef_ref, give_ref, to_east, to_west, to_north, to_south,
    q_ref, basis_ref, tree_ref, sems
):
    loads = []
    for k in range(4):
        part = pl.ds(4 * k, 4)
        loads.append(pltpu.make_async_copy(basis_any.at[part], basis_ref.at[part], sems.at[2 * k]))
        loads.append(pltpu.make_async_copy(q_any.at[part], q_ref.at[part], sems.at[2 * k + 1]))
    loads.append(pltpu.make_async_copy(tree_any, tree_ref, sems.at[8]))
    for load in loads:
        load.start()
    backs = []
    level0 = []
    for leaf in range(LEAVES):
        if leaf % 4 == 0:
            loads[leaf // 2].wait()
            loads[leaf // 2 + 1].wait()
            half = pl.ds(leaf // 2, 2)
            for to, low in ((to_west, leaf), (to_east, leaf + 2)):
                backs.append(pltpu.make_async_copy(q_ref.at[pl.ds(low, 2)], to.at[half], sems.at[9 + len(backs)]))
                backs[-1].start()
            to, row = (to_north, leaf) if leaf < 8 else (to_south, leaf - 8)
            backs.append(pltpu.make_async_copy(q_ref.at[pl.ds(leaf, 4)], to.at[pl.ds(row, 4)], sems.at[9 + len(backs)]))
            backs[-1].start()
        coef = dot(basis_ref[leaf], q_ref[leaf]).astype(BF)
        level0.append(coef)
        r, c = leaf // SIDE, leaf % SIDE
        coef_ref[leaf * RANK : (leaf + 1) * RANK] = coef
        ref, at = (west_ref, r * 2 + c) if c < 2 else (east_ref, r * 2 + c - 2)
        ref[at * RANK : (at + 1) * RANK] = coef
        ref, at = (north_ref, r * 4 + c) if r < 2 else (south_ref, r * 4 + c - 8)
        ref[at * RANK : (at + 1) * RANK] = coef
    loads[8].wait()
    level1 = []
    for r in range(2):
        for c in range(2):
            total = None
            for dr in range(2):
                for dc in range(2):
                    leaf = (2 * r + dr) * SIDE + 2 * c + dc
                    part = dot(tree_ref[leaf], level0[leaf])
                    total = part if total is None else total + part
            coef = total.astype(BF)
            at = r * 2 + c
            level1.append(coef)
            coef_ref[(LEAVES + at) * RANK : (LEAVES + at + 1) * RANK] = coef
            for ref in (east_ref, west_ref, north_ref, south_ref):
                ref[(8 + at) * RANK : (9 + at) * RANK] = coef
    total = None
    for at in range(4):
        part = dot(tree_ref[LEAVES + at], level1[at])
        total = part if total is None else total + part
    give_ref[0:RANK] = total.astype(BF)
    top = tree_ref[TOP]
    give_ref[RANK:PACK] = jnp.concatenate([top[16 * k : 16 * k + 16] for k in range(4)], axis=1)
    for ref, leaves in (
        (west_ref, [r * 4 + c for r in range(4) for c in (0, 1)]),
        (east_ref, [r * 4 + c for r in range(4) for c in (2, 3)]),
        (north_ref, range(8)),
        (south_ref, range(8, 16)),
    ):
        rest = jnp.concatenate([pos_ref[leaf] for leaf in leaves], axis=0)
        for part in range(3):
            held = rest.astype(BF)
            at = 12 * RANK + 16 * part
            ref[at : at + 16] = held
            rest = rest - held.astype(F32)
    for back in backs:
        back.wait()


def go_up(q, basis, tree, points):
    vmem = pl.BlockSpec(memory_space=pltpu.VMEM)
    side = jax.ShapeDtypeStruct((SIDEWAYS, LEAF), BF)
    return pl.pallas_call(
        up_body,
        out_shape=(
            side,
            side,
            side,
            side,
            jax.ShapeDtypeStruct(((LEAVES + 4) * RANK, LEAF), BF),
            jax.ShapeDtypeStruct((PACK, LEAF), BF),
        )
        + (jax.ShapeDtypeStruct((8, LEAF, LEAF), BF),) * 4,
        in_specs=[pl.BlockSpec(memory_space=pl.ANY)] * 3 + [vmem],
        out_specs=[vmem] * 6 + [pl.BlockSpec(memory_space=pl.ANY)] * 4,
        scratch_shapes=[
            pltpu.VMEM((LEAVES, LEAF, LEAF), BF),
            pltpu.VMEM((LEAVES, RANK, LEAF), BF),
            pltpu.VMEM((TOP + 1, RANK, RANK), BF),
            pltpu.SemaphoreType.DMA((21,)),
        ],
        compiler_params=pltpu.CompilerParams(vmem_limit_bytes=BIG),
        cost_estimate=pl.CostEstimate(flops=300_000_000, bytes_accessed=5_000_000, transcendentals=0),
        name="upward",
    )(q, basis, tree, points)


def local_body(
    list_ref, coef_any, west_any, east_any, north_any, south_any, c0_any, c1_any, code_any, sum0, sum1, pad0, pad1, c0_ref, c1_ref, code_ref, sems
):
    loads = []

    def load(source, at, to, row, count):
        rows = pl.ds(at * RANK if at < 100 else at, count * RANK)
        copy = pltpu.make_async_copy(source.at[rows], to.at[pl.ds(row, count * RANK)], sems.at[len(loads)])
        copy.start()
        loads.append(copy)

    def put(pad, extent, row, col, ref, at, count):
        load(ref, at, pad, ((row + 2) * (extent + 4) + col + 2) * RANK, count)

    whole = []
    for k, (source, to) in enumerate(((c0_any, c0_ref), (c1_any, c1_ref), (code_any, code_ref))):
        whole.append(pltpu.make_async_copy(source, to, sems.at[COPIES + k]))
    whole[0].start()
    for r in range(4):
        put(pad0, 4, r, 0, coef_any, r * 4, 4)
        put(pad0, 4, r, -2, west_any, r * 2, 2)
        put(pad0, 4, r, 4, east_any, r * 2, 2)
    for ref, row in ((north_any, -2), (south_any, 4)):
        for r in range(2):
            put(pad0, 4, row + r, 0, ref, r * 4, 4)
            for col, base in ((-2, SIDEWAYS), (4, SIDEWAYS + CORNER)):
                load(ref, base + r * 2 * RANK, pad0, ((row + r + 2) * 8 + col + 2) * RANK, 2)
    split = len(loads)
    for copy in whole[1:]:
        copy.start()
    for r in range(2):
        put(pad1, 2, r, 0, coef_any, LEAVES + r * 2, 2)
        put(pad1, 2, r, -2, west_any, 8 + r * 2, 2)
        put(pad1, 2, r, 2, east_any, 8 + r * 2, 2)
    for ref, row in ((north_any, -2), (south_any, 2)):
        for r in range(2):
            put(pad1, 2, row + r, 0, ref, 8 + r * 2, 2)
            for col, base in ((-2, SIDEWAYS), (2, SIDEWAYS + CORNER)):
                load(ref, base + (4 + r * 2) * RANK, pad1, ((row + r + 2) * 6 + col + 2) * RANK, 2)
    whole[0].wait()
    for copy in loads[:split]:
        copy.wait()
    for a in range(2):
        for b in range(2):
            total = None
            for wy in range(6):
                at = ((2 * a + wy) * 8 + 2 * b) * RANK
                part = dot(c0_ref[:, wy * 6 * RANK : (wy + 1) * 6 * RANK], pad0[at : at + 6 * RANK])
                total = part if total is None else total + part
            for child in range(4):
                leaf = (2 * a + child // 2) * SIDE + 2 * b + child % 2
                sum0[leaf] = total[child * RANK : (child + 1) * RANK]
    for copy in loads[split:] + whole[1:]:
        copy.wait()

    def listed(leaf, carry):
        code = second_cycle(list_ref, leaf)

        @pl.when(code >= 0)
        def _():
            row = leaf // SIDE + code // 5
            col = leaf % SIDE + code % 5
            at = pl.multiple_of((row * 8 + col) * RANK, RANK)
            sum0[leaf] = sum0[leaf] - dot(code_ref[code], pad0[pl.ds(at, RANK)])

        return carry

    lax.fori_loop(0, LEAVES, listed, 0)
    sum1[...] = dot(c1_ref[...], pad1[...])


def local_far(near_list, coefs, west, east, north, south):
    vmem = pl.BlockSpec(memory_space=pltpu.VMEM)
    smem = pl.BlockSpec(memory_space=pltpu.SMEM)
    return pl.pallas_call(
        local_body,
        out_shape=(
            jax.ShapeDtypeStruct((LEAVES, RANK, LEAF), F32),
            jax.ShapeDtypeStruct((4 * RANK, LEAF), F32),
        ),
        in_specs=[smem] + [pl.BlockSpec(memory_space=pl.ANY)] * 8,
        out_specs=[vmem] * 2,
        scratch_shapes=[
            pltpu.VMEM((64 * RANK, LEAF), BF),
            pltpu.VMEM((WINDOW * RANK, LEAF), BF),
            pltpu.VMEM((4 * RANK, WINDOW * RANK), BF),
            pltpu.VMEM((4 * RANK, WINDOW * RANK), BF),
            pltpu.VMEM((25, RANK, RANK), BF),
            pltpu.SemaphoreType.DMA((COPIES + 3,)),
        ],
        compiler_params=pltpu.CompilerParams(vmem_limit_bytes=BIG),
        cost_estimate=pl.CostEstimate(flops=5_000_000_000, bytes_accessed=8_000_000, transcendentals=0),
        name="local_far",
    )(
        near_list,
        coefs,
        west,
        east,
        north,
        south,
        jnp.asarray(window_coupling(0)),
        jnp.asarray(window_coupling(1)),
        jnp.asarray(code_coupling()),
    )


def top_body(
    meta_ref, mine_any, other_any, c2_any, c3_any, tree_any, sum0_any, sum1_any, field_ref, win, parents, c2_ref, c3_ref, all_ref, tree_ref, sum0, sum1, sems
):
    loads = []
    for k, (source, to) in enumerate(((mine_any, all_ref.at[pl.ds(0, mine_any.shape[0])]), (other_any, all_ref.at[pl.ds(mine_any.shape[0], mine_any.shape[0])]), (tree_any, tree_ref), (sum1_any, sum1), (sum0_any, sum0))):
        loads.append(pltpu.make_async_copy(source, to, sems.at[2 + k]))
        loads[-1].start()

    def slab(source, to, at):
        part = pl.ds(pl.multiple_of(meta_ref[2 * WINDOW + at] * RANK, RANK), RANK)
        copy = pltpu.make_async_copy(source.at[part], to, sems.at[at])
        copy.start()
        return copy

    slabs = [slab(c2_any, c2_ref, 0), slab(c3_any, c3_ref, 1)]

    loads[0].wait()
    loads[1].wait()

    def lift(group, carry):
        total = jnp.zeros((RANK, LEAF), F32)
        for child in range(4):
            at = pl.multiple_of((group * 4 + child) * PACK, 16)
            packed = all_ref[pl.ds(at + RANK, 16)]
            matrix = jnp.concatenate([packed[:, k * RANK : (k + 1) * RANK] for k in range(4)], axis=0)
            total = total + dot(matrix, all_ref[pl.ds(at, RANK)])
        parents[pl.ds(pl.multiple_of(group * RANK, RANK), RANK)] = total.astype(BF)
        return carry

    lax.fori_loop(0, parents.shape[0] // RANK, lift, 0)

    def fill(start, source, stride):
        for i in range(WINDOW):
            slot = meta_ref[start + i]
            at = pl.multiple_of(jnp.maximum(slot, 0) * stride, 16)
            kept = jnp.where(slot >= 0, 1.0, 0.0).astype(BF)
            win[i * RANK : (i + 1) * RANK] = source[pl.ds(at, RANK)] * kept

    fill(WINDOW, parents, RANK)
    slabs[1].wait()
    field3 = dot(c3_ref[...], win[...]).astype(BF)
    fill(0, all_ref, PACK)
    slabs[0].wait()
    for load in loads[2:]:
        load.wait()
    field2 = (dot(c2_ref[...], win[...]) + dot_first(tree_ref[TOP], field3)).astype(BF)
    field1 = []
    for at in range(4):
        field1.append(
            (sum1[at * RANK : (at + 1) * RANK] + dot_first(tree_ref[LEAVES + at], field2)).astype(BF)
        )
    for leaf in range(LEAVES):
        above = field1[leaf // SIDE // 2 * 2 + leaf % SIDE // 2]
        field_ref[leaf] = (sum0[leaf] + dot_first(tree_ref[leaf], above)).astype(BF)


def second_cycle(list_ref, leaf):
    return list_ref[leaf]


def top_far(meta, mine, other, tree, sum0, sum1):
    vmem = pl.BlockSpec(memory_space=pltpu.VMEM)
    smem = pl.BlockSpec(memory_space=pltpu.SMEM)
    anywhere = pl.BlockSpec(memory_space=pl.ANY)
    rows = 2 * mine.shape[0]
    devices = rows // PACK
    return pl.pallas_call(
        top_body,
        out_shape=jax.ShapeDtypeStruct((LEAVES, RANK, LEAF), BF),
        in_specs=[smem] + [anywhere] * 7,
        out_specs=vmem,
        scratch_shapes=[
            pltpu.VMEM((WINDOW * RANK, LEAF), BF),
            pltpu.VMEM((devices // 4 * RANK, LEAF), BF),
            pltpu.VMEM((RANK, WINDOW * RANK), BF),
            pltpu.VMEM((RANK, WINDOW * RANK), BF),
            pltpu.VMEM((rows, LEAF), BF),
            pltpu.VMEM((TOP + 1, RANK, RANK), BF),
            pltpu.VMEM((LEAVES, RANK, LEAF), F32),
            pltpu.VMEM((4 * RANK, LEAF), F32),
            pltpu.SemaphoreType.DMA((7,)),
        ],
        compiler_params=pltpu.CompilerParams(vmem_limit_bytes=BIG),
        cost_estimate=pl.CostEstimate(flops=3_000_000_000, bytes_accessed=5_000_000, transcendentals=0),
        name="top_far",
    )(meta, mine, other, jnp.asarray(window_coupling(2)), jnp.asarray(window_coupling(3)), tree, sum0, sum1)


def join_body(north_ref, south_ref, west_ref, east_ref, north_any, south_any, to_north, to_south, sems):
    copies = []

    def move(source, at, to, row, count):
        copy = pltpu.make_async_copy(source.at[pl.ds(at, count)], to.at[pl.ds(row, count)], sems.at[len(copies)])
        copy.start()
        copies.append(copy)

    for own, to, lower in ((north_ref, to_north, 0), (south_ref, to_south, 1)):
        move(own, 0, to, 0, SIDEWAYS)
        for side, base in ((west_ref, SIDEWAYS), (east_ref, SIDEWAYS + CORNER)):
            move(side, 4 * RANK * lower, to, base, 4 * RANK)
            move(side, 8 * RANK, to, base + 4 * RANK, CORNER - 4 * RANK)
    backs = []
    for k, (held, to) in enumerate(((to_north, north_any), (to_south, south_any))):
        for copy in copies[5 * k : 5 * k + 5]:
            copy.wait()
        backs.append(pltpu.make_async_copy(held, to, sems.at[10 + k]))
        backs[-1].start()
    for back in backs:
        back.wait()


def join(north, south, west, east):
    anywhere = pl.BlockSpec(memory_space=pl.ANY)
    message = jax.ShapeDtypeStruct((SIDEWAYS + 2 * CORNER, LEAF), BF)
    return pl.pallas_call(
        join_body,
        out_shape=(message, message),
        in_specs=[anywhere] * 4,
        out_specs=[anywhere] * 2,
        scratch_shapes=[pltpu.VMEM(message.shape, BF)] * 2 + [pltpu.SemaphoreType.DMA((12,))],
        compiler_params=pltpu.CompilerParams(vmem_limit_bytes=BIG),
        cost_estimate=pl.CostEstimate(flops=0, bytes_accessed=4_000_000, transcendentals=0),
        name="join",
    )(north, south, west, east)


def kernel_of(target_x, target_y, source_x, source_y):
    gap_x = target_x - source_x
    gap_y = target_y - source_y
    squared = jnp.maximum(gap_x * gap_x + gap_y * gap_y, 1e-12)
    length = squared * lax.rsqrt(squared)
    phase = length - ((length + rounder) - rounder)
    w = 0.25 - jnp.abs(phase)
    s = w * w
    wave = w * (SINE[0] + s * (SINE[1] + s * SINE[2]))
    return (jnp.exp2(squared * short_rate) + jnp.exp2(squared * long_rate) * wave).astype(BF)


def spread_columns(rows, columns):
    turned = rows.T
    for k in range(columns.shape[1] // 128):
        columns[:, 128 * k : 128 * (k + 1)] = jnp.broadcast_to(turned[:, k : k + 1], (LEAF, 128))


def block_into(to, columns, points, shift_y, shift_x):
    source_x = (points[0:1] + shift_x.astype(F32)) * waves
    source_y = (points[1:2] + shift_y.astype(F32)) * waves
    rows = 16
    source_x = jnp.broadcast_to(source_x, (rows, LEAF))
    source_y = jnp.broadcast_to(source_y, (rows, LEAF))
    for i in range(0, LEAF, rows):
        target_x = columns[i : i + rows, 0:128]
        target_y = columns[i : i + rows, 128:256]
        to[i : i + rows] = kernel_of(
            jnp.concatenate([target_x, target_x], axis=1),
            jnp.concatenate([target_y, target_y], axis=1),
            source_x,
            source_y,
        )


def turn_points(columns, leaf, position, noise):
    rows = jnp.concatenate([position * waves, noise, jnp.zeros((5, LEAF), F32)], axis=0)
    spread_columns(rows, columns.at[leaf])


def repeat(count, at_once, step):
    def several(i, carry):
        for k in range(at_once):
            step(i * at_once + k)
        return carry

    lax.fori_loop(0, count // at_once, several, 0)
    for i in range(count // at_once * at_once, count):
        step(i)


def own_pairs(first, last):
    pairs = []
    for r in range(first, last):
        for c in range(SIDE):
            for dy, dx in ((0, 1), (1, -1), (1, 0), (1, 1)):
                if r + dy < SIDE and 0 <= c + dx < SIDE:
                    pairs.append((r * SIDE + c, (r + dy) * SIDE + c + dx, dy, dx))
    return pairs


def near_own_body(first, last, table_ref, q_any, pos_ref, noise_ref, *refs):
    before_any, out_any, columns, blocks, q_ref, before_ref, out_ref, sems = (None,) * (8 - len(refs)) + refs
    loads = [pltpu.make_async_copy(q_any, q_ref, sems.at[0])]
    if first:
        loads.append(pltpu.make_async_copy(before_any.at[pl.ds(SIDE, SIDE)], before_ref, sems.at[1]))
    for load in loads:
        load.start()
    pairs = own_pairs(first, last)
    start = first * SIDE
    count = (last - first) * SIDE

    def turn(leaf, carry):
        turn_points(columns, leaf, pos_ref[leaf], noise_ref[leaf])
        return carry

    lax.fori_loop(start, start + count, turn, 0)
    zero = jnp.int32(0)

    def single(i):
        block_into(blocks.at[i], columns.at[start + i], pos_ref[start + i], zero, zero)

    repeat(count, 4, single)

    def turned(i):
        blocks[count + 2 * i + 1] = blocks[count + 2 * i].T

    def pair(i):
        at = 4 * i
        place = count + 2 * i
        target, source = table_ref[at], table_ref[at + 1]
        block_into(blocks.at[place], columns.at[target], pos_ref[source], table_ref[at + 2], table_ref[at + 3])

    for i in range(4):
        pair(i)

    def four(i, carry):
        for k in range(4):
            turned(4 * i + k - 4)
        for k in range(4):
            pair(4 * i + k)
        return carry

    steps = len(pairs) // 4
    lax.fori_loop(1, steps, four, 0)
    for i in range(4 * steps - 4, 4 * steps):
        turned(i)
    for i in range(4 * steps, len(pairs)):
        pair(i)
        turned(i)
    for load in loads:
        load.wait()
    parts = {leaf: [(leaf - start, leaf)] for leaf in range(start, start + count)}
    for i, (target, source, _, _) in enumerate(pairs):
        parts[target].append((count + 2 * i, source))
        parts.setdefault(source, []).append((count + 1 + 2 * i, target))
    backs = []
    for leaf, terms in sorted(parts.items()):
        total = None
        for place, source in terms:
            part = dot(blocks[place], q_ref[source])
            total = part if total is None else total + part
        if leaf < start + count:
            noise = jnp.concatenate([columns[leaf, :, 256:384]] * 2, axis=1)
            total = total + noise * q_ref[leaf].astype(F32)
        if first and leaf < start + SIDE:
            total = total + before_ref[leaf - start]
        out_ref[leaf - start] = total
        backs.append(pltpu.make_async_copy(out_ref.at[leaf - start], out_any.at[leaf - start], sems.at[2 + leaf - start]))
        backs[-1].start()
    for back in backs:
        back.wait()


def near_own(first, last, q, points, noise, after, before):
    vmem = pl.BlockSpec(memory_space=pltpu.VMEM)
    smem = pl.BlockSpec(memory_space=pltpu.SMEM)
    anywhere = pl.BlockSpec(memory_space=pl.ANY)
    pairs = own_pairs(first, last)
    leaves = (min(last + 1, SIDE) - first) * SIDE

    def body(after_ref, *refs):
        near_own_body(first, last, *refs)

    return pl.pallas_call(
        body,
        out_shape=jax.ShapeDtypeStruct((leaves, LEAF, LEAF), F32),
        in_specs=[anywhere, smem, anywhere, vmem, vmem] + [anywhere] * len(before),
        out_specs=anywhere,
        scratch_shapes=[
            pltpu.VMEM((LEAVES, LEAF, 384), F32),
            pltpu.VMEM(((last - first) * SIDE + 2 * len(pairs), LEAF, LEAF), BF),
            pltpu.VMEM((LEAVES, LEAF, LEAF), BF),
            pltpu.VMEM((SIDE, LEAF, LEAF), F32),
            pltpu.VMEM((leaves, LEAF, LEAF), F32),
            pltpu.SemaphoreType.DMA((2 + leaves,)),
        ],
        compiler_params=pltpu.CompilerParams(vmem_limit_bytes=BIG),
        cost_estimate=pl.CostEstimate(flops=6_000_000_000, bytes_accessed=4_000_000, transcendentals=8_000_000),
        name="near_own",
    )(after, jnp.asarray(np.array(pairs, np.int32).reshape(-1)), q, points, noise, *before)


def edge_items():
    table = near_table(False)
    return [[leaf, *table[leaf, j]] for leaf in range(LEAVES) for j in range(5) if table[leaf, j, 0] >= 0]


ITEMS = edge_items()
EDGES = len(ITEMS)


def extra_of(list_ref, slot_ref, leaf):
    code = second_cycle(list_ref, leaf)
    place = (leaf // SIDE + code // 5) * 8 + leaf % SIDE + code % 5
    slot = slot_ref[jnp.where(code >= 0, place, 0)]
    return code, slot


def edge_body(
    half_at, list_ref, table_ref, slot_ref, after_ref, own_pos_ref, west_any, east_any, north_any, south_any, out_any,
    columns, parts, points, out_ref, sems,
):
    start = 8 * half_at
    copies = []
    sources = (
        (west_any, 12 * RANK),
        (east_any, 12 * RANK),
        (north_any, 12 * RANK),
        (north_any, SIDEWAYS + 8 * RANK),
        (north_any, SIDEWAYS + CORNER + 8 * RANK),
        (south_any, 12 * RANK),
        (south_any, SIDEWAYS + 8 * RANK),
        (south_any, SIDEWAYS + CORNER + 8 * RANK),
    )
    for k, (source, at) in enumerate(sources):
        copies.append(pltpu.make_async_copy(source.at[pl.ds(at, 48)], parts.at[k], sems.at[k]))
    for copy in copies:
        copy.start()

    def turn(leaf, carry):
        turn_points(columns, leaf, own_pos_ref[leaf], jnp.zeros((1, LEAF), F32))
        return carry

    lax.fori_loop(start, start + 8, turn, 0)
    points[0:LEAVES] = own_pos_ref[...]
    for copy in copies:
        copy.wait()
    slots = (16, 24, 32, 40, 44, 48, 56, 60)
    for k in range(8):
        whole = parts[k].astype(F32)
        whole = (whole[0:16] + whole[16:32]) + whole[32:48]
        first, count = {3: (4, 4), 4: (4, 4), 6: (0, 4), 7: (0, 4)}.get(k, (0, 8))
        for i in range(count):
            points[slots[k] + i] = whole[2 * (first + i) : 2 * (first + i) + 2]

    def fixed(i):
        at = 4 * i
        block_into(
            out_ref.at[i],
            columns.at[table_ref[at]],
            points[table_ref[at + 1]],
            table_ref[at + 2],
            table_ref[at + 3],
        )

    repeat(EDGES // 2, 4, fixed)
    backs = []
    for k, part in enumerate((pl.ds(0, EDGES // 2), pl.ds(EDGES // 2, 8))):
        backs.append(pltpu.make_async_copy(out_ref.at[part], out_any.at[part], sems.at[8 + k]))
    backs[0].start()

    def extra(i):
        code, slot = extra_of(list_ref, slot_ref, start + i)
        code = jnp.maximum(code, 0)
        block_into(out_ref.at[EDGES // 2 + i], columns.at[start + i], points[slot], code // 5 - 2, code % 5 - 2)

    repeat(8, 4, extra)
    backs[1].start()
    for back in backs:
        back.wait()


def edge_blocks(half_at, near_list, after, own_points, west, east, north, south):
    vmem = pl.BlockSpec(memory_space=pltpu.VMEM)
    smem = pl.BlockSpec(memory_space=pltpu.SMEM)
    anywhere = pl.BlockSpec(memory_space=pl.ANY)
    items = [item for item in ITEMS if item[0] // 8 == half_at]
    assert len(items) * 2 == EDGES

    def body(*refs):
        edge_body(half_at, *refs)

    return pl.pallas_call(
        body,
        out_shape=jax.ShapeDtypeStruct((EDGES // 2 + 8, LEAF, LEAF), BF),
        in_specs=[smem, smem, smem, anywhere, vmem] + [anywhere] * 4,
        out_specs=anywhere,
        scratch_shapes=[
            pltpu.VMEM((LEAVES, LEAF, 384), F32),
            pltpu.VMEM((8, 48, LEAF), BF),
            pltpu.VMEM((64, 2, LEAF), F32),
            pltpu.VMEM((EDGES // 2 + 8, LEAF, LEAF), BF),
            pltpu.SemaphoreType.DMA((10,)),
        ],
        compiler_params=pltpu.CompilerParams(vmem_limit_bytes=BIG),
        cost_estimate=pl.CostEstimate(flops=6_000_000_000, bytes_accessed=8_000_000, transcendentals=12_000_000),
        name="edge_blocks",
    )(
        near_list, jnp.asarray(np.array(items, np.int32).reshape(-1)), jnp.asarray(SLOT_OF), after, own_points,
        west, east, north, south,
    )


def final_body(
    list_ref, slot_ref, q_any, west_any, east_any, north_any, north_corner_any, south_any, south_corner_any,
    upper_blocks_any, lower_blocks_any, row0_any, row1_any, row2_any, basis_ref, field_ref, out_any, held, blocks, sums, outs, sems,
):
    firsts = [min(at for at in range(EDGES) if ITEMS[at][0] // SIDE == r) for r in range(SIDE)] + [EDGES]
    stages = [[], [], [], []]
    count = 0

    def copy(stage, source, at, rows, to, row):
        nonlocal count
        made = pltpu.make_async_copy(source.at[pl.ds(at, rows)], to.at[pl.ds(row, rows)], sems.at[count])
        count += 1
        stages[stage].append(made)

    copy(0, north_any, 0, 8, held, 32)
    copy(0, north_corner_any, 0, 8, held, 40)
    for stage, low, high in ((0, 0, 3), (1, 3, 4)):
        copy(stage, west_any, 2 * low, 2 * (high - low), held, 16 + 2 * low)
        copy(stage, east_any, 2 * low, 2 * (high - low), held, 24 + 2 * low)
        copy(stage, q_any, 4 * low, 4 * (high - low), held, 4 * low)
    copy(2, south_any, 0, 8, held, 48)
    copy(2, south_corner_any, 0, 8, held, 56)
    for r in range(SIDE):
        source = upper_blocks_any if r < 2 else lower_blocks_any
        back = 0 if r < 2 else EDGES // 2
        copy(r, source, firsts[r] - back, firsts[r + 1] - firsts[r], blocks, firsts[r])
        copy(r, source, EDGES // 2 + SIDE * (r % 2), SIDE, blocks, EDGES + SIDE * r)
        copy(r, (row0_any, row1_any, row2_any, row2_any)[r], SIDE if r == 3 else 0, SIDE, sums, SIDE * r)
    backs = []
    for r in range(SIDE):
        part = pl.ds(SIDE * r, SIDE)
        backs.append(pltpu.make_async_copy(outs.at[part], out_any.at[part], sems.at[count + r]))
    for r in range(2):
        for made in stages[r]:
            made.start()
    for leaf in range(LEAVES):
        if leaf % SIDE == 0:
            for made in stages[leaf // SIDE]:
                made.wait()
            if leaf // SIDE + 2 < SIDE:
                for made in stages[leaf // SIDE + 2]:
                    made.start()
        total = dot_first(basis_ref[leaf], field_ref[leaf])
        for at in range(EDGES):
            if ITEMS[at][0] == leaf:
                total = total + dot(blocks[at], held[ITEMS[at][1]])
        total = total + sums[leaf]
        sums[leaf] = total
        outs[leaf] = total.astype(BF)
        code, slot = extra_of(list_ref, slot_ref, leaf)

        @pl.when(code >= 0)
        def _(leaf=leaf, slot=slot):
            outs[leaf] = (sums[leaf] + dot(blocks[EDGES + leaf], held[slot])).astype(BF)

        if leaf % SIDE == SIDE - 1:
            backs[leaf // SIDE].start()
    for back in backs:
        back.wait()


def finish(near_list, q, halos, upper_blocks, lower_blocks, sums, basis, field):
    vmem = pl.BlockSpec(memory_space=pltpu.VMEM)
    smem = pl.BlockSpec(memory_space=pltpu.SMEM)
    anywhere = pl.BlockSpec(memory_space=pl.ANY)

    return pl.pallas_call(
        final_body,
        out_shape=jax.ShapeDtypeStruct((LEAVES, LEAF, LEAF), BF),
        in_specs=[smem, smem] + [anywhere] * 12 + [vmem, vmem],
        out_specs=anywhere,
        scratch_shapes=[
            pltpu.VMEM((64, LEAF, LEAF), BF),
            pltpu.VMEM((EDGES + LEAVES, LEAF, LEAF), BF),
            pltpu.VMEM((LEAVES, LEAF, LEAF), F32),
            pltpu.VMEM((LEAVES, LEAF, LEAF), BF),
            pltpu.SemaphoreType.DMA((28,)),
        ],
        compiler_params=pltpu.CompilerParams(vmem_limit_bytes=BIG),
        cost_estimate=pl.CostEstimate(flops=4_000_000_000, bytes_accessed=24_000_000, transcendentals=0),
        name="finish",
    )(near_list, jnp.asarray(SLOT_OF), q, *halos, upper_blocks, lower_blocks, *sums, basis, field)


def window_slots(wide, narrow, steps):
    row, col = lax.axis_index("narrow"), lax.axis_index("wide")
    wy, wx = np.arange(WINDOW) // 6, np.arange(WINDOW) % 6

    def slots(target_y, target_x, scale):
        y = target_y // 2 * 2 - 2 + wy
        x = target_x // 2 * 2 - 2 + wx
        inside = (y >= 0) & (y < narrow // scale) & (x >= 0) & (x < wide // scale)
        apart = {"narrow": (y * scale) ^ row, "wide": (x * scale) ^ col}
        slot = 0
        for at, (axis, bit) in enumerate(steps):
            slot = slot + (apart[axis] // bit & 1) * (1 << at)
        return jnp.where(inside, slot if scale == 1 else slot // 4, -1)

    parity2 = row % 2 * 2 + col % 2
    parity3 = row // 2 % 2 * 2 + col // 2 % 2
    return jnp.concatenate(
        [slots(row, col, 1), slots(row // 2, col // 2, 2), jnp.stack([parity2, parity3])]
    ).astype(jnp.int32)


def per_device(wide, narrow, charges, positions, noise, leaf_basis, transfer, near_list):
    q = charges.reshape(LEAVES, LEAF, LEAF)
    points = positions.reshape(LEAVES, 2, LEAF)
    basis = leaf_basis.reshape(LEAVES, RANK, LEAF)
    tree = transfer[0, 0]
    code_y, code_x = near_list // 5, near_list % 5
    outer = (near_list >= 0) & ((code_y == 0) | (code_y == 4) | (code_x == 0) | (code_x == 4))
    listing = jnp.max(jnp.where(outer, near_list, -1), axis=-1).reshape(-1)
    steps = gather_steps(wide, narrow)
    meta = window_slots(wide, narrow, steps)

    east, west, north, south, coefs, give, to_east, to_west, q_up, q_down = go_up(q, basis, tree, points)
    from_west = shift(east, "wide", 1)
    from_east = shift(west, "wide", -1)
    q_north = shift(q_down, "narrow", 1)
    q_south = shift(q_up, "narrow", -1)

    noise_rows = noise.reshape(LEAVES, 1, LEAF)

    def step(value, at):
        axis, bit = steps[at]
        return lax.ppermute(value, axis, [(i, i ^ bit) for i in range(lax.axis_size(axis))])

    def tie(*values):
        return lax.optimization_barrier(values)

    gathered = give
    other = step(gathered, 0)
    row0 = near_own(0, 1, q, points, noise_rows, give, [])
    other, row0 = tie(other, row0)
    gathered = jnp.concatenate([gathered, other], axis=0)
    other = step(gathered, 1)
    row1 = near_own(1, 2, q, points, noise_rows, gathered, [row0])
    other, from_west, from_east, row1, to_east, to_west, q_north, q_south = tie(
        other, from_west, from_east, row1, to_east, to_west, q_north, q_south
    )
    gathered = jnp.concatenate([gathered, other], axis=0)
    other = step(gathered, 2)
    to_north, to_south = join(north, south, from_west, from_east)
    from_south = shift(to_north, "narrow", -1)
    from_north = shift(to_south, "narrow", 1)
    q_west = shift(to_east, "wide", 1)
    q_east = shift(to_west, "wide", -1)
    row2 = near_own(2, 4, q, points, noise_rows, to_north, [row1])
    other, from_south, from_north, row2 = tie(other, from_south, from_north, row2)
    gathered = jnp.concatenate([gathered, other], axis=0)
    other = step(gathered, 3)
    sums = local_far(listing, coefs, from_west, from_east, from_north, from_south)
    upper_blocks = edge_blocks(0, listing, sums[1], points, from_west, from_east, from_north, from_south)
    other, upper_blocks = tie(other, upper_blocks)
    for at in range(4, len(steps)):
        gathered = jnp.concatenate([gathered, other], axis=0)
        other = step(gathered, at)
        if at == 4:
            lower_blocks = edge_blocks(1, listing, upper_blocks, points, from_west, from_east, from_north, from_south)
            other, lower_blocks, q_west, q_east = tie(other, lower_blocks, q_west, q_east)
            q_north_corner = shift(jnp.stack([q_west[4:8], q_east[4:8]]), "narrow", 1)
            q_south_corner = shift(jnp.stack([q_west[0:4], q_east[0:4]]), "narrow", -1)
    field = top_far(meta, gathered, other, tree, *sums)
    q_north_corner, q_south_corner, field = tie(q_north_corner, q_south_corner, field)
    halos = [
        value.reshape(8, LEAF, LEAF)
        for value in (q_west, q_east, q_north, q_north_corner, q_south, q_south_corner)
    ]
    out = finish(listing, q, halos, upper_blocks, lower_blocks, (row0, row1, row2), basis, field)
    return out.reshape(SIDE, SIDE, LEAF, LEAF)


def solution(mesh):
    wide, narrow = mesh.shape["wide"], mesh.shape["narrow"]
    in_specs = (
        P("narrow", "wide", None, None),
        P("narrow", "wide", None, None),
        P("narrow", "wide", None),
        P("narrow", "wide", None, None),
        P("narrow", "wide", None, None, None),
        P("narrow", "wide", None),
    )
    out_specs = P("narrow", "wide", None, None)

    def step(*arrays):
        return per_device(wide, narrow, *arrays)

    return jax.shard_map(step, mesh=mesh, in_specs=in_specs, out_specs=out_specs, check_vma=False)
```
